32 devices in a mesh: blk: 8 (over y, x, core), rep: 4 (over z).
Axes of the slice: x: 2, y: 2, z: 4, core: 2. Of those that a mesh axis runs over, the one named last changes fastest.
Arguments:
- node_states: float32 [4096, 128], P('blk'), may hold values from -6 to 6
- edge_feats: bfloat16 [32768, 16], P('blk'), may hold values from -6 to 6
- edge_source: int32 [32768], P('blk'), may hold values from 0 to 4095, as said below
- edge_target: int32 [32768], P('blk'), may hold values from 0 to 4095, as said below
- edge_group: int32 [32768], P('blk'), may hold values from 0 to 15
- column_mask: int32 [16, 16], replicated, may hold values 0 or 1
- edge_count: int32 [8], P('blk'), may hold values from 2048 to 4096, as said below
- first_weight: bfloat16 [16, 128], replicated, may hold values from -1.5 to 1.5
- first_bias: float32 [128], replicated, may hold values from -3 to 3
- second_weight: bfloat16 [128, 16384], P(None, 'rep'), may hold values from -0.046875 to 0.046875
- second_bias: float32 [16384], P('rep'), may hold values from -0.3125 to 0.3125
- update_input_weight: bfloat16 [128, 384], replicated, may hold values from -0.5 to 0.5
- update_state_weight: bfloat16 [128, 384], replicated, may hold values from -0.5 to 0.5
- update_input_bias: float32 [384], replicated, may hold values from -1.75 to 1.75
- update_state_bias: float32 [384], replicated, may hold values from -1.75 to 1.75
- state_cotangent: float32 [4096, 128], P('blk'), may hold values from -6 to 6
Outputs:
- final_states: float32 [4096, 128], P('blk')
- grad_states: float32 [4096, 128], P('blk')
- grad_edge_feats: float32 [32768, 16], P('blk')
- grad_first_weight: float32 [16, 128], replicated
- grad_first_bias: float32 [128], replicated
- grad_second_weight: float32 [128, 16384], P(None, 'rep')
- grad_second_bias: float32 [16384], P('rep')
- grad_input_weight: float32 [128, 384], replicated
- grad_state_weight: float32 [128, 384], replicated
- grad_input_bias: float32 [384], replicated
- grad_state_bias: float32 [384], replicated
The draws below stay inside these ranges and needn't reach their ends.
Inputs may be any that keep to these rules, and one draw needn't show every extreme that they name: `edge_source`: the graph is split into node blocks of 512 nodes. Of the 4096 edge slots of block b, exactly 256 have a source in each other block and the remaining 2304 a source in block b itself, in no particular order. `edge_target`: edges held by index b of blk point to nodes b * 512 to (b + 1) * 512 - 1 of that block, in non-decreasing order. The first edge_count[b] slots of block b are live edges, the others are padding. One block is full and one holds half of 4096.
All inputs are finite; a program needn't handle non-finite values.
Results may differ from the reference program's by a relative error of at most 0.008.
The reference program's roundings to bfloat16 on the way count: a program that leaves them out, or rounds other values in their place, can miss the bound.
Values may be sent and summed in bfloat16 or wider, within the bound.
A program may use at most 128 MiB of HBM per device.

```python
import math
import jax
import jax.numpy as jnp
from jax import lax

H = 128
EH = 128
EF = 16
STEPS = 2
GROUPS = 16
E_DEV = 4096
N_DEV = 512
BLOCKS = 8
EDGES = 32768
NODES = 4096


def shuffle_row(row_key, row_values):
    return jax.random.permutation(row_key, row_values)


def draw_edge_source(key, part):
    key = jax.random.fold_in(key, 37)
    block_key, node_key = jax.random.split(key)
    peer_rows = E_DEV // (2 * BLOCKS)
    slot_index = jnp.arange(E_DEV, dtype=jnp.int32)
    offset = jnp.where(slot_index < (BLOCKS - 1) * peer_rows, 1 + slot_index // peer_rows, 0)
    row_index = jnp.arange(BLOCKS, dtype=jnp.int32)[:, None]
    block_of = (row_index + offset[None, :]) % BLOCKS
    row_keys = jax.random.split(block_key, BLOCKS)
    shuffled = jax.vmap(shuffle_row)(row_keys, block_of)
    node_index = jax.random.randint(node_key, (BLOCKS, E_DEV), 0, N_DEV)
    return (shuffled * N_DEV + node_index).reshape(EDGES).astype(jnp.int32)


def draw_edge_target(key, part):
    key = jax.random.fold_in(key, 11)
    local_index = jax.random.randint(key, (BLOCKS, E_DEV), 0, N_DEV)
    local_index = local_index.at[:, 0].set(0).at[:, E_DEV - 1].set(N_DEV - 1)
    local_index = jnp.sort(local_index, axis=1)
    offsets = jnp.arange(BLOCKS, dtype=jnp.int32)[:, None] * N_DEV
    return (local_index + offsets).reshape(EDGES).astype(jnp.int32)


def draw_edge_count(key, part):
    key = jax.random.fold_in(key, 23)
    first_key, second_key, third_key = jax.random.split(key, 3)
    counts = jax.random.randint(first_key, (BLOCKS,), E_DEV // 2, E_DEV + 1)
    full_block = jax.random.randint(second_key, (), 0, BLOCKS)
    half_block = (full_block + 1 + jax.random.randint(third_key, (), 0, BLOCKS - 1)) % BLOCKS
    counts = counts.at[full_block].set(E_DEV).at[half_block].set(E_DEV // 2)
    return counts.astype(jnp.int32)


def with_ends(entries, own_key, least, largest):
    extent = entries.shape
    spot = [jax.random.randint(jax.random.fold_in(own_key, axis), (), 0, extent[axis]) for axis in range(len(extent))]
    entries = entries.at[tuple(spot)].set(least)
    longest = extent.index(max(extent))
    spot[longest] = (spot[longest] + 1) % extent[longest]
    return entries.at[tuple(spot)].set(largest)


def block_levels(stream_key, dims, cuts, smallest, high):
    gain = 1.0
    for dim, blocks in cuts:
        draws = jax.random.uniform(jax.random.fold_in(jax.random.fold_in(stream_key, 6), dim), (blocks,), jnp.float32, smallest / len(cuts), high / len(cuts))
        gain = gain * jnp.repeat(jnp.exp(draws), dims[dim] // blocks).reshape((-1,) + (1,) * (len(dims) - 1 - dim))
    return gain


def noise(own_key, dims, deviation, most, cuts=(), held_as=jnp.bfloat16):
    level = block_levels(own_key, dims, cuts, -0.22, 0.18) if cuts else 1.0
    drawn = jax.random.normal(own_key, dims, jnp.float32) * deviation * level
    return jnp.minimum(jnp.maximum(drawn, -most), most).astype(held_as)


def setup_inputs(seed: int = 0) -> dict:
    keys = jax.random.split(jax.random.key(seed), 17)
    node_states = noise(keys[0], (NODES, H), 1.0, 6.0, ((0, 8),), jnp.float32)
    edge_feats = noise(keys[1], (EDGES, EF), 1.0, 6.0, ((0, 8),))
    edge_source = draw_edge_source(jax.random.fold_in(keys[16], 71), 0)
    edge_target = draw_edge_target(jax.random.fold_in(keys[16], 71), 0)
    edge_group = with_ends(jax.random.randint(keys[4], (EDGES,), 0, GROUPS), jax.random.fold_in(keys[4], 1), 0, GROUPS - 1).astype(jnp.int32)
    column_mask = with_ends((jax.random.randint(keys[5], (GROUPS, EF), 0, 4) < 3).astype(jnp.int32), jax.random.fold_in(keys[5], 1), 0, 1)
    edge_count = draw_edge_count(jax.random.fold_in(keys[16], 71), 0)
    first_weight = noise(keys[7], (EF, EH), EF ** -0.5, 1.5)
    first_bias = noise(keys[8], (EH,), 0.5, 3.0, (), jnp.float32)
    second_weight = noise(keys[9], (EH, H * H), (EH * H) ** -0.5, 0.046875, ((1, 4),))
    second_bias = noise(keys[10], (H * H,), 0.05, 0.3125, ((0, 4),), jnp.float32)
    update_input_weight = noise(keys[11], (H, 3 * H), H ** -0.5, 0.5)
    update_state_weight = noise(keys[12], (H, 3 * H), H ** -0.5, 0.5)
    update_input_bias = noise(keys[13], (3 * H,), 0.3, 1.75, (), jnp.float32)
    update_state_bias = noise(keys[14], (3 * H,), 0.3, 1.75, (), jnp.float32)
    state_cotangent = noise(keys[15], (NODES, H), 1.0, 6.0, ((0, 8),), jnp.float32)
    return {"node_states": node_states, "edge_feats": edge_feats, "edge_source": edge_source, "edge_target": edge_target, "edge_group": edge_group, "column_mask": column_mask, "edge_count": edge_count, "first_weight": first_weight, "first_bias": first_bias, "second_weight": second_weight, "second_bias": second_bias, "update_input_weight": update_input_weight, "update_state_weight": update_state_weight, "update_input_bias": update_input_bias, "update_state_bias": update_state_bias, "state_cotangent": state_cotangent}


@jax.custom_vjp
def low(v):
    return lax.optimization_barrier(v.astype(jnp.bfloat16)).astype(jnp.float32)

@jax.custom_vjp
def low_back(v):
    return v

def low_keep(v):
    return (low(v), None)

def low_pass(kept, grad):
    return (grad,)

def back_keep(v):
    return (v, None)

def back_low(kept, grad):
    return (low(grad),)
low.defvjp(low_keep, low_pass)
low_back.defvjp(back_keep, back_low)

def reference(node_states, edge_feats, edge_source, edge_target, edge_group, column_mask, edge_count, first_weight, first_bias, second_weight, second_bias, update_input_weight, update_state_weight, update_input_bias, update_state_bias, state_cotangent):
    highest = lax.Precision.HIGHEST
    group_mask = column_mask[edge_group].astype(jnp.float32)
    live_edge = (jnp.arange(E_DEV, dtype=jnp.int32)[None, :] < edge_count[:, None]).reshape(EDGES).astype(jnp.float32)
    block_width = math.gcd(EDGES, 2048)
    block_total = EDGES // block_width
    source_blocks = edge_source.reshape(block_total, block_width)
    live_blocks = live_edge.reshape(block_total, block_width)

    def forward(start_states, features, weight_one, bias_one, weight_two, bias_two, input_weight, state_weight, input_bias, state_bias):
        masked = features * group_mask
        feat_blocks = masked.reshape(block_total, block_width, EF)
        state = start_states
        for layer_step in range(STEPS):
            state_low = low(state)

            def message_block(pieces, state_low=state_low):
                feat_block, source_block, live_block = pieces
                pre = jnp.dot(feat_block, weight_one, precision=highest) + bias_one
                hidden = low(jax.nn.silu(pre))
                flat = jnp.dot(hidden, weight_two, precision=highest) + bias_two
                matrices = low(low_back(flat)).reshape(block_width, H, H)
                sources = state_low[source_block]
                message = jnp.einsum('eij,ej->ei', matrices, sources, precision=highest)
                return message * live_block[:, None]
            messages = lax.map(jax.checkpoint(message_block), (feat_blocks, source_blocks, live_blocks)).reshape(EDGES, H)
            summed = jax.ops.segment_sum(messages, edge_target, num_segments=NODES)
            summed_low = low(low_back(summed))
            input_gates = jnp.dot(summed_low, input_weight, precision=highest) + input_bias
            state_gates = jnp.dot(state_low, state_weight, precision=highest) + state_bias
            reset = jax.nn.sigmoid(input_gates[:, :H] + state_gates[:, :H])
            update = jax.nn.sigmoid(input_gates[:, H:2 * H] + state_gates[:, H:2 * H])
            candidate = jnp.tanh(input_gates[:, 2 * H:] + reset * state_gates[:, 2 * H:])
            state = (1.0 - update) * candidate + update * state
        return state
    inputs = (node_states.astype(jnp.float32), edge_feats.astype(jnp.float32), first_weight.astype(jnp.float32), first_bias.astype(jnp.float32), second_weight.astype(jnp.float32), second_bias.astype(jnp.float32), update_input_weight.astype(jnp.float32), update_state_weight.astype(jnp.float32), update_input_bias.astype(jnp.float32), update_state_bias.astype(jnp.float32))
    final_states, pullback = jax.vjp(forward, *inputs)
    grads = pullback(state_cotangent.astype(jnp.float32))
    return (final_states, grads[0], grads[1], grads[2], grads[3], grads[4], grads[5], grads[6], grads[7], grads[8], grads[9])
```

```python
import functools
from types import SimpleNamespace

import jax
import jax.numpy as jnp
from jax import lax
from jax.experimental import pallas as pl
from jax.experimental.pallas import tpu as pltpu
from jax.sharding import PartitionSpec as P

STEPS = 2
TILE = 512
LO = 256
ROWS = 512
F32, BF16, I32 = jnp.float32, jnp.bfloat16, jnp.int32
MESH = pl.DeviceIdType.MESH
VMEM = pl.BlockSpec(memory_space=pltpu.VMEM)

ROW_STATE_WEIGHT = 384
ROW_INPUT_BIAS = 768
ROW_STATE_BIAS = 776
ROW_FIRST = 784
ROW_SECOND_BIAS = 896
SMALL_ROWS = 1024

(P_STATE, P_STATE2, P_WEIGHT, P_SPREAD, P_SPREAD2, P_GRAD, P_GRAD_ALL, P_SMALL_ALL) = range(8)
(
    Z_WEIGHT,
    Z_BIAS,
    Z_SUM,
    Z_SUM2,
    Z_STATE,
    Z_FINAL,
    Z_DELTA,
    Z_DELTA2,
    Z_SOURCE,
    Z_SOURCE2,
    Z_GRADS,
    Z_FEATS,
    Z_FEATS_ALL,
    Z_SECOND,
    Z_SMALL,
) = range(15)


def nn(a, b):
    return jnp.dot(a, b, preferred_element_type=F32)


def nt(a, b):
    return lax.dot_general(a, b, (((1,), (1,)), ((), ())), preferred_element_type=F32)


def iota(shape, dim):
    return lax.broadcasted_iota(I32, shape, dim)


def ones_where(condition):
    return jnp.where(condition, 1.0, 0.0).astype(BF16)


def eye(n):
    return ones_where(iota((n, n), 0) == iota((n, n), 1))


def two(x):
    high = x.astype(BF16)
    return high, (x - high.astype(F32)).astype(BF16)


def three(x):
    high, rest = x.astype(BF16), x
    rest = x - high.astype(F32)
    mid = rest.astype(BF16)
    return high, mid, (rest - mid.astype(F32)).astype(BF16)


def nn2(a, x):
    high, low = two(x)
    return nn(a, high) + nn(a, low)


def nt2(x, b):
    high, low = two(x)
    return nt(high, b) + nt(low, b)


def sizes(mesh, edges, nodes, width):
    s = SimpleNamespace()
    s.B, s.R = mesh.shape["blk"], mesh.shape["rep"]
    s.E, s.N, s.H = edges, nodes, width
    s.J = width // s.R
    s.HIB = nodes // LO
    s.HI = s.HIB * s.B
    s.NQ = nodes // s.R
    s.EQ = edges // s.R
    s.OW = min(s.B, 8)
    s.STRIDE = s.B // s.OW
    s.T = s.J // s.OW
    s.KEEP = s.B <= 8
    s.SMALL = SMALL_ROWS // s.OW
    return s


def scratch(s):
    v = pltpu.VMEM
    jh = s.J * s.H
    shapes = dict(
        nst=v((s.H, s.N), F32),
        stq=v((STEPS, s.HIB, s.J, LO), BF16),
        tab=v((STEPS, s.B, s.HIB, s.J, LO), BF16),
        ys=v((s.R * s.T, s.J, s.H), F32),
        wsend=v((s.R, s.T, s.J, s.H), BF16),
        w2r=v((s.J, s.H, s.H), BF16),
        b2f=v((s.H, s.H), F32),
        baug=v((jh + SMALL_ROWS, s.H), BF16),
        w2k=v((s.H, jh), BF16),
        tl=v((1, s.E), I32),
        ohln=v((s.E, LO), BF16),
        mt=v((32, s.E), BF16),
        gm=v((16, s.E), BF16),
        ht=v((s.H, s.E), BF16),
        st=v((STEPS, s.J, s.E), BF16),
        smt=v((2 * s.H + s.J, s.N), F32),
        ssum=v((STEPS, s.J, s.N), F32),
        rsq=v((s.R, s.H, s.NQ), F32),
        rsl=v((STEPS, s.R, s.H, s.NQ), F32),
        keep=v((STEPS, 5, s.NQ, s.H), F32),
        keept=v((STEPS, 2, s.H, s.NQ), BF16),
        nsq=v((s.H, s.NQ), BF16),
        fin=v((s.NQ, s.H), F32),
        gq=v((STEPS, s.NQ, s.H), BF16),
        gfull=v((STEPS, s.N, s.H), BF16),
        gt=v((s.H, s.N), BF16),
        hg=v((s.H, s.E), F32),
        o=v((jh // 2, TILE), BF16),
        gacc=v((jh, s.H), F32),
        xs=v((ROWS, TILE), BF16),
        scat=v((s.HI * s.J, LO), F32),
        rps=v((s.B, s.HIB * s.J, LO), BF16),
        rpl=v((STEPS, s.B, s.HIB * s.J, LO), BF16),
        fzs=v((STEPS, s.R, s.J, s.NQ), F32),
        fzl=v((STEPS, s.R, s.J, s.NQ), F32),
        gradq=v((s.NQ, s.H), F32),
        small=v((SMALL_ROWS, s.H), F32),
        gland=v((s.B, jh // s.OW + s.SMALL, s.H), BF16),
        gz=v((s.R, s.T * s.J, s.H), BF16),
        sgz=v((s.R, s.SMALL, s.H), BF16),
        fqs=v((16, s.E), BF16),
        fql=v((s.R, 16, s.EQ), BF16),
        ps=pltpu.SemaphoreType.DMA((8, s.B)),
        pr=pltpu.SemaphoreType.DMA((8, s.B)),
        zs=pltpu.SemaphoreType.DMA((15, s.R)),
        zr=pltpu.SemaphoreType.DMA((15, s.R)),
        local=pltpu.SemaphoreType.DMA,
    )
    if not s.KEEP:
        shapes["gsend"] = v((jh + SMALL_ROWS, s.H), BF16)
    if s.KEEP:
        shapes["mat"] = v((jh, s.E), BF16)
    return shapes


IN_NAMES = (
    ["nodes", "feats", "src", "tgt", "grp", "cmask", "count", "w1", "b1"]
    + ["w2", "b2", "win", "wst", "bin", "bst", "cot"]
)
OUT_NAMES = ["final", "grads", "ff", "f", "sgf"]


def whole(s, names, *refs):
    c = SimpleNamespace(**dict(zip(names, refs)))
    B, R, H, J, E, N, NQ, EQ = s.B, s.R, s.H, s.J, s.E, s.N, s.NQ, s.EQ
    T, OW, STRIDE = s.T, s.OW, s.STRIDE
    jh = J * H
    tiles = E // TILE
    b = lax.axis_index("blk")
    r = lax.axis_index("rep")
    owner = b // STRIDE
    is_owner = lax.rem(b, STRIDE) == 0
    sent = []

    def push(src, dst, sems, rems, axis, peer):
        return pltpu.make_async_remote_copy(
            src_ref=src,
            dst_ref=dst,
            send_sem=sems,
            recv_sem=rems,
            device_id={axis: peer},
            device_id_type=MESH,
        )

    def plane(x, src_of, dst):
        copies = []
        for d in range(1, B):
            peer = lax.rem(b + d, B)
            cp = push(src_of(peer), dst, c.ps.at[x, d], c.pr.at[x, d], "blk", peer)
            cp.start()
            copies.append(cp)
        sent.extend(copies)
        return copies

    def line(x, src_of, dst):
        copies = []
        for d in range(1, R):
            peer = lax.rem(r + d, R)
            cp = push(src_of(peer), dst, c.zs.at[x, d], c.zr.at[x, d], "rep", peer)
            cp.start()
            copies.append(cp)
        sent.extend(copies)
        return copies

    def arrive(copies, reuse=False):
        for cp in copies:
            cp.wait_recv()
        if reuse:
            for cp in copies:
                cp.wait_send()
                sent[:] = [other for other in sent if other is not cp]

    def when_owner(fn):
        if STRIDE == 1:
            fn()
        else:
            pl.when(is_owner)(fn)

    def line_owner(x, src_of, dst):
        copies = []
        for d in range(1, R):
            peer = lax.rem(r + d, R)
            copies.append(push(src_of(peer), dst, c.zs.at[x, d], c.zr.at[x, d], "rep", peer))
        when_owner(lambda: [cp.start() for cp in copies] and None)
        owner_sent.extend(copies)
        return copies

    owner_sent = []

    def from_owners(x, src, dst_of):
        if STRIDE == 1:
            copies = plane(x, lambda peer: src, dst_of(owner))
            return lambda: arrive(copies)
        copies = []
        for d in range(1, B):
            peer = lax.rem(b + d, B)
            copies.append(push(src, dst_of(owner), c.ps.at[x, d], c.pr.at[x, owner], "blk", peer))
        when_owner(lambda: [cp.start() for cp in copies] and None)
        owner_sent.extend(copies)

        def wait():
            for q in range(OW):

                @pl.when(b != q * STRIDE)
                def _():
                    push(
                        src, dst_of(q), c.ps.at[x, 0], c.pr.at[x, q], "blk", lax.rem(b + 1, B)
                    ).wait_recv()

        return wait

    def to_owners(x, src_of, dst):
        if STRIDE == 1:
            copies = plane(x, src_of, dst)
            return lambda: arrive(copies)
        for q in range(OW):

            @pl.when(b != q * STRIDE)
            def _():
                push(src_of(q), dst, c.ps.at[x, q], c.pr.at[x, b], "blk", q * STRIDE).start()

        def wait():
            def arrivals():
                for d in range(1, B):
                    peer = lax.rem(b + d, B)
                    push(src_of(0), dst, c.ps.at[x, 0], c.pr.at[x, peer], "blk", peer).wait_recv()

            when_owner(arrivals)
            for q in range(OW):

                @pl.when(b != q * STRIDE)
                def _():
                    push(src_of(q), dst, c.ps.at[x, q], c.pr.at[x, b], "blk", q * STRIDE).wait_send()

        return wait

    def edges(t):
        return pl.ds(pl.multiple_of(t * TILE, TILE), TILE)

    barrier = pltpu.get_barrier_semaphore()
    for d in range(1, B):
        pl.semaphore_signal(
            barrier, inc=1, device_id={"blk": lax.rem(b + d, B)}, device_id_type=MESH
        )
    for d in range(1, R):
        pl.semaphore_signal(
            barrier, inc=1, device_id={"rep": lax.rem(r + d, R)}, device_id_type=MESH
        )

    weight_copy = pltpu.make_async_copy(c.w2, c.w2k, c.local)
    weight_copy.start()
    eye_h = eye(H)
    part = pl.ds(pl.multiple_of(r * J, J), J)

    c.nst[...] = c.nodes[...].T
    own_columns = c.nst[part, :].astype(BF16)
    for k in range(s.HIB):
        c.stq[0, k] = own_columns[:, k * LO : (k + 1) * LO]
    c.tab[0, b] = c.stq[0]
    row = iota((R * T, H), 0)
    pick = ones_where(iota((R * T, H), 1) == (row // T) * J + T * owner + lax.rem(row, T))
    weight_copy.wait()
    for i in range(J):
        c.ys[:, i, :] = nt(pick, c.w2k[:, i * H : (i + 1) * H])
    c.wsend[...] = c.ys[...].astype(BF16).reshape(R, T, J, H)
    pl.semaphore_wait(barrier, B - 1 + R - 1)

    states_in = plane(P_STATE, lambda peer: c.stq.at[0], c.tab.at[0, b])
    strip = pl.ds(pl.multiple_of(T * owner, T), T)
    weight_in = line_owner(Z_WEIGHT, lambda peer: c.wsend.at[peer], c.w2r.at[strip, part, :])
    c.b2f[part, :] = c.b2[...]
    bias_in = line(Z_BIAS, lambda peer: c.b2, c.b2f.at[part, :])

    def own_strip():
        c.w2r[strip, part, :] = c.wsend[r]

    when_owner(own_strip)

    place = iota((1, E), 1)
    c.tl[...] = jnp.where(place < c.count[...], c.tgt[...] - b * N, -1)
    cmt = nt(eye(16), c.cmask[...].astype(F32).astype(BF16)).astype(BF16)
    b1 = three(c.b1[...])
    first = jnp.concatenate(
        [c.w1[...].astype(F32)] + [x.astype(F32) for x in b1] + [jnp.zeros((13, H), F32)], axis=0
    ).astype(BF16)
    w1ta = nt(eye_h, first).astype(BF16)
    eye_t = eye(LO)

    def target_rows(t):
        return ones_where(iota((N, TILE), 0) == c.tl[:, edges(t)])

    def low_rows(t):
        return ones_where(iota((LO, TILE), 0) == (c.src[:, edges(t)] & (LO - 1)))

    def prepare(t, carry):
        e = edges(t)
        groups = ones_where(iota((16, TILE), 0) == c.grp[:, e])
        gm = nn(cmt, groups)
        c.gm[:, e] = gm.astype(BF16)
        masked = c.feats[:, e].astype(F32) * gm
        ones = jnp.where(iota((16, TILE), 0) < 3, 1.0, 0.0)
        mt = jnp.concatenate([masked, ones], axis=0).astype(BF16)
        c.mt[:, e] = mt
        pre = nn(w1ta, mt)
        c.ht[:, e] = (pre * jax.nn.sigmoid(pre)).astype(BF16)
        lows = low_rows(t)
        for k in range(TILE // LO):
            rows = pl.ds(pl.multiple_of(t * TILE + k * LO, LO), LO)
            c.ohln[rows, :] = nt(eye_t, lows[:, k * LO : (k + 1) * LO]).astype(BF16)
        return carry

    lax.fori_loop(0, tiles, prepare, 0)

    when_owner(lambda: arrive(weight_in))
    weight_wait = from_owners(
        P_WEIGHT,
        c.w2r.at[strip],
        lambda q: c.w2r.at[pl.ds(pl.multiple_of(T * q, T), T)],
    )

    def gather(step):
        def one(t, carry):
            e = edges(t)
            lows = low_rows(t)
            high = c.src[:, e] // LO
            total = jnp.zeros((J, TILE), F32)
            per = ROWS // J
            for g in range(s.HI // per):
                blocks = per // s.HIB
                table = c.tab[step, g * blocks : (g + 1) * blocks].reshape(ROWS, LO)
                rows = nn(table, lows)
                for k in range(per):
                    total = total + jnp.where(high == g * per + k, rows[k * J : (k + 1) * J], 0.0)
            c.st[step, :, e] = total.astype(BF16)
            return carry

        lax.fori_loop(0, tiles, one, 0)

    arrive(states_in)
    gather(0)

    arrive(bias_in)
    b2 = jnp.concatenate(three(c.b2f[...]), axis=1)

    def bias_columns(j, carry):
        at = iota((3 * H, H), 0)
        to = iota((3 * H, H), 1)
        move = ones_where((lax.rem(at, H) == r * J + j) & (to == at // H))
        c.baug[pl.ds(pl.multiple_of(j * H, H), H), :] = nn(b2, move).astype(BF16)
        return carry

    lax.fori_loop(0, J, bias_columns, 0)
    weight_wait()

    def turned(j, carry):
        c.w2k[:, pl.ds(pl.multiple_of(j * H, H), H)] = nt(eye_h, c.w2r[j]).astype(BF16)
        return carry

    lax.fori_loop(0, J, turned, 0)

    chunk = ROWS // H

    def hidden_rows(e):
        ones = jnp.where(iota((H, TILE), 0) < 3, 1.0, 0.0).astype(BF16)
        return jnp.concatenate([c.ht[:, e], ones], axis=0)

    def matrices(k, e, hidden, store):
        rows = slice(k * ROWS, (k + 1) * ROWS)
        if s.KEEP and not store:
            return c.mat[rows, e].astype(F32)
        left = jnp.concatenate(
            [c.w2r[k * chunk : (k + 1) * chunk].reshape(ROWS, H), c.baug[rows, :]], axis=1
        )
        low = nn(left, hidden).astype(BF16)
        if s.KEEP:
            c.mat[rows, e] = low
        return low.astype(F32)

    def messages(step):
        c.smt[...] = jnp.zeros_like(c.smt)

        def one(t, carry):
            e = edges(t)
            hidden = None if s.KEEP and step > 0 else hidden_rows(e)
            low = c.st[step, :, e]
            source = low.astype(F32)
            total = jnp.zeros((H, TILE), F32)
            for k in range(J // chunk):
                m = matrices(k, e, hidden, step == 0)
                for q in range(chunk):
                    j = k * chunk + q
                    total = total + m[q * H : (q + 1) * H] * source[j : j + 1, :]
            high, rest = two(total)
            rows = jnp.concatenate([high, rest, low], axis=0)
            c.smt[...] += nt(rows, target_rows(t))
            return carry

        lax.fori_loop(0, tiles, one, 0)
        summed = c.smt[0:H, :] + c.smt[H : 2 * H, :]
        c.ssum[step] = c.smt[2 * H : 2 * H + J, :]
        for q in range(R):
            c.rsq[q] = summed[:, q * NQ : (q + 1) * NQ]
        c.rsl[step, r] = c.rsq[r]
        return line(Z_SUM + step, lambda peer: c.rsq.at[peer], c.rsl.at[step, r])

    def gates(step, before, before_t):
        summed = c.rsl[step, 0]
        for q in range(1, R):
            summed = summed + c.rsl[step, q]
        summed_low = summed.T.astype(BF16)
        gi = nn(summed_low, c.win[...]) + c.bin[...]
        gs = nn(before.astype(BF16), c.wst[...]) + c.bst[...]
        reset = jax.nn.sigmoid(gi[:, :H] + gs[:, :H])
        update = jax.nn.sigmoid(gi[:, H : 2 * H] + gs[:, H : 2 * H])
        state_part = gs[:, 2 * H :]
        candidate = jnp.tanh(gi[:, 2 * H :] + reset * state_part)
        for k, x in enumerate((before, reset, update, candidate, state_part)):
            c.keep[step, k] = x
        c.keept[step, 0] = summed.astype(BF16)
        c.keept[step, 1] = before_t
        return (1.0 - update) * candidate + update * before

    nodes_here = pl.ds(pl.multiple_of(r * NQ, NQ), NQ)
    sums = messages(0)
    arrive(sums, reuse=True)
    state = gates(0, c.nodes[nodes_here, :], c.nst[:, nodes_here].astype(BF16))
    state_t = state.T.astype(BF16)
    c.nsq[...] = state_t
    hib = r // (LO // NQ)
    lanes = pl.ds(pl.multiple_of(lax.rem(r, LO // NQ) * NQ, NQ), NQ)
    c.stq[1, hib, :, lanes] = c.nsq[part, :]
    pieces = line(
        Z_STATE,
        lambda peer: c.nsq.at[pl.ds(pl.multiple_of(peer * J, J), J), :],
        c.stq.at[1, hib, :, lanes],
    )
    arrive(pieces)
    c.tab[1, b] = c.stq[1]
    arrive(plane(P_STATE2, lambda peer: c.stq.at[1], c.tab.at[1, b]))
    gather(1)
    sums = messages(1)
    arrive(sums)
    final = gates(1, state, state_t)
    c.fin[...] = final
    c.final[nodes_here, :] = final
    final_in = line(Z_FINAL, lambda peer: c.fin, c.final.at[nodes_here, :])

    c.small[...] = jnp.zeros_like(c.small)
    c.gacc[...] = jnp.zeros_like(c.gacc)

    def deltas(step, grad):
        before, reset, update, candidate, state_part = [c.keep[step, k] for k in range(5)]
        dn = grad * (1.0 - update)
        dz = grad * (before - candidate)
        dpn = dn * (1.0 - candidate * candidate)
        dpz = dz * update * (1.0 - update)
        dpr = dpn * state_part * reset * (1.0 - reset)
        to_input = jnp.concatenate([dpr, dpz, dpn], axis=1)
        to_state = jnp.concatenate([dpr, dpz, dpn * reset], axis=1)
        summed_grad = nt2(to_input, c.win[...]).astype(BF16)
        c.gq[step] = summed_grad
        c.gfull[step, nodes_here, :] = summed_grad
        copies = line(Z_DELTA + step, lambda peer: c.gq.at[step], c.gfull.at[step, nodes_here, :])
        gwi = nn2(c.keept[step, 0], to_input)
        gws = nn2(c.keept[step, 1], to_state)
        gbi = jnp.sum(to_input, axis=0, keepdims=True)
        gbs = jnp.sum(to_state, axis=0, keepdims=True)
        for k in range(3):
            cut = slice(k * H, (k + 1) * H)
            c.small[k * H : (k + 1) * H, :] += gwi[:, cut]
            c.small[ROW_STATE_WEIGHT + k * H : ROW_STATE_WEIGHT + (k + 1) * H, :] += gws[:, cut]
            c.small[ROW_INPUT_BIAS + k : ROW_INPUT_BIAS + k + 1, :] += gbi[:, cut]
            c.small[ROW_STATE_BIAS + k : ROW_STATE_BIAS + k + 1, :] += gbs[:, cut]
        c.gradq[...] = grad * update + nt2(to_state, c.wst[...])
        return copies

    def node_grads(step):
        c.gt[...] = nt(eye_h, c.gfull[step]).astype(BF16)
        rows = pl.ds(ROW_SECOND_BIAS + pl.multiple_of(r * J, J), J)
        high, low = two(c.ssum[step])
        c.small[rows, :] += nn(high, c.gfull[step]) + nn(low, c.gfull[step])

    def weights_tile(step, t):
        e = edges(t)
        at_edges = nn(c.gt[...], target_rows(t)).astype(BF16)
        source = c.st[step, :, e].astype(F32)
        got = None if step == STEPS - 1 else c.hg[:, e]
        half = J // 2
        for part_of in range(2):
            for q in range(half):
                j = part_of * half + q
                spread_row = jnp.broadcast_to(source[j : j + 1, :], (16, TILE)).astype(BF16)
                c.o[q * H : (q + 1) * H, :] = (
                    at_edges.reshape(H // 16, 16, TILE) * spread_row[None]
                ).reshape(H, TILE)
            base = part_of * half * H
            more = nn(c.w2k[:, base : base + half * H], c.o[...])
            got = more if got is None else got + more
            for k in range(half * H // ROWS):
                rows = slice(base + k * ROWS, base + (k + 1) * ROWS)
                c.gacc[rows, :] += nt(c.o[k * ROWS : (k + 1) * ROWS, :], c.ht[:, e])
        c.hg[:, e] = got

    def weights(step, begin, end):
        def one(t, carry):
            weights_tile(step, t)
            return carry

        lax.fori_loop(begin, end, one, 0)

    def sources(step):
        c.scat[...] = jnp.zeros_like(c.scat)

        def one(t, carry):
            e = edges(t)
            hidden = None if s.KEEP else hidden_rows(e)
            at_edges = nn(c.gt[...], target_rows(t))
            parts = []
            for k in range(J // chunk):
                m = matrices(k, e, hidden, False)
                for q in range(chunk):
                    parts.append(
                        jnp.sum(m[q * H : (q + 1) * H] * at_edges, axis=0, keepdims=True)
                    )
            got = jnp.concatenate(parts, axis=0)
            high = c.src[:, e] // LO
            per = ROWS // J
            for g in range(s.HI // per):
                for k in range(per):
                    c.xs[k * J : (k + 1) * J, :] = jnp.where(high == g * per + k, got, 0.0).astype(
                        BF16
                    )
                c.scat[g * ROWS : (g + 1) * ROWS, :] += nn(c.xs[...], c.ohln[e, :])
            return carry

        lax.fori_loop(0, tiles, one, 0)
        c.rps[...] = c.scat[...].astype(BF16).reshape(B, s.HIB * J, LO)
        c.rpl[step, b] = c.rps[b]
        return plane(P_SPREAD + step, lambda peer: c.rps.at[peer], c.rpl.at[step, b])

    def share_sources(step):
        total = c.rpl[step, 0].astype(F32)
        for q in range(1, B):
            total = total + c.rpl[step, q].astype(F32)
        for q in range(R):
            k, lane = (q * NQ) // LO, (q * NQ) % LO
            c.fzs[step, q] = total[k * J : (k + 1) * J, lane : lane + NQ]
        c.fzl[step, r] = c.fzs[step, r]
        return line(Z_SOURCE + step, lambda peer: c.fzs.at[step, peer], c.fzl.at[step, r])

    def state_grad(step):
        return c.gradq[...] + c.fzl[step].reshape(H, NQ).T

    last = STEPS - 1
    copies = deltas(last, c.cot[nodes_here, :])
    arrive(copies)
    node_grads(last)
    spread = sources(last)
    weights(last, 0, 3)
    arrive(spread, reuse=True)
    pieces = share_sources(last)
    weights(last, 3, 4)
    arrive(pieces)
    copies = deltas(0, state_grad(last))
    weights(last, 4, tiles)
    arrive(copies)
    node_grads(0)
    weights(0, 0, tiles)

    w1 = c.w1[...]

    def first_layer(t, carry):
        e = edges(t)
        mt = c.mt[:, e]
        pre = nn(w1ta, mt)
        gate = jax.nn.sigmoid(pre)
        pre_grad = c.hg[:, e] * gate * (1.0 + pre * (1.0 - gate))
        high, low = two(pre_grad)
        c.fqs[:, e] = ((nn(w1, high) + nn(w1, low)) * c.gm[:, e].astype(F32)).astype(BF16)
        c.small[ROW_FIRST : ROW_FIRST + 32, :] += nt(mt, high) + nt(mt, low)
        return carry

    lax.fori_loop(0, tiles, first_layer, 0)
    edges_here = pl.ds(pl.multiple_of(r * EQ, EQ), EQ)
    c.fql[r] = c.fqs[:, edges_here]
    feats_in = line(
        Z_FEATS,
        lambda peer: c.fqs.at[:, pl.ds(pl.multiple_of(peer * EQ, EQ), EQ)],
        c.fql.at[r],
    )

    per_owner = jh // OW
    piece = per_owner + s.SMALL
    outgoing = c.baug if s.KEEP else c.gsend
    for q in range(OW):
        at = q * piece
        outgoing[at : at + per_owner, :] = c.gacc[q * per_owner : (q + 1) * per_owner, :].astype(
            BF16
        )
        outgoing[at + per_owner : at + piece, :] = c.small[
            q * s.SMALL : (q + 1) * s.SMALL, :
        ].astype(BF16)

    def piece_of(q):
        return pl.ds(pl.multiple_of(q * piece, 16), piece)

    def own_grads():
        c.gland[b] = outgoing[piece_of(owner), :]

    when_owner(own_grads)
    grads_wait = to_owners(P_GRAD, lambda q: outgoing.at[piece_of(q), :], c.gland.at[b])

    spread = sources(0)

    grads_wait()

    def reduce_grads():
        for t in range(T):
            rows = slice(t * H, (t + 1) * H)
            total = c.gland[0, rows, :].astype(F32)
            for q in range(1, B):
                total = total + c.gland[q, rows, :].astype(F32)
            total = total.astype(BF16)
            for q in range(R):
                c.gz[q, t * J : (t + 1) * J, :] = total[q * J : (q + 1) * J, :]
        rows = slice(per_owner, per_owner + s.SMALL)
        total = c.gland[0, rows, :].astype(F32)
        for q in range(1, B):
            total = total + c.gland[q, rows, :].astype(F32)
        c.sgz[r] = total.astype(BF16)
        c.f[r, owner] = c.gz[r]

    when_owner(reduce_grads)
    second_in = line_owner(Z_SECOND, lambda peer: c.gz.at[peer], c.f.at[r, owner])
    small_in = line_owner(Z_SMALL, lambda peer: c.sgz.at[r], c.sgz.at[r])

    arrive(feats_in)
    feats = c.fql[0].astype(F32)
    for q in range(1, R):
        feats = feats + c.fql[q].astype(F32)
    c.ff[:, edges_here] = feats.astype(BF16)
    feats_all = line(Z_FEATS_ALL, lambda peer: c.ff.at[:, edges_here], c.ff.at[:, edges_here])

    arrive(spread)
    pieces = share_sources(0)

    when_owner(lambda: arrive(second_in))
    second_wait = from_owners(P_GRAD_ALL, c.f.at[:, owner], lambda q: c.f.at[:, q])

    def sum_small():
        arrive(small_in)
        total = c.sgz[0].astype(F32)
        for q in range(1, R):
            total = total + c.sgz[q].astype(F32)
        c.sgf[owner] = total.astype(BF16)

    when_owner(sum_small)
    small_wait = from_owners(P_SMALL_ALL, c.sgf.at[owner], lambda q: c.sgf.at[q])

    arrive(pieces)
    grad = state_grad(0)
    c.gradq[...] = grad
    c.grads[nodes_here, :] = grad
    grads_in = line(Z_GRADS, lambda peer: c.gradq, c.grads.at[nodes_here, :])

    arrive(feats_all)
    arrive(final_in)
    second_wait()
    small_wait()
    arrive(grads_in)
    for cp in sent:
        cp.wait_send()
    when_owner(lambda: [cp.wait_send() for cp in owner_sent] and None)


def finish(s, f_ref, ff_ref, sg_ref, feats_ref, w2_ref, win_ref, wst_ref, bin_ref, bst_ref, w1_ref, b1_ref, b2_ref, wide, turn):
    H, J = s.H, s.J
    wide[...] = f_ref[...].reshape(H * J, H).astype(F32)
    for i in range(J):
        w2_ref[:, i * H : (i + 1) * H] = wide[pl.ds(i, H, stride=J), :].T
    small = sg_ref[...].reshape(SMALL_ROWS, H).astype(F32)
    for k in range(3):
        cut = slice(k * H, (k + 1) * H)
        win_ref[:, cut] = small[k * H : (k + 1) * H]
        wst_ref[:, cut] = small[ROW_STATE_WEIGHT + k * H : ROW_STATE_WEIGHT + (k + 1) * H]
        bin_ref[:, cut] = small[ROW_INPUT_BIAS + k : ROW_INPUT_BIAS + k + 1]
        bst_ref[:, cut] = small[ROW_STATE_BIAS + k : ROW_STATE_BIAS + k + 1]
    w1_ref[...] = small[ROW_FIRST : ROW_FIRST + 16]
    b1_ref[...] = small[ROW_FIRST + 16 : ROW_FIRST + 17]
    turn[...] = small[ROW_SECOND_BIAS : ROW_SECOND_BIAS + H].T
    r = lax.axis_index("rep")
    b2_ref[...] = turn[pl.ds(pl.multiple_of(r * J, J), J), :]
    feats_ref[...] = ff_ref[...].astype(F32)


def body(
    s,
    node_states,
    edge_feats,
    edge_source,
    edge_target,
    edge_group,
    column_mask,
    edge_count,
    first_weight,
    first_bias,
    second_weight,
    second_bias,
    update_input_weight,
    update_state_weight,
    update_input_bias,
    update_state_bias,
    state_cotangent,
):
    H, N, E = s.H, s.N, s.E
    shapes = scratch(s)
    names = IN_NAMES + OUT_NAMES + list(shapes)
    sds = jax.ShapeDtypeStruct
    final, grads, ff, f, sgf = pl.pallas_call(
        functools.partial(whole, s, names),
        out_shape=[
            sds((N, H), F32),
            sds((N, H), F32),
            sds((16, E), BF16),
            sds((s.R, s.OW, s.T * s.J, H), BF16),
            sds((s.OW, s.SMALL, H), BF16),
        ],
        in_specs=[VMEM] * 9 + [pl.BlockSpec(memory_space=pl.ANY)] + [VMEM] * 6,
        out_specs=[VMEM] * 5,
        scratch_shapes=list(shapes.values()),
        compiler_params=pltpu.CompilerParams(
            collective_id=0, has_side_effects=True, vmem_limit_bytes=63 * 2**20
        ),
        name="edge_network",
    )(
        node_states,
        edge_feats.T,
        edge_source.reshape(1, E),
        edge_target.reshape(1, E),
        edge_group.reshape(1, E),
        column_mask,
        edge_count.reshape(1, 1),
        first_weight,
        first_bias.reshape(1, H),
        second_weight,
        second_bias.reshape(s.J, H),
        update_input_weight,
        update_state_weight,
        update_input_bias.reshape(1, 3 * H),
        update_state_bias.reshape(1, 3 * H),
        state_cotangent,
    )
    feats, w2, win, wst, bin_, bst, w1, b1, b2 = pl.pallas_call(
        functools.partial(finish, s),
        out_shape=[
            sds((16, E), F32),
            sds((H, s.J * H), F32),
            sds((H, 3 * H), F32),
            sds((H, 3 * H), F32),
            sds((1, 3 * H), F32),
            sds((1, 3 * H), F32),
            sds((16, H), F32),
            sds((1, H), F32),
            sds((s.J, H), F32),
        ],
        in_specs=[VMEM] * 3,
        out_specs=[VMEM] * 9,
        scratch_shapes=[pltpu.VMEM((H * s.J, H), F32), pltpu.VMEM((H, H), F32)],
        compiler_params=pltpu.CompilerParams(vmem_limit_bytes=32 * 2**20),
        name="finish",
    )(f, ff, sgf)
    return (
        final,
        grads,
        feats.T,
        w1,
        b1.reshape(-1),
        w2,
        b2.reshape(-1),
        win,
        wst,
        bin_.reshape(-1),
        bst.reshape(-1),
    )


def solution(mesh):
    in_specs = (
        P("blk", None),
        P("blk", None),
        P("blk"),
        P("blk"),
        P("blk"),
        P(),
        P("blk"),
        P(),
        P(),
        P(None, "rep"),
        P("rep"),
        P(),
        P(),
        P(),
        P(),
        P("blk", None),
    )
    out_specs = (
        P("blk", None),
        P("blk", None),
        P("blk", None),
        P(),
        P(),
        P(None, "rep"),
        P("rep"),
        P(),
        P(),
        P(),
        P(),
    )

    def run(*args):
        nodes, edges, width = args[0].shape[0], args[2].shape[0], args[0].shape[1]
        return body(sizes(mesh, edges, nodes, width), *args)

    return jax.shard_map(run, mesh=mesh, in_specs=in_specs, out_specs=out_specs, check_vma=False)
```

```python
import functools
from types import SimpleNamespace

import jax
import jax.numpy as jnp
from jax import lax
from jax.experimental import pallas as pl
from jax.experimental.pallas import tpu as pltpu
from jax.sharding import PartitionSpec as P

STEPS = 2
TILE = 512
LO = 256
ROWS = 512
SLAB = 32
F32, BF16, I32 = jnp.float32, jnp.bfloat16, jnp.int32
MESH = pl.DeviceIdType.MESH
VMEM = pl.BlockSpec(memory_space=pltpu.VMEM)

ROW_STATE_WEIGHT = 384
ROW_INPUT_BIAS = 768
ROW_STATE_BIAS = 776
ROW_FIRST = 784
ROW_SECOND_BIAS = 896
SMALL_ROWS = 1024

(
    P_STATE,
    P_STATE2,
    P_WEIGHT,
    P_WEIGHT_PAIR,
    P_SPREAD,
    P_SPREAD2,
    P_GRAD_PAIR,
    P_GRAD,
    P_SMALL,
    P_GRAD_ALL,
    P_GRAD_ALL_PAIR,
    PLANES,
) = range(12)
(
    Z_WEIGHT,
    Z_BIAS,
    Z_SUM,
    Z_SUM2,
    Z_STATE,
    Z_FINAL,
    Z_DELTA,
    Z_DELTA2,
    Z_SOURCE,
    Z_SOURCE2,
    Z_GRADS,
    Z_FEATS,
    Z_FEATS_ALL,
    Z_SECOND,
    Z_SMALL,
    LINES,
) = range(16)


def nn(a, b):
    return jnp.dot(a, b, preferred_element_type=F32)


def nt(a, b):
    return lax.dot_general(a, b, (((1,), (1,)), ((), ())), preferred_element_type=F32)


def iota(shape, dim):
    return lax.broadcasted_iota(I32, shape, dim)


def ones_where(condition):
    return jnp.where(condition, 1.0, 0.0).astype(BF16)


def eye(n):
    return ones_where(iota((n, n), 0) == iota((n, n), 1))


def two(x):
    high = x.astype(BF16)
    return high, (x - high.astype(F32)).astype(BF16)


def three(x):
    high, rest = x.astype(BF16), x
    rest = x - high.astype(F32)
    mid = rest.astype(BF16)
    return high, mid, (rest - mid.astype(F32)).astype(BF16)


def nn2(a, x):
    high, low = two(x)
    return nn(a, high) + nn(a, low)


def nt2(x, b):
    high, low = two(x)
    return nt(high, b) + nt(low, b)


def sizes(mesh, edges, nodes, width):
    s = SimpleNamespace()
    s.B, s.R = mesh.shape["blk"], mesh.shape["rep"]
    s.E, s.N, s.H = edges, nodes, width
    s.J = width // s.R
    s.HIB = nodes // LO
    s.HI = s.HIB * s.B
    s.NQ = nodes // s.R
    s.EQ = edges // s.R
    s.OW = min(s.B, 8)
    s.STRIDE = s.B // s.OW
    s.T = s.J // s.OW
    s.KEEP = s.B <= 8
    s.SMALL = SMALL_ROWS // s.OW
    s.C = s.B // 2
    return s


def scratch(s):
    v = pltpu.VMEM
    jh = s.J * s.H
    shapes = dict(
        nst=v((s.H, s.N), F32),
        stq=v((STEPS, s.HIB, s.J, LO), BF16),
        tab=v((STEPS, s.B, s.HIB, s.J, LO), BF16),
        ys=v((s.R * s.T, s.J, s.H), F32),
        wsend=v((s.R, s.T, s.J, s.H), BF16),
        w2r=v((s.J, s.H, s.H), BF16),
        b2f=v((s.H, s.H), F32),
        baug=v((jh, s.H), BF16),
        w2k=v((s.H, jh), BF16),
        tl=v((1, s.E), I32),
        ohln=v((s.E, LO), BF16),
        mt=v((32, s.E), BF16),
        gm=v((16, s.E), BF16),
        ht=v((s.H, s.E), BF16),
        st=v((STEPS, s.J, s.E), BF16),
        sf=v((s.J, s.E), F32),
        ge=v((s.H, s.E), BF16),
        smt=v((2 * s.H + s.J, s.N), F32),
        ssum=v((STEPS, s.J, s.N), F32),
        rsq=v((s.R, s.H, s.NQ), F32),
        rsl=v((STEPS, s.R, s.H, s.NQ), F32),
        keep=v((STEPS, 5, s.NQ, s.H), F32),
        keept=v((STEPS, 2, s.H, s.NQ), BF16),
        nsq=v((s.H, s.NQ), BF16),
        fin=v((s.NQ, s.H), F32),
        gq=v((STEPS, s.NQ, s.H), BF16),
        gfull=v((STEPS, s.N, s.H), BF16),
        hg=v((s.H, s.E), F32),
        o=v((jh // 2, TILE), BF16),
        gacc=v((jh, s.H), F32),
        xs=v((ROWS, TILE), BF16),
        scat=v((s.HI * s.J, LO), F32),
        rps=v((s.B, s.HIB * s.J, LO), BF16),
        rpl=v((STEPS, s.B, s.HIB * s.J, LO), BF16),
        fzs=v((STEPS, s.R, s.J, s.NQ), F32),
        fzl=v((STEPS, s.R, s.J, s.NQ), F32),
        gradq=v((s.NQ, s.H), F32),
        gradl=v((s.NQ, s.H), BF16),
        small=v((SMALL_ROWS, s.H), F32),
        sgsend=v((SMALL_ROWS, s.H), BF16),
        sgland=v((s.B, s.SMALL, s.H), BF16),
        gz=v((s.R, s.T * s.J, s.H), BF16),
        sgz=v((s.R, s.SMALL, s.H), BF16),
        fqs=v((16, s.E), BF16),
        fql=v((s.R, 16, s.EQ), BF16),
        ps=pltpu.SemaphoreType.DMA((PLANES, s.B)),
        pr=pltpu.SemaphoreType.DMA((PLANES, s.B)),
        zs=pltpu.SemaphoreType.DMA((LINES, s.R)),
        zr=pltpu.SemaphoreType.DMA((LINES, s.R)),
        local=pltpu.SemaphoreType.DMA,
    )
    piece = (jh // s.OW, s.H)
    if s.STRIDE == 1:
        shapes["gpair"] = v((s.C,) + piece, BF16)
        shapes["gsum"] = v((s.C,) + piece, BF16)
        shapes["gland"] = v((s.C,) + piece, BF16)
    else:
        shapes["gland"] = v((s.B,) + piece, BF16)
        shapes["gsend"] = v((jh, s.H), BF16)
    if s.KEEP:
        shapes["mat"] = v((jh, s.E), BF16)
    return shapes


IN_NAMES = (
    ["nodes", "feats", "src", "tgt", "grp", "cmask", "count", "w1", "b1"]
    + ["w2", "b2", "win", "wst", "bin", "bst", "cot"]
)
OUT_NAMES = ["final", "grads", "ff", "f"]


def whole(s, names, *refs):
    c = SimpleNamespace(**dict(zip(names, refs)))
    B, R, H, J, E, N, NQ, EQ = s.B, s.R, s.H, s.J, s.E, s.N, s.NQ, s.EQ
    T, OW, STRIDE = s.T, s.OW, s.STRIDE
    jh = J * H
    tiles = E // TILE
    b = lax.axis_index("blk")
    r = lax.axis_index("rep")
    owner = b // STRIDE
    is_owner = lax.rem(b, STRIDE) == 0
    sent = []

    def push(src, dst, sems, rems, axis, peer):
        return pltpu.make_async_remote_copy(
            src_ref=src,
            dst_ref=dst,
            send_sem=sems,
            recv_sem=rems,
            device_id={axis: peer},
            device_id_type=MESH,
        )

    def plane(x, src_of, dst):
        copies = []
        for d in range(1, B):
            peer = lax.rem(b + d, B)
            cp = push(src_of(peer), dst, c.ps.at[x, d], c.pr.at[x, d], "blk", peer)
            cp.start()
            copies.append(cp)
        sent.extend(copies)
        return copies

    def line(x, src_of, dst):
        copies = []
        for d in range(1, R):
            peer = lax.rem(r + d, R)
            cp = push(src_of(peer), dst, c.zs.at[x, d], c.zr.at[x, d], "rep", peer)
            cp.start()
            copies.append(cp)
        sent.extend(copies)
        return copies

    def arrive(copies, reuse=False):
        for cp in copies:
            cp.wait_recv()
        if reuse:
            for cp in copies:
                cp.wait_send()
                sent[:] = [other for other in sent if other is not cp]

    def when_owner(fn):
        if STRIDE == 1:
            fn()
        else:
            pl.when(is_owner)(fn)

    def line_owner(x, src_of, dst):
        copies = []
        for d in range(1, R):
            peer = lax.rem(r + d, R)
            copies.append(push(src_of(peer), dst, c.zs.at[x, d], c.zr.at[x, d], "rep", peer))
        when_owner(lambda: [cp.start() for cp in copies] and None)
        owner_sent.extend(copies)
        return copies

    owner_sent = []

    def from_owners(x, x2, strip_of):
        if STRIDE == 1:
            return gather_pairs(x, x2, strip_of)
        copies = []
        for d in range(1, B):
            peer = lax.rem(b + d, B)
            strip = strip_of(owner)
            copies.append(push(strip, strip, c.ps.at[x, d], c.pr.at[x, owner], "blk", peer))
        when_owner(lambda: [cp.start() for cp in copies] and None)
        owner_sent.extend(copies)

        def wait():
            for q in range(OW):

                @pl.when(b != q * STRIDE)
                def _():
                    strip = strip_of(q)
                    peer = lax.rem(b + 1, B)
                    push(strip, strip, c.ps.at[x, 0], c.pr.at[x, q], "blk", peer).wait_recv()

        return lambda: None, wait

    chip, core = b // 2, lax.rem(b, 2)

    def device(other, its_core):
        return 2 * lax.rem(other, s.C) + its_core

    def gather_pairs(x, x2, strip_of):
        first, then = [], []
        for m in range(1, s.C):
            mine = strip_of(b)
            first.append(
                push(mine, mine, c.ps.at[x, m], c.pr.at[x, m], "blk", device(chip + m, core))
            )
        for m in range(s.C):
            held = strip_of(device(chip + s.C - m, core))
            then.append(
                push(held, held, c.ps.at[x2, m], c.pr.at[x2, m], "blk", device(chip, 1 - core))
            )
        for cp in first + then[:1]:
            cp.start()

        def relay():
            for m in range(1, s.C):
                first[m - 1].wait_recv()
                then[m].start()

        def wait():
            arrive(then)

        sent.extend(first + then)
        return relay, wait

    def to_owners(x, src_of, dst):
        if STRIDE == 1:
            copies = plane(x, src_of, dst)
            return lambda: arrive(copies)
        for q in range(OW):

            @pl.when(b != q * STRIDE)
            def _():
                push(src_of(q), dst, c.ps.at[x, q], c.pr.at[x, b], "blk", q * STRIDE).start()

        def wait():
            def arrivals():
                for d in range(1, B):
                    peer = lax.rem(b + d, B)
                    push(src_of(0), dst, c.ps.at[x, 0], c.pr.at[x, peer], "blk", peer).wait_recv()

            when_owner(arrivals)
            for q in range(OW):

                @pl.when(b != q * STRIDE)
                def _():
                    push(src_of(q), dst, c.ps.at[x, q], c.pr.at[x, b], "blk", q * STRIDE).wait_send()

        return wait

    def edges(t):
        return pl.ds(pl.multiple_of(t * TILE, TILE), TILE)

    barrier = pltpu.get_barrier_semaphore()
    for d in range(1, B):
        pl.semaphore_signal(
            barrier, inc=1, device_id={"blk": lax.rem(b + d, B)}, device_id_type=MESH
        )
    for d in range(1, R):
        pl.semaphore_signal(
            barrier, inc=1, device_id={"rep": lax.rem(r + d, R)}, device_id_type=MESH
        )

    weight_copy = pltpu.make_async_copy(c.w2, c.w2k, c.local)
    weight_copy.start()
    eye_h = eye(H)
    part = pl.ds(pl.multiple_of(r * J, J), J)

    c.nst[...] = c.nodes[...].T
    own_columns = c.nst[part, :].astype(BF16)
    for k in range(s.HIB):
        c.stq[0, k] = own_columns[:, k * LO : (k + 1) * LO]
    c.tab[0, b] = c.stq[0]
    row = iota((R * T, H), 0)
    pick = ones_where(iota((R * T, H), 1) == (row // T) * J + T * owner + lax.rem(row, T))
    weight_copy.wait()
    for i in range(J):
        c.ys[:, i, :] = nt(pick, c.w2k[:, i * H : (i + 1) * H])
    c.wsend[...] = c.ys[...].astype(BF16).reshape(R, T, J, H)
    pl.semaphore_wait(barrier, B - 1 + R - 1)

    states_in = plane(P_STATE, lambda peer: c.stq.at[0], c.tab.at[0, b])
    strip = pl.ds(pl.multiple_of(T * owner, T), T)
    weight_in = line_owner(Z_WEIGHT, lambda peer: c.wsend.at[peer], c.w2r.at[strip, part, :])
    c.b2f[part, :] = c.b2[...]
    bias_in = line(Z_BIAS, lambda peer: c.b2, c.b2f.at[part, :])

    def own_strip():
        c.w2r[strip, part, :] = c.wsend[r]

    when_owner(own_strip)

    place = iota((1, E), 1)
    c.tl[...] = jnp.where(place < c.count[...], c.tgt[...] - b * N, -1)
    cmt = nt(eye(16), c.cmask[...].astype(F32).astype(BF16)).astype(BF16)
    b1 = three(c.b1[...])
    first = jnp.concatenate(
        [c.w1[...].astype(F32)] + [x.astype(F32) for x in b1] + [jnp.zeros((13, H), F32)], axis=0
    ).astype(BF16)
    w1ta = nt(eye_h, first).astype(BF16)
    eye_t = eye(LO)

    def target_rows(t):
        return ones_where(iota((N, TILE), 0) == c.tl[:, edges(t)])

    def low_rows(t):
        return ones_where(iota((LO, TILE), 0) == (c.src[:, edges(t)] & (LO - 1)))

    def prepare(t, carry):
        e = edges(t)
        groups = ones_where(iota((16, TILE), 0) == c.grp[:, e])
        gm = nn(cmt, groups)
        c.gm[:, e] = gm.astype(BF16)
        masked = c.feats[:, e].astype(F32) * gm
        ones = jnp.where(iota((16, TILE), 0) < 3, 1.0, 0.0)
        mt = jnp.concatenate([masked, ones], axis=0).astype(BF16)
        c.mt[:, e] = mt
        pre = nn(w1ta, mt)
        c.ht[:, e] = (pre * jax.nn.sigmoid(pre)).astype(BF16)
        lows = low_rows(t)
        for k in range(TILE // LO):
            rows = pl.ds(pl.multiple_of(t * TILE + k * LO, LO), LO)
            c.ohln[rows, :] = nt(eye_t, lows[:, k * LO : (k + 1) * LO]).astype(BF16)
        return carry

    lax.fori_loop(0, tiles, prepare, 0)

    when_owner(lambda: arrive(weight_in))
    weight_relay, weight_wait = from_owners(
        P_WEIGHT,
        P_WEIGHT_PAIR,
        lambda q: c.w2r.at[pl.ds(pl.multiple_of(T * q, T), T)],
    )

    def gather(step):
        def one(t, carry):
            e = edges(t)
            lows = low_rows(t)
            high = c.src[:, e] // LO
            total = jnp.zeros((J, TILE), F32)
            per = ROWS // J
            for g in range(s.HI // per):
                blocks = per // s.HIB
                table = c.tab[step, g * blocks : (g + 1) * blocks].reshape(ROWS, LO)
                rows = nn(table, lows)
                for k in range(per):
                    total = total + jnp.where(high == g * per + k, rows[k * J : (k + 1) * J], 0.0)
            c.st[step, :, e] = total.astype(BF16)
            c.sf[:, e] = total
            return carry

        lax.fori_loop(0, tiles, one, 0)

    arrive(states_in)
    gather(0)
    weight_relay()

    arrive(bias_in)
    b2 = jnp.concatenate(three(c.b2f[...]), axis=1)

    def bias_columns(j, carry):
        at = iota((3 * H, H), 0)
        to = iota((3 * H, H), 1)
        move = ones_where((lax.rem(at, H) == r * J + j) & (to == at // H))
        c.baug[pl.ds(pl.multiple_of(j * H, H), H), :] = nn(b2, move).astype(BF16)
        return carry

    lax.fori_loop(0, J, bias_columns, 0, unroll=8)
    weight_wait()

    def turned(j, carry):
        c.w2k[:, pl.ds(pl.multiple_of(j * H, H), H)] = nt(eye_h, c.w2r[j]).astype(BF16)
        return carry

    lax.fori_loop(0, J, turned, 0, unroll=8)

    chunk = ROWS // H

    def hidden_rows(e):
        ones = jnp.where(iota((H, TILE), 0) < 3, 1.0, 0.0).astype(BF16)
        return jnp.concatenate([c.ht[:, e], ones], axis=0)

    def held_messages(e):
        parts = []
        for k in range(H // SLAB):
            total = jnp.zeros((SLAB, TILE), F32)
            for j in range(J):
                at = j * H + k * SLAB
                total = total + c.mat[at : at + SLAB, e].astype(F32) * c.sf[j : j + 1, e]
            parts.append(total)
        return jnp.concatenate(parts, axis=0)

    def held_sources(e):
        grads = c.ge[:, e]
        half, few = J // 2, H // 2
        rows = iota((half, half * few), 0)
        sums = ones_where(rows == iota((half, half * few), 1) // few)
        parts = []
        for k in range(2):
            held = c.mat[k * half * H : (k + 1) * half * H, e].reshape(half, H, TILE)
            product = held * grads[None]
            product = product[:, :few] + product[:, few:]
            parts.append(nn(sums, product.reshape(half * few, TILE)))
        return jnp.concatenate(parts, axis=0)

    def matrices(k, e, hidden):
        rows = slice(k * ROWS, (k + 1) * ROWS)
        left = jnp.concatenate(
            [c.w2r[k * chunk : (k + 1) * chunk].reshape(ROWS, H), c.baug[rows, :]], axis=1
        )
        low = nn(left, hidden).astype(BF16)
        if s.KEEP:
            c.mat[rows, e] = low
        return low.astype(F32)

    def messages(step):
        c.smt[...] = jnp.zeros_like(c.smt)

        def one(t, carry):
            e = edges(t)
            low = c.st[step, :, e]
            if s.KEEP and step > 0:
                total = held_messages(e)
            else:
                source = low.astype(F32)
                hidden = hidden_rows(e)
                total = jnp.zeros((H, TILE), F32)
                for k in range(J // chunk):
                    m = matrices(k, e, hidden)
                    for q in range(chunk):
                        j = k * chunk + q
                        total = total + m[q * H : (q + 1) * H] * source[j : j + 1, :]
            high, rest = two(total)
            rows = jnp.concatenate([high, rest, low], axis=0)
            c.smt[...] += nt(rows, target_rows(t))
            return carry

        lax.fori_loop(0, tiles, one, 0)
        summed = c.smt[0:H, :] + c.smt[H : 2 * H, :]
        c.ssum[step] = c.smt[2 * H : 2 * H + J, :]
        for q in range(R):
            c.rsq[q] = summed[:, q * NQ : (q + 1) * NQ]
        c.rsl[step, r] = c.rsq[r]
        return line(Z_SUM + step, lambda peer: c.rsq.at[peer], c.rsl.at[step, r])

    def gate_bias(ref):
        return jnp.concatenate([ref[k : k + 1, :] for k in range(3)], axis=1)

    def gates(step, before, before_t):
        summed = c.rsl[step, 0]
        for q in range(1, R):
            summed = summed + c.rsl[step, q]
        summed_low = summed.T.astype(BF16)
        gi = nn(summed_low, c.win[...]) + gate_bias(c.bin)
        gs = nn(before.astype(BF16), c.wst[...]) + gate_bias(c.bst)
        reset = jax.nn.sigmoid(gi[:, :H] + gs[:, :H])
        update = jax.nn.sigmoid(gi[:, H : 2 * H] + gs[:, H : 2 * H])
        state_part = gs[:, 2 * H :]
        candidate = jnp.tanh(gi[:, 2 * H :] + reset * state_part)
        for k, x in enumerate((before, reset, update, candidate, state_part)):
            c.keep[step, k] = x
        c.keept[step, 0] = summed.astype(BF16)
        c.keept[step, 1] = before_t
        return (1.0 - update) * candidate + update * before

    nodes_here = pl.ds(pl.multiple_of(r * NQ, NQ), NQ)
    sums = messages(0)
    arrive(sums, reuse=True)
    state = gates(0, c.nodes[nodes_here, :], c.nst[:, nodes_here].astype(BF16))
    state_t = state.T.astype(BF16)
    c.nsq[...] = state_t
    hib = r // (LO // NQ)
    lanes = pl.ds(pl.multiple_of(lax.rem(r, LO // NQ) * NQ, NQ), NQ)
    c.stq[1, hib, :, lanes] = c.nsq[part, :]
    pieces = line(
        Z_STATE,
        lambda peer: c.nsq.at[pl.ds(pl.multiple_of(peer * J, J), J), :],
        c.stq.at[1, hib, :, lanes],
    )
    arrive(pieces)
    c.tab[1, b] = c.stq[1]
    arrive(plane(P_STATE2, lambda peer: c.stq.at[1], c.tab.at[1, b]))
    gather(1)
    sums = messages(1)
    arrive(sums)
    final = gates(1, state, state_t)
    c.fin[...] = final
    c.final[nodes_here, :] = final

    c.small[...] = jnp.zeros_like(c.small)
    c.gacc[...] = jnp.zeros_like(c.gacc)

    def deltas(step, grad):
        before, reset, update, candidate, state_part = [c.keep[step, k] for k in range(5)]
        dn = grad * (1.0 - update)
        dz = grad * (before - candidate)
        dpn = dn * (1.0 - candidate * candidate)
        dpz = dz * update * (1.0 - update)
        dpr = dpn * state_part * reset * (1.0 - reset)
        to_input = jnp.concatenate([dpr, dpz, dpn], axis=1)
        to_state = jnp.concatenate([dpr, dpz, dpn * reset], axis=1)
        summed_grad = nt2(to_input, c.win[...]).astype(BF16)
        c.gq[step] = summed_grad
        c.gfull[step, nodes_here, :] = summed_grad
        copies = line(Z_DELTA + step, lambda peer: c.gq.at[step], c.gfull.at[step, nodes_here, :])
        gwi = nn2(c.keept[step, 0], to_input)
        gws = nn2(c.keept[step, 1], to_state)
        gbi = jnp.sum(to_input, axis=0, keepdims=True)
        gbs = jnp.sum(to_state, axis=0, keepdims=True)
        for k in range(3):
            cut = slice(k * H, (k + 1) * H)
            c.small[k * H : (k + 1) * H, :] += gwi[:, cut]
            c.small[ROW_STATE_WEIGHT + k * H : ROW_STATE_WEIGHT + (k + 1) * H, :] += gws[:, cut]
            c.small[ROW_INPUT_BIAS + k : ROW_INPUT_BIAS + k + 1, :] += gbi[:, cut]
            c.small[ROW_STATE_BIAS + k : ROW_STATE_BIAS + k + 1, :] += gbs[:, cut]
        c.gradq[...] = grad * update + nt2(to_state, c.wst[...])
        return copies

    def node_grads(step):
        gt = nt(eye_h, c.gfull[step]).astype(BF16)

        def one(t, carry):
            c.ge[:, edges(t)] = nn(gt, target_rows(t)).astype(BF16)
            return carry

        lax.fori_loop(0, tiles, one, 0, unroll=2)
        rows = pl.ds(ROW_SECOND_BIAS + pl.multiple_of(r * J, J), J)
        high, low = two(c.ssum[step])
        c.small[rows, :] += nn(high, c.gfull[step]) + nn(low, c.gfull[step])

    def weights_tile(step, t):
        e = edges(t)
        at_edges = c.ge[:, e]
        source = c.st[step, :, e].astype(F32)
        got = None if step == STEPS - 1 else c.hg[:, e]
        half = J // 2
        for part_of in range(2):
            for q in range(half):
                j = part_of * half + q
                spread_row = jnp.broadcast_to(source[j : j + 1, :], (16, TILE)).astype(BF16)
                c.o[q * H : (q + 1) * H, :] = (
                    at_edges.reshape(H // 16, 16, TILE) * spread_row[None]
                ).reshape(H, TILE)
            base = part_of * half * H
            more = nn(c.w2k[:, base : base + half * H], c.o[...])
            got = more if got is None else got + more
            for k in range(half * H // ROWS):
                rows = slice(base + k * ROWS, base + (k + 1) * ROWS)
                c.gacc[rows, :] += nt(c.o[k * ROWS : (k + 1) * ROWS, :], c.ht[:, e])
        c.hg[:, e] = got

    def weights(step, begin, end):
        def one(t, carry):
            weights_tile(step, t)
            return carry

        lax.fori_loop(begin, end, one, 0)

    def sources(step):
        c.scat[...] = jnp.zeros_like(c.scat)

        def one(t, carry):
            e = edges(t)
            if s.KEEP:
                got = held_sources(e)
            else:
                at_edges = c.ge[:, e].astype(F32)
                hidden = hidden_rows(e)
                parts = []
                for k in range(J // chunk):
                    m = matrices(k, e, hidden)
                    for q in range(chunk):
                        parts.append(
                            jnp.sum(m[q * H : (q + 1) * H] * at_edges, axis=0, keepdims=True)
                        )
                got = jnp.concatenate(parts, axis=0)
            high = c.src[:, e] // LO
            per = ROWS // J
            for g in range(s.HI // per):
                for k in range(per):
                    c.xs[k * J : (k + 1) * J, :] = jnp.where(high == g * per + k, got, 0.0).astype(
                        BF16
                    )
                c.scat[g * ROWS : (g + 1) * ROWS, :] += nn(c.xs[...], c.ohln[e, :])
            return carry

        lax.fori_loop(0, tiles, one, 0)
        c.rps[...] = c.scat[...].astype(BF16).reshape(B, s.HIB * J, LO)
        c.rpl[step, b] = c.rps[b]
        return plane(P_SPREAD + step, lambda peer: c.rps.at[peer], c.rpl.at[step, b])

    def share_sources(step):
        total = c.rpl[step, 0].astype(F32)
        for q in range(1, B):
            total = total + c.rpl[step, q].astype(F32)
        for q in range(R):
            k, lane = (q * NQ) // LO, (q * NQ) % LO
            c.fzs[step, q] = total[k * J : (k + 1) * J, lane : lane + NQ]
        c.fzl[step, r] = c.fzs[step, r]
        return line(Z_SOURCE + step, lambda peer: c.fzs.at[step, peer], c.fzl.at[step, r])

    def state_grad(step):
        return c.gradq[...] + c.fzl[step].reshape(H, NQ).T

    last = STEPS - 1
    copies = deltas(last, c.cot[nodes_here, :])
    arrive(copies)
    final_in = line(Z_FINAL, lambda peer: c.fin, c.final.at[nodes_here, :])
    node_grads(last)
    spread = sources(last)
    weights(last, 0, 3)
    arrive(spread, reuse=True)
    pieces = share_sources(last)
    weights(last, 3, 4)
    arrive(pieces)
    copies = deltas(0, state_grad(last))
    weights(last, 4, tiles)
    arrive(copies)
    node_grads(0)
    weights(0, 0, tiles)

    per_owner = jh // OW

    def grad_rows(q):
        return c.gacc[pl.ds(pl.multiple_of(q * per_owner, per_owner), per_owner), :]

    if STRIDE == 1:
        pair = []
        for m in range(s.C):
            rows = slice(m * per_owner, (m + 1) * per_owner)
            c.baug[rows, :] = grad_rows(device(m, 1 - core)).astype(BF16)
            x = P_GRAD_PAIR
            cp = push(
                c.baug.at[rows, :],
                c.gpair.at[m],
                c.ps.at[x, m],
                c.pr.at[x, m],
                "blk",
                device(chip, 1 - core),
            )
            cp.start()
            pair.append(cp)
        sent.extend(pair)
    else:
        c.gsend[...] = c.gacc[...].astype(BF16)

        def own_grads():
            c.gland[b] = grad_rows(owner).astype(BF16)

        when_owner(own_grads)
        grads_wait = to_owners(
            P_GRAD,
            lambda q: c.gsend.at[pl.ds(pl.multiple_of(q * per_owner, per_owner), per_owner), :],
            c.gland.at[b],
        )

    w1 = c.w1[...]

    def first_layer(t, carry):
        e = edges(t)
        mt = c.mt[:, e]
        pre = nn(w1ta, mt)
        gate = jax.nn.sigmoid(pre)
        pre_grad = c.hg[:, e] * gate * (1.0 + pre * (1.0 - gate))
        high, low = two(pre_grad)
        c.fqs[:, e] = ((nn(w1, high) + nn(w1, low)) * c.gm[:, e].astype(F32)).astype(BF16)
        c.small[ROW_FIRST : ROW_FIRST + 32, :] += nt(mt, high) + nt(mt, low)
        return carry

    lax.fori_loop(0, tiles, first_layer, 0)

    if STRIDE == 1:
        across = []
        for m in list(range(1, s.C)) + [0]:
            other = lax.rem(chip + m, s.C)
            pair_piece = c.gpair.at[other]
            if m == 1:
                arrive(pair)
            total = grad_rows(device(other, core)) + pair_piece[...].astype(F32)
            if m == 0:
                c.gland[chip] = total.astype(BF16)
                continue
            c.gsum[m] = total.astype(BF16)
            x = P_GRAD
            cp = push(
                c.gsum.at[m],
                c.gland.at[chip],
                c.ps.at[x, m],
                c.pr.at[x, m],
                "blk",
                device(other, core),
            )
            cp.start()
            across.append(cp)
        sent.extend(across)

        def grads_wait():
            arrive(across)

    edges_here = pl.ds(pl.multiple_of(r * EQ, EQ), EQ)
    c.fql[r] = c.fqs[:, edges_here]
    feats_in = line(
        Z_FEATS,
        lambda peer: c.fqs.at[:, pl.ds(pl.multiple_of(peer * EQ, EQ), EQ)],
        c.fql.at[r],
    )

    c.sgsend[...] = c.small[...].astype(BF16)

    def small_rows(q):
        return pl.ds(pl.multiple_of(q * s.SMALL, s.SMALL), s.SMALL)

    def own_small():
        c.sgland[b] = c.sgsend[small_rows(owner), :]

    when_owner(own_small)
    small_wait = to_owners(P_SMALL, lambda q: c.sgsend.at[small_rows(q), :], c.sgland.at[b])

    spread = sources(0)

    def total_of(ref, rows, count):
        total = ref[0, rows, :].astype(F32)
        for q in range(1, count):
            total = total + ref[q, rows, :].astype(F32)
        return total

    grads_wait()

    def reduce_grads():
        for t in range(T):
            total = total_of(c.gland, slice(t * H, (t + 1) * H), s.C if STRIDE == 1 else B)
            total = total.astype(BF16)
            for q in range(R):
                c.gz[q, t * J : (t + 1) * J, :] = total[q * J : (q + 1) * J, :]
        c.f[r, owner] = c.gz[r]

    when_owner(reduce_grads)
    second_in = line_owner(Z_SECOND, lambda peer: c.gz.at[peer], c.f.at[r, owner])
    small_wait()

    def reduce_small():
        c.sgz[r] = total_of(c.sgland, slice(None), B).astype(BF16)

    when_owner(reduce_small)
    small_in = line_owner(Z_SMALL, lambda peer: c.sgz.at[r], c.sgz.at[r])

    arrive(feats_in)
    c.ff[:, edges_here] = total_of(c.fql, slice(None), R).astype(BF16)
    feats_all = line(Z_FEATS_ALL, lambda peer: c.ff.at[:, edges_here], c.ff.at[:, edges_here])

    arrive(spread)
    pieces = share_sources(0)

    def sum_small():
        arrive(small_in)
        c.f[R, owner] = total_of(c.sgz, slice(None), R).astype(BF16)
        arrive(second_in)

    when_owner(sum_small)
    second_relay, second_wait = from_owners(
        P_GRAD_ALL, P_GRAD_ALL_PAIR, lambda q: c.f.at[:, q]
    )

    arrive(pieces)
    grad = state_grad(0).astype(BF16)
    c.gradl[...] = grad
    c.grads[nodes_here, :] = grad
    grads_in = line(Z_GRADS, lambda peer: c.gradl, c.grads.at[nodes_here, :])

    arrive(feats_all)
    arrive(final_in)
    second_relay()
    arrive(grads_in)
    second_wait()
    for cp in sent:
        cp.wait_send()
    when_owner(lambda: [cp.wait_send() for cp in owner_sent] and None)


FINISH_NAMES = (
    ["f", "ff", "final", "grads"]
    + ["o_final", "o_grads", "feats", "w2", "win", "wst", "bin", "bst", "w1", "b1", "b2"]
    + ["hf", "hff", "hgrads", "wide", "turn", "sems"]
)


def finish(s, *refs):
    c = SimpleNamespace(**dict(zip(FINISH_NAMES, refs)))
    H, J = s.H, s.J
    pairs = [(c.f, c.hf), (c.ff, c.hff), (c.grads, c.hgrads), (c.final, c.o_final)]
    copies = [pltpu.make_async_copy(x, y, c.sems.at[k]) for k, (x, y) in enumerate(pairs)]
    for cp in copies:
        cp.start()
    copies[0].wait()
    c.wide[...] = c.hf[0 : s.R].reshape(H * J, H).astype(F32)
    for i in range(J):
        c.w2[:, i * H : (i + 1) * H] = c.wide[pl.ds(i, H, stride=J), :].T
    small = c.hf[s.R].reshape(SMALL_ROWS, H).astype(F32)
    for k in range(3):
        cut = slice(k * H, (k + 1) * H)
        c.win[:, cut] = small[k * H : (k + 1) * H]
        c.wst[:, cut] = small[ROW_STATE_WEIGHT + k * H : ROW_STATE_WEIGHT + (k + 1) * H]
    c.bin[...] = small[ROW_INPUT_BIAS : ROW_INPUT_BIAS + 3]
    c.bst[...] = small[ROW_STATE_BIAS : ROW_STATE_BIAS + 3]
    c.w1[...] = small[ROW_FIRST : ROW_FIRST + 16]
    c.b1[...] = small[ROW_FIRST + 16 : ROW_FIRST + 17]
    c.turn[...] = small[ROW_SECOND_BIAS : ROW_SECOND_BIAS + H].T
    r = lax.axis_index("rep")
    c.b2[...] = c.turn[pl.ds(pl.multiple_of(r * J, J), J), :]
    copies[1].wait()
    c.feats[...] = c.hff[...].astype(F32)
    copies[2].wait()
    c.o_grads[...] = c.hgrads[...].astype(F32)
    copies[3].wait()


def body(
    s,
    node_states,
    edge_feats,
    edge_source,
    edge_target,
    edge_group,
    column_mask,
    edge_count,
    first_weight,
    first_bias,
    second_weight,
    second_bias,
    update_input_weight,
    update_state_weight,
    update_input_bias,
    update_state_bias,
    state_cotangent,
):
    H, N, E = s.H, s.N, s.E
    shapes = scratch(s)
    names = IN_NAMES + OUT_NAMES + list(shapes)
    sds = jax.ShapeDtypeStruct
    final, grads, ff, f = pl.pallas_call(
        functools.partial(whole, s, names),
        out_shape=[
            sds((N, H), F32),
            sds((N, H), BF16),
            sds((16, E), BF16),
            sds((s.R + 1, s.OW, s.T * s.J, H), BF16),
        ],
        in_specs=[VMEM] * 9 + [pl.BlockSpec(memory_space=pl.ANY)] + [VMEM] * 6,
        out_specs=[VMEM] * 4,
        scratch_shapes=list(shapes.values()),
        compiler_params=pltpu.CompilerParams(
            collective_id=0, has_side_effects=True, vmem_limit_bytes=63 * 2**20
        ),
        name="edge_network",
    )(
        node_states,
        edge_feats.T,
        edge_source.reshape(1, E),
        edge_target.reshape(1, E),
        edge_group.reshape(1, E),
        column_mask,
        edge_count.reshape(1, 1),
        first_weight,
        first_bias.reshape(1, H),
        second_weight,
        second_bias.reshape(s.J, H),
        update_input_weight,
        update_state_weight,
        update_input_bias.reshape(3, H),
        update_state_bias.reshape(3, H),
        state_cotangent,
    )
    hbm = pl.BlockSpec(memory_space=pl.ANY)
    final, grads, feats, w2, win, wst, bin_, bst, w1, b1, b2 = pl.pallas_call(
        functools.partial(finish, s),
        out_shape=[
            sds((N, H), F32),
            sds((N, H), F32),
            sds((16, E), F32),
            sds((H, s.J * H), F32),
            sds((H, 3 * H), F32),
            sds((H, 3 * H), F32),
            sds((3, H), F32),
            sds((3, H), F32),
            sds((16, H), F32),
            sds((1, H), F32),
            sds((s.J, H), F32),
        ],
        in_specs=[hbm] * 4,
        out_specs=[hbm] + [VMEM] * 10,
        scratch_shapes=[
            pltpu.VMEM((s.R + 1, s.OW, s.T * s.J, H), BF16),
            pltpu.VMEM((16, E), BF16),
            pltpu.VMEM((N, H), BF16),
            pltpu.VMEM((H * s.J, H), F32),
            pltpu.VMEM((H, H), F32),
            pltpu.SemaphoreType.DMA((4,)),
        ],
        compiler_params=pltpu.CompilerParams(vmem_limit_bytes=60 * 2**20),
        name="finish",
    )(f, ff, final, grads)
    return (
        final,
        grads,
        feats.T,
        w1,
        b1.reshape(-1),
        w2,
        b2.reshape(-1),
        win,
        wst,
        bin_.reshape(-1),
        bst.reshape(-1),
    )


def solution(mesh):
    in_specs = (
        P("blk", None),
        P("blk", None),
        P("blk"),
        P("blk"),
        P("blk"),
        P(),
        P("blk"),
        P(),
        P(),
        P(None, "rep"),
        P("rep"),
        P(),
        P(),
        P(),
        P(),
        P("blk", None),
    )
    out_specs = (
        P("blk", None),
        P("blk", None),
        P("blk", None),
        P(),
        P(),
        P(None, "rep"),
        P("rep"),
        P(),
        P(),
        P(),
        P(),
    )

    def run(*args):
        nodes, edges, width = args[0].shape[0], args[2].shape[0], args[0].shape[1]
        return body(sizes(mesh, edges, nodes, width), *args)

    return jax.shard_map(run, mesh=mesh, in_specs=in_specs, out_specs=out_specs, check_vma=False)
```

```python
import functools
from types import SimpleNamespace

import jax
import jax.numpy as jnp
from jax import lax
from jax.experimental import pallas as pl
from jax.experimental.pallas import tpu as pltpu
from jax.sharding import PartitionSpec as P

STEPS = 2
TILE = 512
LO = 256
ROWS = 512
SLAB = 32
VISITS = (22, 34)
F32, BF16, I32 = jnp.float32, jnp.bfloat16, jnp.int32
MESH = pl.DeviceIdType.MESH
VMEM = pl.BlockSpec(memory_space=pltpu.VMEM)

ROW_STATE_WEIGHT = 384
ROW_INPUT_BIAS = 768
ROW_STATE_BIAS = 776
GROUP = 16
FIRST_ROWS = 32
ROW_SECOND_BIAS = 896
SMALL_ROWS = 1024

(
    P_STATE,
    P_STATE2,
    P_WEIGHT,
    P_WEIGHT_PAIR,
    P_SPREAD,
    P_SPREAD2,
    P_GRAD_PAIR,
    P_GRAD,
    P_SMALL,
    P_FIRST,
    P_GRAD_ALL,
    P_GRAD_ALL_PAIR,
    PLANES,
) = range(13)
(
    Z_WEIGHT,
    Z_BIAS,
    Z_SUM,
    Z_SUM2,
    Z_STATE,
    Z_FINAL,
    Z_DELTA,
    Z_DELTA2,
    Z_SOURCE,
    Z_SOURCE2,
    Z_GRADS,
    Z_FEATS,
    Z_FEATS_ALL,
    Z_SECOND,
    Z_SMALL,
    Z_FIRST,
    LINES,
) = range(17)


def nn(a, b):
    return jnp.dot(a, b, preferred_element_type=F32)


def nt(a, b):
    return lax.dot_general(a, b, (((1,), (1,)), ((), ())), preferred_element_type=F32)


def iota(shape, dim):
    return lax.broadcasted_iota(I32, shape, dim)


def ones_where(condition):
    return jnp.where(condition, 1.0, 0.0).astype(BF16)


def eye(n):
    return ones_where(iota((n, n), 0) == iota((n, n), 1))


def two(x):
    high = x.astype(BF16)
    return high, (x - high.astype(F32)).astype(BF16)


def three(x):
    high, rest = x.astype(BF16), x
    rest = x - high.astype(F32)
    mid = rest.astype(BF16)
    return high, mid, (rest - mid.astype(F32)).astype(BF16)


def nn2(a, x):
    high, low = two(x)
    return nn(a, high) + nn(a, low)


def nt2(x, b):
    high, low = two(x)
    return nt(high, b) + nt(low, b)


def sizes(mesh, edges, nodes, width):
    s = SimpleNamespace()
    s.B, s.R = mesh.shape["blk"], mesh.shape["rep"]
    s.E, s.N, s.H = edges, nodes, width
    s.J = width // s.R
    s.HIB = nodes // LO
    s.HI = s.HIB * s.B
    s.NQ = nodes // s.R
    s.EQ = edges // s.R
    s.OW = min(s.B, 8)
    s.STRIDE = s.B // s.OW
    s.T = s.J // s.OW
    s.KEEP = s.B <= 8
    s.SMALL = SMALL_ROWS // s.OW
    s.C = s.B // 2
    s.G = nodes // GROUP
    s.V = s.G + edges // LO
    return s


def scratch(s):
    v = pltpu.VMEM
    jh = s.J * s.H
    shapes = dict(
        nst=v((s.H, s.N), F32),
        stq=v((STEPS, s.HIB, s.J, LO), BF16),
        tab=v((STEPS, s.B, s.HIB, s.J, LO), BF16),
        ys=v((s.R * s.T, s.J, s.H), F32),
        wsend=v((s.R, s.T, s.J, s.H), BF16),
        w2r=v((s.J, s.H, s.H), BF16),
        b2f=v((s.H, s.H), F32),
        baug=v((s.J, s.H, s.H), BF16),
        w2k=v((s.H, jh), BF16),
        tl=v((1, s.E), I32),
        ohln=v((s.E, LO), BF16),
        mt=v((32, s.E), BF16),
        gm=v((16, s.E), BF16),
        ht=v((s.E // LO, s.H, LO), BF16),
        tlc=v((s.E // LO, 1, LO), I32),
        st=v((STEPS, s.J, s.E), BF16),
        sc=v((s.E // LO, s.J, LO), F32),
        ge=v((s.H, s.E), BF16),
        smt=v((2 * s.H + s.J, s.N), F32),
        ssum=v((STEPS, s.J, s.N), F32),
        rsq=v((s.R, s.H, s.NQ), F32),
        rsl=v((STEPS, s.R, s.H, s.NQ), F32),
        keep=v((STEPS, 5, s.NQ, s.H), F32),
        keept=v((STEPS, 2, s.H, s.NQ), BF16),
        nsq=v((s.H, s.NQ), BF16),
        fin=v((s.NQ, s.H), F32),
        gq=v((STEPS, s.NQ // GROUP, GROUP, s.H), BF16),
        gfull=v((STEPS, s.G, GROUP, s.H), BF16),
        hg=v((s.H, s.E), F32),
        gacc=v((jh, s.H), F32),
        xs=v((ROWS, TILE), BF16),
        scat=v((s.HI * s.J, LO), F32),
        rps=v((s.B, s.HIB * s.J, LO), BF16),
        rpl=v((STEPS, s.B, s.HIB * s.J, LO), BF16),
        fzs=v((STEPS, s.R, s.J, s.NQ), F32),
        fzl=v((STEPS, s.R, s.J, s.NQ), F32),
        gradq=v((s.NQ, s.H), F32),
        gradl=v((s.NQ, s.H), BF16),
        small=v((SMALL_ROWS, s.H), F32),
        q0=v((s.V, s.J * GROUP, s.H), BF16),
        gv=v((s.V * GROUP, s.H), BF16),
        planv=v((8, 128), I32),
        plan=pltpu.SMEM((8, 128), I32),
        firsts=v((FIRST_ROWS, s.H), F32),
        flz=v((s.R, FIRST_ROWS, s.H), F32),
        flp=v((s.B, FIRST_ROWS, s.H), F32),
        sgsend=v((SMALL_ROWS, s.H), BF16),
        sgland=v((s.B, s.SMALL, s.H), BF16),
        gz=v((s.R, s.T * s.J, s.H), BF16),
        sgz=v((s.R, s.SMALL, s.H), BF16),
        fqs=v((16, s.E), BF16),
        fql=v((s.R, 16, s.EQ), BF16),
        ps=pltpu.SemaphoreType.DMA((PLANES, s.B)),
        pr=pltpu.SemaphoreType.DMA((PLANES, s.B)),
        zs=pltpu.SemaphoreType.DMA((LINES, s.R)),
        zr=pltpu.SemaphoreType.DMA((LINES, s.R)),
        local=pltpu.SemaphoreType.DMA,
        ins=pltpu.SemaphoreType.DMA((len(IN_NAMES),)),
    )
    piece = (jh // s.OW, s.H)
    if s.STRIDE > 1:
        shapes["gland"] = v((s.B,) + piece, BF16)
        shapes["gsend"] = v((jh, s.H), BF16)
    if s.KEEP:
        shapes["mat"] = v((jh, s.E), BF16)
    return shapes


IN_NAMES = (
    ["nodes", "feats", "src", "tgt", "grp", "cmask", "count", "w1", "b1"]
    + ["w2", "b2", "win", "wst", "bin", "bst", "cot"]
)
OUT_NAMES = ["final", "grads", "ff", "f", "fl"]


def whole(s, names, *refs):
    c = SimpleNamespace(**dict(zip(names, refs)))
    B, R, H, J, E, N, NQ, EQ = s.B, s.R, s.H, s.J, s.E, s.N, s.NQ, s.EQ
    T, OW, STRIDE = s.T, s.OW, s.STRIDE
    jh = J * H
    tiles = E // TILE
    b = lax.axis_index("blk")
    r = lax.axis_index("rep")
    owner = b // STRIDE
    is_owner = lax.rem(b, STRIDE) == 0
    sent = []

    def push(src, dst, sems, rems, axis, peer):
        return pltpu.make_async_remote_copy(
            src_ref=src,
            dst_ref=dst,
            send_sem=sems,
            recv_sem=rems,
            device_id={axis: peer},
            device_id_type=MESH,
        )

    def plane(x, src_of, dst):
        copies = []
        for d in range(1, B):
            peer = lax.rem(b + d, B)
            cp = push(src_of(peer), dst, c.ps.at[x, d], c.pr.at[x, d], "blk", peer)
            cp.start()
            copies.append(cp)
        sent.extend(copies)
        return copies

    def line(x, src_of, dst):
        copies = []
        for d in range(1, R):
            peer = lax.rem(r + d, R)
            cp = push(src_of(peer), dst, c.zs.at[x, d], c.zr.at[x, d], "rep", peer)
            cp.start()
            copies.append(cp)
        sent.extend(copies)
        return copies

    def arrive(copies, reuse=False):
        for cp in copies:
            cp.wait_recv()
        if reuse:
            release(copies)

    def release(copies):
        for cp in copies:
            cp.wait_send()
            sent[:] = [other for other in sent if other is not cp]

    def when_owner(fn):
        if STRIDE == 1:
            fn()
        else:
            pl.when(is_owner)(fn)

    def line_owner(x, src_of, dst):
        copies = []
        for d in range(1, R):
            peer = lax.rem(r + d, R)
            copies.append(push(src_of(peer), dst, c.zs.at[x, d], c.zr.at[x, d], "rep", peer))
        when_owner(lambda: [cp.start() for cp in copies] and None)
        owner_sent.extend(copies)
        return copies

    owner_sent = []

    def from_owners(x, x2, strip_of):
        if STRIDE == 1:
            return gather_pairs(x, x2, strip_of)
        copies = []
        for d in range(1, B):
            peer = lax.rem(b + d, B)
            strip = strip_of(owner)
            copies.append(push(strip, strip, c.ps.at[x, d], c.pr.at[x, owner], "blk", peer))
        when_owner(lambda: [cp.start() for cp in copies] and None)
        owner_sent.extend(copies)

        def wait():
            for q in range(OW):

                @pl.when(b != q * STRIDE)
                def _():
                    strip = strip_of(q)
                    peer = lax.rem(b + 1, B)
                    push(strip, strip, c.ps.at[x, 0], c.pr.at[x, q], "blk", peer).wait_recv()

        return lambda: None, wait, [], []

    chip, core = b // 2, lax.rem(b, 2)

    def device(other, its_core):
        return 2 * lax.rem(other, s.C) + its_core

    def gather_pairs(x, x2, strip_of):
        first, then = [], []
        for m in range(1, s.C):
            mine = strip_of(b)
            first.append(
                push(mine, mine, c.ps.at[x, m], c.pr.at[x, m], "blk", device(chip + m, core))
            )
        for m in range(s.C):
            held = strip_of(device(chip + s.C - m, core))
            then.append(
                push(held, held, c.ps.at[x2, m], c.pr.at[x2, m], "blk", device(chip, 1 - core))
            )
        for cp in first + then[:1]:
            cp.start()

        def relay():
            for m in range(1, s.C):
                first[m - 1].wait_recv()
                then[m].start()

        def wait():
            arrive(then)

        sent.extend(first + then)
        return relay, wait, first, then

    def to_owners(x, src_of, dst):
        if STRIDE == 1:
            copies = plane(x, src_of, dst)
            return lambda: arrive(copies)
        for q in range(OW):

            @pl.when(b != q * STRIDE)
            def _():
                push(src_of(q), dst, c.ps.at[x, q], c.pr.at[x, b], "blk", q * STRIDE).start()

        def wait():
            def arrivals():
                for d in range(1, B):
                    peer = lax.rem(b + d, B)
                    push(src_of(0), dst, c.ps.at[x, 0], c.pr.at[x, peer], "blk", peer).wait_recv()

            when_owner(arrivals)
            for q in range(OW):

                @pl.when(b != q * STRIDE)
                def _():
                    push(src_of(q), dst, c.ps.at[x, q], c.pr.at[x, b], "blk", q * STRIDE).wait_send()

        return wait

    def edges(t):
        return pl.ds(pl.multiple_of(t * TILE, TILE), TILE)

    barrier = pltpu.get_barrier_semaphore()
    for d in range(1, B):
        pl.semaphore_signal(
            barrier, inc=1, device_id={"blk": lax.rem(b + d, B)}, device_id_type=MESH
        )
    for d in range(1, R):
        pl.semaphore_signal(
            barrier, inc=1, device_id={"rep": lax.rem(r + d, R)}, device_id_type=MESH
        )

    loads = {}
    for k, name in enumerate(IN_NAMES):
        to = c.w2k if name == "w2" else getattr(c, name)
        loads[name] = pltpu.make_async_copy(getattr(c, "in_" + name), to, c.ins.at[k])
    for name in ["nodes", "w2"]:
        loads[name].start()
    for name in IN_NAMES:
        if name not in ("nodes", "w2"):
            loads[name].start()
    eye_h = eye(H)
    part = pl.ds(pl.multiple_of(r * J, J), J)

    loads["nodes"].wait()
    c.nst[...] = c.nodes[...].T
    own_columns = c.nst[part, :].astype(BF16)
    for k in range(s.HIB):
        c.stq[0, k] = own_columns[:, k * LO : (k + 1) * LO]
    c.tab[0, b] = c.stq[0]
    row = iota((R * T, H), 0)
    pick = ones_where(iota((R * T, H), 1) == (row // T) * J + T * owner + lax.rem(row, T))
    loads["w2"].wait()
    for i in range(J):
        c.ys[:, i, :] = nt(pick, c.w2k[:, i * H : (i + 1) * H])
    c.wsend[...] = c.ys[...].astype(BF16).reshape(R, T, J, H)
    for name in IN_NAMES:
        if name not in ("nodes", "w2"):
            loads[name].wait()
    pl.semaphore_wait(barrier, B - 1 + R - 1)

    states_in = plane(P_STATE, lambda peer: c.stq.at[0], c.tab.at[0, b])
    strip = pl.ds(pl.multiple_of(T * owner, T), T)
    weight_in = line_owner(Z_WEIGHT, lambda peer: c.wsend.at[peer], c.w2r.at[strip, part, :])
    c.b2f[part, :] = c.b2[...]
    bias_in = line(Z_BIAS, lambda peer: c.b2, c.b2f.at[part, :])

    def own_strip():
        c.w2r[strip, part, :] = c.wsend[r]

    when_owner(own_strip)

    place = iota((1, E), 1)
    c.tl[...] = jnp.where(place < c.count[...], c.tgt[...] - b * N, -1)
    for k in range(E // LO):
        c.tlc[k] = c.tl[:, k * LO : (k + 1) * LO]
    ends = jnp.where(c.tgt[...] - b * N < GROUP * (iota((s.G, E), 0) + 1), 1, 0)
    ends = jnp.sum(ends, axis=1, keepdims=True)
    left_in = jnp.maximum((ends + (LO - 1)) // LO - 1, 0)
    group = iota((s.G, 128), 0)
    leave = group + jnp.where(group == s.G - 1, E // LO - 1, left_in)
    visited = jnp.sum(jnp.where(leave < iota((s.G, 128), 1), 1, 0), axis=0, keepdims=True)
    c.planv[...] = jnp.broadcast_to(visited, (8, 128))
    plan_copy = pltpu.make_async_copy(c.planv, c.plan, c.local)
    plan_copy.start()
    cmt = nt(eye(16), c.cmask[...].astype(F32).astype(BF16)).astype(BF16)
    b1 = three(c.b1[...])
    first = jnp.concatenate(
        [c.w1[...].astype(F32)] + [x.astype(F32) for x in b1] + [jnp.zeros((13, H), F32)], axis=0
    ).astype(BF16)
    w1ta = nt(eye_h, first).astype(BF16)
    eye_t = eye(LO)

    def target_rows(t):
        return ones_where(iota((N, TILE), 0) == c.tl[:, edges(t)])

    def low_rows(t):
        return ones_where(iota((LO, TILE), 0) == (c.src[:, edges(t)] & (LO - 1)))

    per_tile = TILE // LO

    def put(ref, t, value):
        for k in range(per_tile):
            ref[t * per_tile + k] = value[:, k * LO : (k + 1) * LO]

    def take(ref, t):
        return jnp.concatenate([ref[t * per_tile + k] for k in range(per_tile)], axis=1)

    def source_row(j, t):
        rows = [c.sc[t * per_tile + k, j : j + 1, :] for k in range(per_tile)]
        return jnp.concatenate(rows, axis=1)

    def prepare(t, carry):
        e = edges(t)
        groups = ones_where(iota((16, TILE), 0) == c.grp[:, e])
        gm = nn(cmt, groups)
        c.gm[:, e] = gm.astype(BF16)
        masked = c.feats[:, e].astype(F32) * gm
        ones = jnp.where(iota((16, TILE), 0) < 3, 1.0, 0.0)
        mt = jnp.concatenate([masked, ones], axis=0).astype(BF16)
        c.mt[:, e] = mt
        pre = nn(w1ta, mt)
        put(c.ht, t, (pre * jax.nn.sigmoid(pre)).astype(BF16))
        lows = low_rows(t)
        for k in range(TILE // LO):
            rows = pl.ds(pl.multiple_of(t * TILE + k * LO, LO), LO)
            c.ohln[rows, :] = nt(eye_t, lows[:, k * LO : (k + 1) * LO]).astype(BF16)
        return carry

    lax.fori_loop(0, tiles, prepare, 0)

    when_owner(lambda: arrive(weight_in))
    weight_relay, weight_wait, weight_chip, weight_pair = from_owners(
        P_WEIGHT,
        P_WEIGHT_PAIR,
        lambda q: c.w2r.at[pl.ds(pl.multiple_of(T * q, T), T)],
    )

    def gather(step):
        def one(t, carry):
            e = edges(t)
            lows = low_rows(t)
            high = c.src[:, e] // LO
            total = jnp.zeros((J, TILE), F32)
            per = ROWS // J
            for g in range(s.HI // per):
                blocks = per // s.HIB
                table = c.tab[step, g * blocks : (g + 1) * blocks].reshape(ROWS, LO)
                rows = nn(table, lows)
                for k in range(per):
                    total = total + jnp.where(high == g * per + k, rows[k * J : (k + 1) * J], 0.0)
            c.st[step, :, e] = total.astype(BF16)
            put(c.sc, t, total)
            return carry

        lax.fori_loop(0, tiles, one, 0)

    arrive(states_in)
    gather(0)
    arrive(bias_in)
    b2 = jnp.concatenate(three(c.b2f[...]), axis=1)

    def bias_columns(j, carry):
        at = iota((3 * H, H), 0)
        to = iota((3 * H, H), 1)
        move = ones_where((lax.rem(at, H) == r * J + j) & (to == at // H))
        c.baug[j] = nn(b2, move).astype(BF16)
        return carry

    lax.fori_loop(0, J, bias_columns, 0, unroll=8)

    def turned(j, carry):
        c.w2k[:, pl.ds(pl.multiple_of(j * H, H), H)] = nt(eye_h, c.w2r[j]).astype(BF16)
        return carry

    chunk = ROWS // H

    def hidden_rows(t):
        ones = jnp.where(iota((H, TILE), 0) < 3, 1.0, 0.0).astype(BF16)
        return jnp.concatenate([take(c.ht, t), ones], axis=0)

    def held_messages(t):
        e = edges(t)
        parts = []
        for k in range(H // SLAB):
            total = jnp.zeros((SLAB, TILE), F32)
            for j in range(J):
                at = j * H + k * SLAB
                total = total + c.mat[at : at + SLAB, e].astype(F32) * source_row(j, t)
            parts.append(total)
        return jnp.concatenate(parts, axis=0)

    def held_sources(e):
        grads = c.ge[:, e]
        half, few = J // 2, H // 2
        rows = iota((half, half * few), 0)
        sums = ones_where(rows == iota((half, half * few), 1) // few)
        parts = []
        for k in range(2):
            held = c.mat[k * half * H : (k + 1) * half * H, e].reshape(half, H, TILE)
            product = held * grads[None]
            product = product[:, :few] + product[:, few:]
            parts.append(nn(sums, product.reshape(half * few, TILE)))
        return jnp.concatenate(parts, axis=0)

    def matrices(k, e, hidden):
        cut = slice(k * chunk, (k + 1) * chunk)
        left = jnp.concatenate(
            [c.w2r[cut].reshape(ROWS, H), c.baug[cut].reshape(ROWS, H)], axis=1
        )
        return nn(left, hidden).astype(BF16).astype(F32)

    def first_pass(strips, start):
        def one(t, carry):
            e = edges(t)
            hidden = hidden_rows(t)
            total = jnp.zeros((H, TILE), F32) if start else c.hg[:, e]
            for q in strips:
                cut = pl.ds(pl.multiple_of(q * T, T), T)
                left = jnp.concatenate(
                    [c.w2r[cut].reshape(T * H, H), c.baug[cut].reshape(T * H, H)], axis=1
                )
                low = nn(left, hidden).astype(BF16)
                c.mat[pl.ds(pl.multiple_of(q * T * H, T * H), T * H), e] = low
                m = low.astype(F32)
                for p in range(T):
                    total = total + m[p * H : (p + 1) * H] * source_row(q * T + p, t)
            c.hg[:, e] = total
            return carry

        lax.fori_loop(0, tiles, one, 0)

    def messages(step):
        c.smt[...] = jnp.zeros_like(c.smt)

        def one(t, carry):
            e = edges(t)
            low = c.st[step, :, e]
            if s.KEEP:
                total = held_messages(t) if step > 0 else c.hg[:, e]
            else:
                source = low.astype(F32)
                hidden = hidden_rows(t)
                total = jnp.zeros((H, TILE), F32)
                for k in range(J // chunk):
                    m = matrices(k, e, hidden)
                    for q in range(chunk):
                        j = k * chunk + q
                        total = total + m[q * H : (q + 1) * H] * source[j : j + 1, :]
            high, rest = two(total)
            rows = jnp.concatenate([high, rest, low], axis=0)
            c.smt[...] += nt(rows, target_rows(t))
            return carry

        lax.fori_loop(0, tiles, one, 0, unroll=2)
        summed = c.smt[0:H, :] + c.smt[H : 2 * H, :]
        c.ssum[step] = c.smt[2 * H : 2 * H + J, :]
        for q in range(R):
            c.rsq[q] = summed[:, q * NQ : (q + 1) * NQ]
        c.rsl[step, r] = c.rsq[r]
        return line(Z_SUM + step, lambda peer: c.rsq.at[peer], c.rsl.at[step, r])

    def gate_bias(ref):
        return jnp.concatenate([ref[k : k + 1, :] for k in range(3)], axis=1)

    def gates(step, before, before_t):
        summed = c.rsl[step, 0]
        for q in range(1, R):
            summed = summed + c.rsl[step, q]
        summed_low = summed.T.astype(BF16)
        gi = nn(summed_low, c.win[...]) + gate_bias(c.bin)
        gs = nn(before.astype(BF16), c.wst[...]) + gate_bias(c.bst)
        reset = jax.nn.sigmoid(gi[:, :H] + gs[:, :H])
        update = jax.nn.sigmoid(gi[:, H : 2 * H] + gs[:, H : 2 * H])
        state_part = gs[:, 2 * H :]
        candidate = jnp.tanh(gi[:, 2 * H :] + reset * state_part)
        for k, x in enumerate((before, reset, update, candidate, state_part)):
            c.keep[step, k] = x
        c.keept[step, 0] = summed.astype(BF16)
        c.keept[step, 1] = before_t
        return (1.0 - update) * candidate + update * before

    def products(begin, end):
        def one(t, carry):
            g = c.plan[0, t]
            ch = t - g
            mine = ones_where(iota((GROUP, LO), 0) + g * GROUP == c.tlc[ch])
            source = c.sc[ch]
            parts = []
            for j in range(J):
                row = jnp.broadcast_to(source[j : j + 1, :], (GROUP, LO)).astype(BF16)
                parts.append(row * mine)
            c.q0[t] = nt(jnp.concatenate(parts, axis=0), c.ht[ch]).astype(BF16)
            return carry

        lax.fori_loop(begin, end, one, 0)

    plan_copy.wait()
    nodes_here = pl.ds(pl.multiple_of(r * NQ, NQ), NQ)
    groups_here = pl.ds(pl.multiple_of(r * (NQ // GROUP), NQ // GROUP), NQ // GROUP)
    if s.KEEP:
        weight_relay()
        arrive(weight_pair)
        half = OW // 2
        first_pass(range(half), True)
        first_pass(range(half, OW), False)
    else:
        weight_wait()
    sums = messages(0)
    lax.fori_loop(0, J, turned, 0, unroll=8)
    products(0, VISITS[0])
    arrive(sums, reuse=True)
    release(weight_chip + weight_pair)
    state = gates(0, c.nodes[nodes_here, :], c.nst[:, nodes_here].astype(BF16))
    state_t = state.T.astype(BF16)
    c.nsq[...] = state_t
    hib = r // (LO // NQ)
    lanes = pl.ds(pl.multiple_of(lax.rem(r, LO // NQ) * NQ, NQ), NQ)
    c.stq[1, hib, :, lanes] = c.nsq[part, :]
    pieces = line(
        Z_STATE,
        lambda peer: c.nsq.at[pl.ds(pl.multiple_of(peer * J, J), J), :],
        c.stq.at[1, hib, :, lanes],
    )
    products(VISITS[0], VISITS[1])
    arrive(pieces)
    c.tab[1, b] = c.stq[1]
    states_in = plane(P_STATE2, lambda peer: c.stq.at[1], c.tab.at[1, b])
    products(VISITS[1], s.V)
    arrive(states_in)
    gather(1)
    sums = messages(1)
    arrive(sums)
    final = gates(1, state, state_t)
    c.fin[...] = final
    c.final[nodes_here, :] = final

    c.small[...] = jnp.zeros_like(c.small)
    c.gacc[...] = jnp.zeros_like(c.gacc)

    def deltas(step, grad):
        before, reset, update, candidate, state_part = [c.keep[step, k] for k in range(5)]
        dn = grad * (1.0 - update)
        dz = grad * (before - candidate)
        dpn = dn * (1.0 - candidate * candidate)
        dpz = dz * update * (1.0 - update)
        dpr = dpn * state_part * reset * (1.0 - reset)
        to_input = jnp.concatenate([dpr, dpz, dpn], axis=1)
        to_state = jnp.concatenate([dpr, dpz, dpn * reset], axis=1)
        summed_grad = nt2(to_input, c.win[...]).astype(BF16)
        c.gq[step] = summed_grad.reshape(NQ // GROUP, GROUP, H)
        c.gfull[step, groups_here] = c.gq[step]
        copies = line(Z_DELTA + step, lambda peer: c.gq.at[step], c.gfull.at[step, groups_here])
        gwi = nn2(c.keept[step, 0], to_input)
        gws = nn2(c.keept[step, 1], to_state)
        gbi = jnp.sum(to_input, axis=0, keepdims=True)
        gbs = jnp.sum(to_state, axis=0, keepdims=True)
        for k in range(3):
            cut = slice(k * H, (k + 1) * H)
            c.small[k * H : (k + 1) * H, :] += gwi[:, cut]
            c.small[ROW_STATE_WEIGHT + k * H : ROW_STATE_WEIGHT + (k + 1) * H, :] += gws[:, cut]
            c.small[ROW_INPUT_BIAS + k : ROW_INPUT_BIAS + k + 1, :] += gbi[:, cut]
            c.small[ROW_STATE_BIAS + k : ROW_STATE_BIAS + k + 1, :] += gbs[:, cut]
        c.gradq[...] = grad * update + nt2(to_state, c.wst[...])
        return copies

    def node_grads(step):
        held = c.gfull[step].reshape(N, H)
        gt = nt(eye_h, held).astype(BF16)

        def one(t, carry):
            c.ge[:, edges(t)] = nn(gt, target_rows(t)).astype(BF16)
            return carry

        lax.fori_loop(0, tiles, one, 0, unroll=2)
        rows = pl.ds(ROW_SECOND_BIAS + pl.multiple_of(r * J, J), J)
        high, low = two(c.ssum[step])
        c.small[rows, :] += nn(high, held) + nn(low, held)

    def weights_tile(step, t, second):
        e = edges(t)
        at_edges = c.ge[:, e]
        source = c.st[step, :, e].astype(F32)
        got = None if step == STEPS - 1 else c.hg[:, e]
        spread = at_edges.reshape(H // 16, 16, TILE)
        for k in range(jh // ROWS):
            parts = []
            for j in range(k * ROWS // H, (k + 1) * ROWS // H):
                row = jnp.broadcast_to(source[j : j + 1, :], (16, TILE)).astype(BF16)
                parts.append((spread * row[None]).reshape(H, TILE))
            outer = jnp.concatenate(parts, axis=0)
            rows = slice(k * ROWS, (k + 1) * ROWS)
            more = nn(c.w2k[:, rows], outer)
            got = more if got is None else got + more
            if second:
                c.gacc[rows, :] += nt(outer, take(c.ht, t))
        c.hg[:, e] = got

    def weights(step, begin, end):
        def one(t, carry):
            weights_tile(step, t, step == STEPS - 1)
            return carry

        lax.fori_loop(begin, end, one, 0)

    def sources(step, begin, end):
        if begin == 0:
            c.scat[...] = jnp.zeros_like(c.scat)

        def one(t, carry):
            e = edges(t)
            if s.KEEP:
                got = held_sources(e)
            else:
                at_edges = c.ge[:, e].astype(F32)
                hidden = hidden_rows(t)
                parts = []
                for k in range(J // chunk):
                    m = matrices(k, e, hidden)
                    for q in range(chunk):
                        parts.append(
                            jnp.sum(m[q * H : (q + 1) * H] * at_edges, axis=0, keepdims=True)
                        )
                got = jnp.concatenate(parts, axis=0)
            high = c.src[:, e] // LO
            per = ROWS // J
            for g in range(s.HI // per):
                for k in range(per):
                    c.xs[k * J : (k + 1) * J, :] = jnp.where(high == g * per + k, got, 0.0).astype(
                        BF16
                    )
                c.scat[g * ROWS : (g + 1) * ROWS, :] += nn(c.xs[...], c.ohln[e, :])
            return carry

        lax.fori_loop(begin, end, one, 0)

    def spread_sources(step):
        c.rps[...] = c.scat[...].astype(BF16).reshape(B, s.HIB * J, LO)
        c.rpl[step, b] = c.rps[b]
        return plane(P_SPREAD + step, lambda peer: c.rps.at[peer], c.rpl.at[step, b])

    def share_sources(step):
        total = c.rpl[step, 0].astype(F32)
        for q in range(1, B):
            total = total + c.rpl[step, q].astype(F32)
        for q in range(R):
            k, lane = (q * NQ) // LO, (q * NQ) % LO
            c.fzs[step, q] = total[k * J : (k + 1) * J, lane : lane + NQ]
        c.fzl[step, r] = c.fzs[step, r]
        return line(Z_SOURCE + step, lambda peer: c.fzs.at[step, peer], c.fzl.at[step, r])

    def state_grad(step):
        return c.gradq[...] + c.fzl[step].reshape(H, NQ).T

    last = STEPS - 1
    copies = deltas(last, c.cot[nodes_here, :])
    arrive(copies)
    final_in = line(Z_FINAL, lambda peer: c.fin, c.final.at[nodes_here, :])
    node_grads(last)
    sources(last, 0, tiles)
    spread = spread_sources(last)
    weights(last, 0, 3)
    arrive(spread, reuse=True)
    pieces = share_sources(last)
    weights(last, 3, 5)
    arrive(pieces)
    copies = deltas(0, state_grad(last))
    weights(last, 5, tiles)
    arrive(copies)
    def group_rows(t, carry):
        rows = pl.ds(pl.multiple_of(t * GROUP, GROUP), GROUP)
        c.gv[rows, :] = c.gfull[0, jnp.minimum(c.plan[0, t], s.G - 1)]
        return carry

    lax.fori_loop(0, s.V, group_rows, 0, unroll=8)
    grads_t = nt(eye_h, c.gv[...]).astype(BF16)

    def second_weight_rows(k, carry):
        held = [
            c.q0[:, pl.ds(pl.multiple_of((2 * k + p) * GROUP, GROUP), GROUP), :] for p in range(2)
        ]
        held = [x.reshape(s.V * GROUP, H) for x in held]
        more = nn(grads_t, jnp.concatenate(held, axis=1))
        for p in range(2):
            rows = pl.ds(pl.multiple_of((2 * k + p) * H, H), H)
            c.gacc[rows, :] += more[:, p * H : (p + 1) * H]
        return carry

    lax.fori_loop(0, J // 2, second_weight_rows, 0, unroll=4)

    per_owner = jh // OW

    def grad_rows(q):
        return c.gacc[pl.ds(pl.multiple_of(q * per_owner, per_owner), per_owner), :]

    if STRIDE == 1:
        def pieces_in(ref, first):
            return lambda m: ref.at[pl.ds(pl.multiple_of((first + m) * T, T), T)]

        from_pair, from_chip = pieces_in(c.w2r, 0), pieces_in(c.w2r, s.C)
        to_pair, to_chip = pieces_in(c.baug, 0), pieces_in(c.baug, s.C)
        pair = []
        for m in range(s.C):
            piece = grad_rows(device(m, 1 - core)).astype(BF16).reshape(T, H, H)
            c.baug[m * T : (m + 1) * T] = piece
            x = P_GRAD_PAIR
            cp = push(
                to_pair(m),
                from_pair(m),
                c.ps.at[x, m],
                c.pr.at[x, m],
                "blk",
                device(chip, 1 - core),
            )
            cp.start()
            pair.append(cp)
        sent.extend(pair)
    else:
        c.gsend[...] = c.gacc[...].astype(BF16)

        def own_grads():
            c.gland[b] = grad_rows(owner).astype(BF16)

        when_owner(own_grads)
        grads_wait = to_owners(
            P_GRAD,
            lambda q: c.gsend.at[pl.ds(pl.multiple_of(q * per_owner, per_owner), per_owner), :],
            c.gland.at[b],
        )

    node_grads(0)

    c.sgsend[...] = c.small[...].astype(BF16)

    def small_rows(q):
        return pl.ds(pl.multiple_of(q * s.SMALL, s.SMALL), s.SMALL)

    def own_small():
        c.sgland[b] = c.sgsend[small_rows(owner), :]

    when_owner(own_small)
    small_wait = to_owners(P_SMALL, lambda q: c.sgsend.at[small_rows(q), :], c.sgland.at[b])

    if STRIDE == 1:
        across = []
        for m in list(range(1, s.C)) + [0]:
            other = lax.rem(chip + m, s.C)
            if m == 1:
                arrive(pair)
            total = grad_rows(device(other, core)).reshape(T, H, H)
            total = (total + from_pair(other)[...].astype(F32)).astype(BF16)
            if m == 0:
                c.w2r[pl.ds(pl.multiple_of((s.C + chip) * T, T), T)] = total
                continue
            c.baug[(s.C + m) * T : (s.C + m + 1) * T] = total
            x = P_GRAD
            cp = push(
                to_chip(m),
                from_chip(chip),
                c.ps.at[x, m],
                c.pr.at[x, m],
                "blk",
                device(other, core),
            )
            cp.start()
            across.append(cp)
        sent.extend(across)

        def grads_wait():
            arrive(across)

    def total_of(ref, rows, count):
        total = ref[0, rows, :].astype(F32)
        for q in range(1, count):
            total = total + ref[q, rows, :].astype(F32)
        return total

    sources(0, 0, tiles)
    spread = spread_sources(0)
    small_wait()

    def reduce_small():
        c.sgz[r] = total_of(c.sgland, slice(None), B).astype(BF16)

    when_owner(reduce_small)
    small_in = line_owner(Z_SMALL, lambda peer: c.sgz.at[r], c.sgz.at[r])
    weights(0, 0, 2)
    grads_wait()

    def reduce_grads():
        for t in range(T):
            if STRIDE == 1:
                total = c.w2r[s.C * T + t].astype(F32)
                for q in range(1, s.C):
                    total = total + c.w2r[(s.C + q) * T + t].astype(F32)
            else:
                total = total_of(c.gland, slice(t * H, (t + 1) * H), B)
            total = total.astype(BF16)
            for q in range(R):
                c.gz[q, t * J : (t + 1) * J, :] = total[q * J : (q + 1) * J, :]
        c.f[r, owner] = c.gz[r]

    when_owner(reduce_grads)
    second_in = line_owner(Z_SECOND, lambda peer: c.gz.at[peer], c.f.at[r, owner])
    weights(0, 2, 5)
    arrive(spread)
    pieces = share_sources(0)
    weights(0, 5, 7)

    def sum_small():
        arrive(small_in)
        c.f[R, owner] = total_of(c.sgz, slice(None), R).astype(BF16)
        arrive(second_in)

    when_owner(sum_small)
    second_relay, second_wait, _, _ = from_owners(
        P_GRAD_ALL, P_GRAD_ALL_PAIR, lambda q: c.f.at[:, q]
    )

    weights(0, 7, tiles)

    w1 = c.w1[...]
    c.firsts[...] = jnp.zeros_like(c.firsts)

    def first_layer(t, carry):
        e = edges(t)
        mt = c.mt[:, e]
        pre = nn(w1ta, mt)
        gate = jax.nn.sigmoid(pre)
        pre_grad = c.hg[:, e] * gate * (1.0 + pre * (1.0 - gate))
        high, low = two(pre_grad)
        c.fqs[:, e] = ((nn(w1, high) + nn(w1, low)) * c.gm[:, e].astype(F32)).astype(BF16)
        c.firsts[...] += nt(mt, high) + nt(mt, low)
        return carry

    lax.fori_loop(0, tiles, first_layer, 0)
    edges_here = pl.ds(pl.multiple_of(r * EQ, EQ), EQ)
    c.fql[r] = c.fqs[:, edges_here]
    feats_in = line(
        Z_FEATS,
        lambda peer: c.fqs.at[:, pl.ds(pl.multiple_of(peer * EQ, EQ), EQ)],
        c.fql.at[r],
    )
    c.flz[r] = c.firsts[...]
    firsts_in = line(Z_FIRST, lambda peer: c.firsts, c.flz.at[r])

    arrive(pieces)
    grad = state_grad(0).astype(BF16)
    c.gradl[...] = grad
    c.grads[nodes_here, :] = grad
    grads_in = line(Z_GRADS, lambda peer: c.gradl, c.grads.at[nodes_here, :])

    arrive(feats_in)
    c.ff[:, edges_here] = total_of(c.fql, slice(None), R).astype(BF16)
    feats_all = line(Z_FEATS_ALL, lambda peer: c.ff.at[:, edges_here], c.ff.at[:, edges_here])
    arrive(firsts_in)
    c.flp[b] = total_of(c.flz, slice(None), R)
    firsts_all = plane(P_FIRST, lambda peer: c.flp.at[b], c.flp.at[b])
    second_relay()
    arrive(grads_in)
    arrive(final_in)
    arrive(firsts_all)
    c.fl[...] = total_of(c.flp, slice(None), B)
    arrive(feats_all)
    second_wait()
    for cp in sent:
        cp.wait_send()
    when_owner(lambda: [cp.wait_send() for cp in owner_sent] and None)


FINISH_NAMES = (
    ["f", "ff", "final", "grads", "fl"]
    + ["o_final", "o_grads", "feats", "w2", "win", "wst", "bin", "bst", "w1", "b1", "b2"]
    + ["hf", "hff", "hgrads", "hfl", "wide", "turn", "sems"]
)


def finish(s, *refs):
    c = SimpleNamespace(**dict(zip(FINISH_NAMES, refs)))
    H, J = s.H, s.J
    pairs = [(c.f, c.hf), (c.ff, c.hff), (c.grads, c.hgrads), (c.final, c.o_final)]
    pairs.append((c.fl, c.hfl))
    copies = [pltpu.make_async_copy(x, y, c.sems.at[k]) for k, (x, y) in enumerate(pairs)]
    for cp in copies:
        cp.start()
    copies[0].wait()
    c.wide[...] = c.hf[0 : s.R].reshape(H * J, H).astype(F32)
    for i in range(J):
        c.w2[:, i * H : (i + 1) * H] = c.wide[pl.ds(i, H, stride=J), :].T
    small = c.hf[s.R].reshape(SMALL_ROWS, H).astype(F32)
    for k in range(3):
        cut = slice(k * H, (k + 1) * H)
        c.win[:, cut] = small[k * H : (k + 1) * H]
        c.wst[:, cut] = small[ROW_STATE_WEIGHT + k * H : ROW_STATE_WEIGHT + (k + 1) * H]
    c.bin[...] = small[ROW_INPUT_BIAS : ROW_INPUT_BIAS + 3]
    c.bst[...] = small[ROW_STATE_BIAS : ROW_STATE_BIAS + 3]
    copies[4].wait()
    c.w1[...] = c.hfl[0:16]
    c.b1[...] = c.hfl[16:17]
    c.turn[...] = small[ROW_SECOND_BIAS : ROW_SECOND_BIAS + H].T
    r = lax.axis_index("rep")
    c.b2[...] = c.turn[pl.ds(pl.multiple_of(r * J, J), J), :]
    copies[1].wait()
    c.feats[...] = c.hff[...].astype(F32)
    copies[2].wait()
    c.o_grads[...] = c.hgrads[...].astype(F32)
    copies[3].wait()


def body(
    s,
    node_states,
    edge_feats,
    edge_source,
    edge_target,
    edge_group,
    column_mask,
    edge_count,
    first_weight,
    first_bias,
    second_weight,
    second_bias,
    update_input_weight,
    update_state_weight,
    update_input_bias,
    update_state_bias,
    state_cotangent,
):
    H, N, E = s.H, s.N, s.E
    shapes = scratch(s)
    names = ["in_" + k for k in IN_NAMES] + OUT_NAMES + IN_NAMES + list(shapes)
    sds = jax.ShapeDtypeStruct
    hbm = pl.BlockSpec(memory_space=pl.ANY)
    operands = (
        node_states,
        edge_feats.T,
        edge_source.reshape(1, E),
        edge_target.reshape(1, E),
        edge_group.reshape(1, E),
        column_mask,
        edge_count.reshape(1, 1),
        first_weight,
        first_bias.reshape(1, H),
        second_weight,
        second_bias.reshape(s.J, H),
        update_input_weight,
        update_state_weight,
        update_input_bias.reshape(3, H),
        update_state_bias.reshape(3, H),
        state_cotangent,
    )
    held = [
        pltpu.VMEM((8, 128) if name == "w2" else x.shape, F32 if name == "w2" else x.dtype)
        for name, x in zip(IN_NAMES, operands)
    ]
    final, grads, ff, f, fl = pl.pallas_call(
        functools.partial(whole, s, names),
        out_shape=[
            sds((N, H), F32),
            sds((N, H), BF16),
            sds((16, E), BF16),
            sds((s.R + 1, s.OW, s.T * s.J, H), BF16),
            sds((FIRST_ROWS, H), F32),
        ],
        in_specs=[hbm] * 16,
        out_specs=[VMEM] * 5,
        scratch_shapes=held + list(shapes.values()),
        compiler_params=pltpu.CompilerParams(
            collective_id=0, has_side_effects=True, vmem_limit_bytes=63 * 2**20
        ),
        name="edge_network",
    )(*operands)
    final, grads, feats, w2, win, wst, bin_, bst, w1, b1, b2 = pl.pallas_call(
        functools.partial(finish, s),
        out_shape=[
            sds((N, H), F32),
            sds((N, H), F32),
            sds((16, E), F32),
            sds((H, s.J * H), F32),
            sds((H, 3 * H), F32),
            sds((H, 3 * H), F32),
            sds((3, H), F32),
            sds((3, H), F32),
            sds((16, H), F32),
            sds((1, H), F32),
            sds((s.J, H), F32),
        ],
        in_specs=[hbm] * 5,
        out_specs=[VMEM] * 11,
        scratch_shapes=[
            pltpu.VMEM((s.R + 1, s.OW, s.T * s.J, H), BF16),
            pltpu.VMEM((16, E), BF16),
            pltpu.VMEM((N, H), BF16),
            pltpu.VMEM((FIRST_ROWS, H), F32),
            pltpu.VMEM((H * s.J, H), F32),
            pltpu.VMEM((H, H), F32),
            pltpu.SemaphoreType.DMA((5,)),
        ],
        compiler_params=pltpu.CompilerParams(vmem_limit_bytes=60 * 2**20),
        name="finish",
    )(f, ff, final, grads, fl)
    return (
        final,
        grads,
        feats.T,
        w1,
        b1.reshape(-1),
        w2,
        b2.reshape(-1),
        win,
        wst,
        bin_.reshape(-1),
        bst.reshape(-1),
    )


def solution(mesh):
    in_specs = (
        P("blk", None),
        P("blk", None),
        P("blk"),
        P("blk"),
        P("blk"),
        P(),
        P("blk"),
        P(),
        P(),
        P(None, "rep"),
        P("rep"),
        P(),
        P(),
        P(),
        P(),
        P("blk", None),
    )
    out_specs = (
        P("blk", None),
        P("blk", None),
        P("blk", None),
        P(),
        P(),
        P(None, "rep"),
        P("rep"),
        P(),
        P(),
        P(),
        P(),
    )

    def run(*args):
        nodes, edges, width = args[0].shape[0], args[2].shape[0], args[0].shape[1]
        return body(sizes(mesh, edges, nodes, width), *args)

    return jax.shard_map(run, mesh=mesh, in_specs=in_specs, out_specs=out_specs, check_vma=False)
```

```python
import functools
from types import SimpleNamespace

import jax
import jax.numpy as jnp
from jax import lax
from jax.experimental import pallas as pl
from jax.experimental.pallas import tpu as pltpu
from jax.sharding import PartitionSpec as P

STEPS = 2
TILE = 512
LO = 256
ROWS = 512
SLAB = 32
VISITS = (22, 34)
NEAR = 2
F32, BF16, I32 = jnp.float32, jnp.bfloat16, jnp.int32
MESH = pl.DeviceIdType.MESH
VMEM = pl.BlockSpec(memory_space=pltpu.VMEM)

ROW_STATE_WEIGHT = 384
ROW_INPUT_BIAS = 768
ROW_STATE_BIAS = 776
GROUP = 16
FIRST_ROWS = 32
ROW_SECOND_BIAS = 896
SMALL_ROWS = 1024

(
    P_STATE,
    P_STATE2,
    P_WEIGHT,
    P_WEIGHT_PAIR,
    P_SPREAD,
    P_SPREAD2,
    P_GRAD_PAIR,
    P_GRAD,
    P_SMALL,
    P_FIRST,
    P_GRAD_ALL,
    P_GRAD_ALL_PAIR,
    PLANES,
) = range(13)
(
    Z_WEIGHT,
    Z_BIAS,
    Z_SUM,
    Z_SUM2,
    Z_STATE,
    Z_FINAL,
    Z_DELTA,
    Z_DELTA2,
    Z_SOURCE,
    Z_SOURCE2,
    Z_GRADS,
    Z_FEATS,
    Z_FEATS_ALL,
    Z_SECOND,
    Z_SMALL,
    Z_FIRST,
    LINES,
) = range(17)


def nn(a, b):
    return jnp.dot(a, b, preferred_element_type=F32)


def nt(a, b):
    return lax.dot_general(a, b, (((1,), (1,)), ((), ())), preferred_element_type=F32)


def iota(shape, dim):
    return lax.broadcasted_iota(I32, shape, dim)


def ones_where(condition):
    return jnp.where(condition, 1.0, 0.0).astype(BF16)


def eye(n):
    return ones_where(iota((n, n), 0) == iota((n, n), 1))


def two(x):
    high = x.astype(BF16)
    return high, (x - high.astype(F32)).astype(BF16)


def three(x):
    high, rest = x.astype(BF16), x
    rest = x - high.astype(F32)
    mid = rest.astype(BF16)
    return high, mid, (rest - mid.astype(F32)).astype(BF16)


def nn2(a, x):
    high, low = two(x)
    return nn(a, high) + nn(a, low)


def nt2(x, b):
    high, low = two(x)
    return nt(high, b) + nt(low, b)


def sizes(mesh, edges, nodes, width):
    s = SimpleNamespace()
    s.B, s.R = mesh.shape["blk"], mesh.shape["rep"]
    s.E, s.N, s.H = edges, nodes, width
    s.J = width // s.R
    s.HIB = nodes // LO
    s.HI = s.HIB * s.B
    s.NQ = nodes // s.R
    s.EQ = edges // s.R
    s.OW = min(s.B, 8)
    s.STRIDE = s.B // s.OW
    s.T = s.J // s.OW
    s.KEEP = s.B <= 8
    s.SMALL = SMALL_ROWS // s.OW
    s.C = s.B // 2
    s.G = nodes // GROUP
    s.V = s.G + edges // LO
    return s


def scratch(s):
    v = pltpu.VMEM
    jh = s.J * s.H
    shapes = dict(
        nst=v((s.H, s.N), F32),
        stq=v((STEPS, s.HIB, s.J, LO), BF16),
        tab=v((STEPS, s.B, s.HIB, s.J, LO), BF16),
        ys=v((s.R * s.T, s.J, s.H), F32),
        wsend=v((s.R, s.T, s.J, s.H), BF16),
        w2r=v((s.J, s.H, s.H), BF16),
        b2f=v((s.H, s.H), F32),
        baug=v((s.J, s.H, s.H), BF16),
        w2k=v((s.H, jh), BF16),
        tl=v((1, s.E), I32),
        ohln=v((s.E, LO), BF16),
        mt=v((32, s.E), BF16),
        gm=v((16, s.E), BF16),
        ht=v((s.E // LO, s.H, LO), BF16),
        tlc=v((s.E // LO, 1, LO), I32),
        st=v((STEPS, s.J, s.E), BF16),
        sf=v((s.J, s.E), F32),
        sc=v((s.E // LO, s.J, LO), BF16),
        ge=v((s.H, s.E), BF16),
        smt=v((2 * s.H + s.J, s.N), F32),
        ssum=v((STEPS, s.J, s.N), F32),
        rsq=v((s.R, s.H, s.NQ), F32),
        rsl=v((STEPS, s.R, s.H, s.NQ), F32),
        keep=v((STEPS, 5, s.NQ, s.H), F32),
        keept=v((STEPS, 2, s.H, s.NQ), BF16),
        nsq=v((s.H, s.NQ), BF16),
        fin=v((s.NQ, s.H), F32),
        gq=v((STEPS, s.NQ // GROUP, GROUP, s.H), BF16),
        gfull=v((STEPS, s.G, GROUP, s.H), BF16),
        hg=v((s.H, s.E), F32),
        gacc=v((jh, s.H), F32),
        xs=v((ROWS, TILE), BF16),
        scat=v((s.HI * s.J, LO), F32),
        rps=v((s.B, s.HIB * s.J, LO), BF16),
        rpl=v((STEPS, s.B, s.HIB * s.J, LO), BF16),
        fzs=v((STEPS, s.R, s.J, s.NQ), F32),
        fzl=v((STEPS, s.R, s.J, s.NQ), F32),
        gradq=v((s.NQ, s.H), F32),
        gradl=v((s.NQ, s.H), BF16),
        small=v((SMALL_ROWS, s.H), F32),
        q0=v((s.V, s.J * GROUP, s.H), BF16),
        gv=v((s.V * GROUP, s.H), BF16),
        planv=v((8, 128), I32),
        plan=pltpu.SMEM((8, 128), I32),
        firsts=v((FIRST_ROWS, s.H), F32),
        flz=v((s.R, FIRST_ROWS, s.H), F32),
        flp=v((s.B, FIRST_ROWS, s.H), F32),
        sgsend=v((SMALL_ROWS, s.H), BF16),
        sgland=v((s.B, s.SMALL, s.H), BF16),
        gz=v((s.R, s.T * s.J, s.H), BF16),
        sgz=v((s.R, s.SMALL, s.H), BF16),
        fqs=v((16, s.E), BF16),
        fql=v((s.R, 16, s.EQ), BF16),
        ps=pltpu.SemaphoreType.DMA((PLANES, s.B)),
        pr=pltpu.SemaphoreType.DMA((PLANES, s.B)),
        zs=pltpu.SemaphoreType.DMA((LINES, s.R)),
        zr=pltpu.SemaphoreType.DMA((LINES, s.R)),
        local=pltpu.SemaphoreType.DMA,
        ins=pltpu.SemaphoreType.DMA((len(IN_NAMES),)),
    )
    piece = (jh // s.OW, s.H)
    if s.STRIDE > 1:
        shapes["gland"] = v((s.B,) + piece, BF16)
        shapes["gsend"] = v((jh, s.H), BF16)
    if s.KEEP:
        shapes["mat"] = v((jh, s.E), BF16)
        shapes["sums"] = v((2, s.J, jh // 4), BF16)
    return shapes


IN_NAMES = (
    ["nodes", "feats", "src", "tgt", "grp", "cmask", "count", "w1", "b1"]
    + ["w2", "b2", "win", "wst", "bin", "bst", "cot"]
)
OUT_NAMES = ["final", "grads", "ff", "f", "fl"]


def whole(s, names, *refs):
    c = SimpleNamespace(**dict(zip(names, refs)))
    B, R, H, J, E, N, NQ, EQ = s.B, s.R, s.H, s.J, s.E, s.N, s.NQ, s.EQ
    T, OW, STRIDE = s.T, s.OW, s.STRIDE
    jh = J * H
    tiles = E // TILE
    b = lax.axis_index("blk")
    r = lax.axis_index("rep")
    owner = b // STRIDE
    is_owner = lax.rem(b, STRIDE) == 0
    sent = []

    def push(src, dst, sems, rems, axis, peer):
        return pltpu.make_async_remote_copy(
            src_ref=src,
            dst_ref=dst,
            send_sem=sems,
            recv_sem=rems,
            device_id={axis: peer},
            device_id_type=MESH,
        )

    def plane(x, src_of, dst):
        copies = []
        for d in range(1, B):
            peer = lax.rem(b + d, B)
            cp = push(src_of(peer), dst, c.ps.at[x, d], c.pr.at[x, d], "blk", peer)
            cp.start()
            copies.append(cp)
        sent.extend(copies)
        return copies

    def line(x, src_of, dst):
        copies = []
        for d in range(1, R):
            peer = lax.rem(r + d, R)
            cp = push(src_of(peer), dst, c.zs.at[x, d], c.zr.at[x, d], "rep", peer)
            cp.start()
            copies.append(cp)
        sent.extend(copies)
        return copies

    def arrive(copies, reuse=False):
        for cp in copies:
            cp.wait_recv()
        if reuse:
            release(copies)

    def release(copies):
        for cp in copies:
            cp.wait_send()
            sent[:] = [other for other in sent if other is not cp]

    def when_owner(fn):
        if STRIDE == 1:
            fn()
        else:
            pl.when(is_owner)(fn)

    def line_owner(x, src_of, dst):
        copies = []
        for d in range(1, R):
            peer = lax.rem(r + d, R)
            copies.append(push(src_of(peer), dst, c.zs.at[x, d], c.zr.at[x, d], "rep", peer))
        when_owner(lambda: [cp.start() for cp in copies] and None)
        owner_sent.extend(copies)
        return copies

    owner_sent = []

    def from_owners(x, strip_of):
        copies = []
        for d in range(1, B):
            peer = lax.rem(b + d, B)
            strip = strip_of(owner)
            copies.append(push(strip, strip, c.ps.at[x, d], c.pr.at[x, owner], "blk", peer))
        when_owner(lambda: [cp.start() for cp in copies] and None)
        owner_sent.extend(copies)

        def wait():
            for q in range(OW):

                @pl.when(b != q * STRIDE)
                def _():
                    strip = strip_of(q)
                    peer = lax.rem(b + 1, B)
                    push(strip, strip, c.ps.at[x, 0], c.pr.at[x, q], "blk", peer).wait_recv()

        return lambda: None, wait, [], []

    chip, core = b // 2, lax.rem(b, 2)

    column, line_of = lax.rem(chip, 2), chip // 2
    lines = max(s.C // 2, 1)

    def device(m, its_core, back=False):
        up = lines - m // 2 if back else m // 2
        return 2 * (2 * lax.rem(line_of + up, lines) + lax.rem(column + lax.rem(m, 2), 2)) + its_core

    def slot_rows(at):
        if STRIDE > 1:
            return at
        slot = at // T
        held_by = jnp.where(slot < s.C, core, 1 - core)
        return T * device(lax.rem(slot, s.C), held_by, True) + lax.rem(at, T)

    def slot(k):
        return c.w2r.at[k * T : (k + 1) * T]

    def gather_pairs(x, x2, first_of, then_of, late=s.C):
        first, then = [], []
        for m in range(1, s.C):
            src, dst = first_of(m)
            first.append(push(src, dst, c.ps.at[x, m], c.pr.at[x, m], "blk", device(m, core)))
        for m in range(s.C):
            src, dst = then_of(m)
            then.append(
                push(src, dst, c.ps.at[x2, m], c.pr.at[x2, m], "blk", device(0, 1 - core))
            )
        for cp in first[:late] + then[:1]:
            cp.start()

        def relay(begin=1, end=s.C):
            for m in range(begin, end):
                first[m - 1].wait_recv()
                then[m].start()

        def wait():
            arrive(then)

        sent.extend(first + then)
        return relay, wait, first, then

    def to_owners(x, src_of, dst):
        if STRIDE == 1:
            copies = plane(x, src_of, dst)
            return lambda: arrive(copies)
        for q in range(OW):

            @pl.when(b != q * STRIDE)
            def _():
                push(src_of(q), dst, c.ps.at[x, q], c.pr.at[x, b], "blk", q * STRIDE).start()

        def wait():
            def arrivals():
                for d in range(1, B):
                    peer = lax.rem(b + d, B)
                    push(src_of(0), dst, c.ps.at[x, 0], c.pr.at[x, peer], "blk", peer).wait_recv()

            when_owner(arrivals)
            for q in range(OW):

                @pl.when(b != q * STRIDE)
                def _():
                    push(src_of(q), dst, c.ps.at[x, q], c.pr.at[x, b], "blk", q * STRIDE).wait_send()

        return wait

    def edges(t):
        return pl.ds(pl.multiple_of(t * TILE, TILE), TILE)

    barrier = pltpu.get_barrier_semaphore()
    for d in range(1, B):
        pl.semaphore_signal(
            barrier, inc=1, device_id={"blk": lax.rem(b + d, B)}, device_id_type=MESH
        )
    for d in range(1, R):
        pl.semaphore_signal(
            barrier, inc=1, device_id={"rep": lax.rem(r + d, R)}, device_id_type=MESH
        )

    loads = {}
    for k, name in enumerate(IN_NAMES):
        to = c.w2k if name == "w2" else getattr(c, name)
        loads[name] = pltpu.make_async_copy(getattr(c, "in_" + name), to, c.ins.at[k])
    for name in ["nodes", "w2"]:
        loads[name].start()
    for name in IN_NAMES:
        if name not in ("nodes", "w2"):
            loads[name].start()
    eye_h = eye(H)
    part = pl.ds(pl.multiple_of(r * J, J), J)

    loads["nodes"].wait()
    c.nst[...] = c.nodes[...].T
    own_columns = c.nst[part, :].astype(BF16)
    for k in range(s.HIB):
        c.stq[0, k] = own_columns[:, k * LO : (k + 1) * LO]
    c.tab[0, b] = c.stq[0]
    row = iota((R * T, H), 0)
    pick = ones_where(iota((R * T, H), 1) == (row // T) * J + T * owner + lax.rem(row, T))
    loads["w2"].wait()
    for i in range(J):
        c.ys[:, i, :] = nt(pick, c.w2k[:, i * H : (i + 1) * H])
    c.wsend[...] = c.ys[...].astype(BF16).reshape(R, T, J, H)
    for name in IN_NAMES:
        if name not in ("nodes", "w2"):
            loads[name].wait()
    pl.semaphore_wait(barrier, B - 1 + R - 1)

    states_in = plane(P_STATE, lambda peer: c.stq.at[0], c.tab.at[0, b])
    strip = pl.ds(0 if STRIDE == 1 else pl.multiple_of(T * owner, T), T)
    weight_in = line_owner(Z_WEIGHT, lambda peer: c.wsend.at[peer], c.w2r.at[strip, part, :])
    c.b2f[part, :] = c.b2[...]
    bias_in = line(Z_BIAS, lambda peer: c.b2, c.b2f.at[part, :])

    def own_strip():
        c.w2r[strip, part, :] = c.wsend[r]

    when_owner(own_strip)

    place = iota((1, E), 1)
    c.tl[...] = jnp.where(place < c.count[...], c.tgt[...] - b * N, -1)
    for k in range(E // LO):
        c.tlc[k] = c.tl[:, k * LO : (k + 1) * LO]
    ends = jnp.where(c.tgt[...] - b * N < GROUP * (iota((s.G, E), 0) + 1), 1, 0)
    ends = jnp.sum(ends, axis=1, keepdims=True)
    left_in = jnp.maximum((ends + (LO - 1)) // LO - 1, 0)
    group = iota((s.G, 128), 0)
    leave = group + jnp.where(group == s.G - 1, E // LO - 1, left_in)
    visited = jnp.sum(jnp.where(leave < iota((s.G, 128), 1), 1, 0), axis=0, keepdims=True)
    c.planv[...] = jnp.broadcast_to(visited, (8, 128))
    plan_copy = pltpu.make_async_copy(c.planv, c.plan, c.local)
    plan_copy.start()
    cmt = nt(eye(16), c.cmask[...].astype(F32).astype(BF16)).astype(BF16)
    b1 = three(c.b1[...])
    first = jnp.concatenate(
        [c.w1[...].astype(F32)] + [x.astype(F32) for x in b1] + [jnp.zeros((13, H), F32)], axis=0
    ).astype(BF16)
    w1ta = nt(eye_h, first).astype(BF16)
    eye_t = eye(LO)

    def target_rows(t):
        return ones_where(iota((N, TILE), 0) == c.tl[:, edges(t)])

    def low_rows(t):
        return ones_where(iota((LO, TILE), 0) == (c.src[:, edges(t)] & (LO - 1)))

    per_tile = TILE // LO

    def put(ref, t, value):
        for k in range(per_tile):
            ref[t * per_tile + k] = value[:, k * LO : (k + 1) * LO]

    def hidden_of(t):
        return jnp.concatenate([c.ht[t * per_tile + k] for k in range(per_tile)], axis=1)

    def prepare(t, carry):
        e = edges(t)
        groups = ones_where(iota((16, TILE), 0) == c.grp[:, e])
        gm = nn(cmt, groups)
        c.gm[:, e] = gm.astype(BF16)
        masked = c.feats[:, e].astype(F32) * gm
        ones = jnp.where(iota((16, TILE), 0) < 3, 1.0, 0.0)
        mt = jnp.concatenate([masked, ones], axis=0).astype(BF16)
        c.mt[:, e] = mt
        pre = nn(w1ta, mt)
        hidden = (pre * jax.nn.sigmoid(pre)).astype(BF16)
        put(c.ht, t, hidden)
        lows = low_rows(t)
        for k in range(TILE // LO):
            rows = pl.ds(pl.multiple_of(t * TILE + k * LO, LO), LO)
            c.ohln[rows, :] = nt(eye_t, lows[:, k * LO : (k + 1) * LO]).astype(BF16)
        return carry

    lax.fori_loop(0, tiles, prepare, 0)

    when_owner(lambda: arrive(weight_in))
    if STRIDE == 1:
        weight_relay, weight_wait, weight_chip, weight_pair = gather_pairs(
            P_WEIGHT,
            P_WEIGHT_PAIR,
            lambda m: (slot(0), slot(m)),
            lambda m: (slot(m), slot(s.C + m)),
        )
    else:
        weight_relay, weight_wait, weight_chip, weight_pair = from_owners(
            P_WEIGHT, lambda q: c.w2r.at[pl.ds(pl.multiple_of(T * q, T), T)]
        )

    to_slots = ones_where(iota((J, J), 1) == slot_rows(iota((J, J), 0)))
    from_slots = ones_where(iota((J, J), 0) == slot_rows(iota((J, J), 1)))

    def gather(step):
        if STRIDE == 1:
            for q in range(B):
                for k in range(s.HIB):
                    c.tab[step, q, k] = nn(to_slots, c.tab[step, q, k]).astype(BF16)

        def one(t, carry):
            e = edges(t)
            lows = low_rows(t)
            high = c.src[:, e] // LO
            total = jnp.zeros((J, TILE), F32)
            per = ROWS // J
            for g in range(s.HI // per):
                blocks = per // s.HIB
                table = c.tab[step, g * blocks : (g + 1) * blocks].reshape(ROWS, LO)
                rows = nn(table, lows)
                for k in range(per):
                    total = total + jnp.where(high == g * per + k, rows[k * J : (k + 1) * J], 0.0)
            c.st[step, :, e] = total.astype(BF16)
            c.sf[:, e] = total
            if step == 0:
                put(c.sc, t, total.astype(BF16))
            return carry

        lax.fori_loop(0, tiles, one, 0)

    arrive(states_in)
    gather(0)
    arrive(bias_in)
    b2 = jnp.concatenate(three(c.b2f[...]), axis=1)

    def bias_columns(j, carry):
        at = iota((3 * H, H), 0)
        to = iota((3 * H, H), 1)
        move = ones_where((lax.rem(at, H) == r * J + slot_rows(j)) & (to == at // H))
        c.baug[j] = nn(b2, move).astype(BF16)
        return carry

    lax.fori_loop(0, J, bias_columns, 0, unroll=8)

    def turned(j, carry):
        c.w2k[:, pl.ds(pl.multiple_of(j * H, H), H)] = nt(eye_h, c.w2r[j]).astype(BF16)
        return carry

    chunk = ROWS // H

    def hidden_rows(t):
        ones = jnp.where(iota((H, TILE), 0) < 3, 1.0, 0.0).astype(BF16)
        return jnp.concatenate([hidden_of(t), ones], axis=0)

    def held_messages(t):
        e = edges(t)
        parts = []
        for k in range(H // SLAB):
            total = jnp.zeros((SLAB, TILE), F32)
            for j in range(J):
                at = j * H + k * SLAB
                total = total + c.mat[at : at + SLAB, e].astype(F32) * c.sf[j : j + 1, e]
            parts.append(total)
        return jnp.concatenate(parts, axis=0)

    half, few = J // 2, H // 2
    if s.KEEP:
        rows, columns = iota((J, half * few), 0), iota((J, half * few), 1) // few
        for k in range(2):
            c.sums[k] = ones_where(rows == slot_rows(columns + k * half))

    def held_sources(e):
        grads = c.ge[:, e]
        total = jnp.zeros((J, TILE), F32)
        for k in range(2):
            held = c.mat[k * half * H : (k + 1) * half * H, e].reshape(half, H, TILE)
            product = held * grads[None]
            product = product[:, :few] + product[:, few:]
            total = total + nn(c.sums[k], product.reshape(half * few, TILE))
        return total

    def matrices(k, e, hidden):
        cut = slice(k * chunk, (k + 1) * chunk)
        left = jnp.concatenate(
            [c.w2r[cut].reshape(ROWS, H), c.baug[cut].reshape(ROWS, H)], axis=1
        )
        return nn(left, hidden).astype(BF16).astype(F32)

    def first_pass(strips, start):
        def one(t, carry):
            e = edges(t)
            hidden = hidden_rows(t)
            total = jnp.zeros((H, TILE), F32) if start else c.hg[:, e]
            for q in strips:
                cut = slice(q * T, (q + 1) * T)
                left = jnp.concatenate(
                    [c.w2r[cut].reshape(T * H, H), c.baug[cut].reshape(T * H, H)], axis=1
                )
                low = nn(left, hidden).astype(BF16)
                c.mat[q * T * H : (q + 1) * T * H, e] = low
                m = low.astype(F32)
                for p in range(T):
                    total = total + m[p * H : (p + 1) * H] * c.sf[q * T + p : q * T + p + 1, e]
            c.hg[:, e] = total
            return carry

        lax.fori_loop(0, tiles, one, 0, unroll=4 if len(strips) < 3 else 2)

    def messages(step):
        c.smt[...] = jnp.zeros_like(c.smt)

        def one(t, carry):
            e = edges(t)
            low = c.st[step, :, e]
            if s.KEEP:
                total = held_messages(t) if step > 0 else c.hg[:, e]
            else:
                source = low.astype(F32)
                hidden = hidden_rows(t)
                total = jnp.zeros((H, TILE), F32)
                for k in range(J // chunk):
                    m = matrices(k, e, hidden)
                    for q in range(chunk):
                        j = k * chunk + q
                        total = total + m[q * H : (q + 1) * H] * source[j : j + 1, :]
            high, rest = two(total)
            rows = jnp.concatenate([high, rest, low], axis=0)
            c.smt[...] += nt(rows, target_rows(t))
            return carry

        lax.fori_loop(0, tiles, one, 0, unroll=2)
        summed = c.smt[0:H, :] + c.smt[H : 2 * H, :]
        c.ssum[step] = c.smt[2 * H : 2 * H + J, :]
        for q in range(R):
            c.rsq[q] = summed[:, q * NQ : (q + 1) * NQ]
        c.rsl[step, r] = c.rsq[r]
        return line(Z_SUM + step, lambda peer: c.rsq.at[peer], c.rsl.at[step, r])

    def gate_bias(ref):
        return jnp.concatenate([ref[k : k + 1, :] for k in range(3)], axis=1)

    def gates(step, before, before_t):
        summed = c.rsl[step, 0]
        for q in range(1, R):
            summed = summed + c.rsl[step, q]
        summed_low = summed.T.astype(BF16)
        gi = nn(summed_low, c.win[...]) + gate_bias(c.bin)
        gs = nn(before.astype(BF16), c.wst[...]) + gate_bias(c.bst)
        reset = jax.nn.sigmoid(gi[:, :H] + gs[:, :H])
        update = jax.nn.sigmoid(gi[:, H : 2 * H] + gs[:, H : 2 * H])
        state_part = gs[:, 2 * H :]
        candidate = jnp.tanh(gi[:, 2 * H :] + reset * state_part)
        for k, x in enumerate((before, reset, update, candidate, state_part)):
            c.keep[step, k] = x
        c.keept[step, 0] = summed.astype(BF16)
        c.keept[step, 1] = before_t
        return (1.0 - update) * candidate + update * before

    def products(begin, end):
        def one(t, carry):
            g = c.plan[0, t]
            ch = t - g
            mine = ones_where(iota((GROUP, LO), 0) + g * GROUP == c.tlc[ch])
            source = c.sc[ch].astype(F32)
            parts = []
            for j in range(J):
                row = jnp.broadcast_to(source[j : j + 1, :], (GROUP, LO)).astype(BF16)
                parts.append(row * mine)
            c.q0[t] = nt(jnp.concatenate(parts, axis=0), c.ht[ch]).astype(BF16)
            return carry

        lax.fori_loop(begin, end, one, 0)

    plan_copy.wait()
    nodes_here = pl.ds(pl.multiple_of(r * NQ, NQ), NQ)
    groups_here = pl.ds(pl.multiple_of(r * (NQ // GROUP), NQ // GROUP), NQ // GROUP)
    if s.KEEP:
        near = NEAR + 1
        first_pass([0], True)
        weight_relay()
        first_pass(range(1, s.C), False)
        arrive(weight_pair)
        first_pass(range(s.C, OW), False)
    else:
        weight_wait()
    sums = messages(0)
    lax.fori_loop(0, J, turned, 0, unroll=8)
    products(0, VISITS[0])
    arrive(sums, reuse=True)
    release(weight_chip + weight_pair)
    state = gates(0, c.nodes[nodes_here, :], c.nst[:, nodes_here].astype(BF16))
    state_t = state.T.astype(BF16)
    c.nsq[...] = state_t
    hib = r // (LO // NQ)
    lanes = pl.ds(pl.multiple_of(lax.rem(r, LO // NQ) * NQ, NQ), NQ)
    c.stq[1, hib, :, lanes] = c.nsq[part, :]
    pieces = line(
        Z_STATE,
        lambda peer: c.nsq.at[pl.ds(pl.multiple_of(peer * J, J), J), :],
        c.stq.at[1, hib, :, lanes],
    )
    products(VISITS[0], VISITS[1])
    arrive(pieces)
    c.tab[1, b] = c.stq[1]
    states_in = plane(P_STATE2, lambda peer: c.stq.at[1], c.tab.at[1, b])
    products(VISITS[1], s.V)
    arrive(states_in)
    gather(1)
    sums = messages(1)
    arrive(sums)
    final = gates(1, state, state_t)
    c.fin[...] = final
    c.final[nodes_here, :] = final

    c.small[...] = jnp.zeros_like(c.small)
    c.gacc[...] = jnp.zeros_like(c.gacc)

    def deltas(step, grad):
        before, reset, update, candidate, state_part = [c.keep[step, k] for k in range(5)]
        dn = grad * (1.0 - update)
        dz = grad * (before - candidate)
        dpn = dn * (1.0 - candidate * candidate)
        dpz = dz * update * (1.0 - update)
        dpr = dpn * state_part * reset * (1.0 - reset)
        to_input = jnp.concatenate([dpr, dpz, dpn], axis=1)
        to_state = jnp.concatenate([dpr, dpz, dpn * reset], axis=1)
        summed_grad = nt2(to_input, c.win[...]).astype(BF16)
        c.gq[step] = summed_grad.reshape(NQ // GROUP, GROUP, H)
        c.gfull[step, groups_here] = c.gq[step]
        copies = line(Z_DELTA + step, lambda peer: c.gq.at[step], c.gfull.at[step, groups_here])
        gwi = nn2(c.keept[step, 0], to_input)
        gws = nn2(c.keept[step, 1], to_state)
        gbi = jnp.sum(to_input, axis=0, keepdims=True)
        gbs = jnp.sum(to_state, axis=0, keepdims=True)
        for k in range(3):
            cut = slice(k * H, (k + 1) * H)
            c.small[k * H : (k + 1) * H, :] += gwi[:, cut]
            c.small[ROW_STATE_WEIGHT + k * H : ROW_STATE_WEIGHT + (k + 1) * H, :] += gws[:, cut]
            c.small[ROW_INPUT_BIAS + k : ROW_INPUT_BIAS + k + 1, :] += gbi[:, cut]
            c.small[ROW_STATE_BIAS + k : ROW_STATE_BIAS + k + 1, :] += gbs[:, cut]
        c.gradq[...] = grad * update + nt2(to_state, c.wst[...])
        return copies

    def node_grads(step):
        held = c.gfull[step].reshape(N, H)
        gt = nt(eye_h, held).astype(BF16)

        def one(t, carry):
            c.ge[:, edges(t)] = nn(gt, target_rows(t)).astype(BF16)
            return carry

        lax.fori_loop(0, tiles, one, 0, unroll=2)
        rows = pl.ds(ROW_SECOND_BIAS + pl.multiple_of(r * J, J), J)
        high, low = [nn(from_slots, x).astype(BF16) for x in two(c.ssum[step])]
        c.small[rows, :] += nn(high, held) + nn(low, held)

    def weights_tile(step, t, second):
        e = edges(t)
        at_edges = c.ge[:, e]
        source = c.st[step, :, e].astype(F32)
        got = None if step == STEPS - 1 else c.hg[:, e]
        spread = at_edges.reshape(H // 16, 16, TILE)
        for k in range(jh // ROWS):
            parts = []
            for j in range(k * ROWS // H, (k + 1) * ROWS // H):
                row = jnp.broadcast_to(source[j : j + 1, :], (16, TILE)).astype(BF16)
                parts.append((spread * row[None]).reshape(H, TILE))
            outer = jnp.concatenate(parts, axis=0)
            rows = slice(k * ROWS, (k + 1) * ROWS)
            more = nn(c.w2k[:, rows], outer)
            got = more if got is None else got + more
            if second:
                c.gacc[rows, :] += nt(outer, hidden_of(t))
        c.hg[:, e] = got

    def weights(step, begin, end):
        def one(t, carry):
            weights_tile(step, t, step == STEPS - 1)
            return carry

        lax.fori_loop(begin, end, one, 0)

    def sources(step, begin, end):
        if begin == 0:
            c.scat[...] = jnp.zeros_like(c.scat)

        def one(t, carry):
            e = edges(t)
            if s.KEEP:
                got = held_sources(e)
            else:
                at_edges = c.ge[:, e].astype(F32)
                hidden = hidden_rows(t)
                parts = []
                for k in range(J // chunk):
                    m = matrices(k, e, hidden)
                    for q in range(chunk):
                        parts.append(
                            jnp.sum(m[q * H : (q + 1) * H] * at_edges, axis=0, keepdims=True)
                        )
                got = jnp.concatenate(parts, axis=0)
            high = c.src[:, e] // LO
            per = ROWS // J
            for g in range(s.HI // per):
                for k in range(per):
                    c.xs[k * J : (k + 1) * J, :] = jnp.where(high == g * per + k, got, 0.0).astype(
                        BF16
                    )
                c.scat[g * ROWS : (g + 1) * ROWS, :] += nn(c.xs[...], c.ohln[e, :])
            return carry

        lax.fori_loop(begin, end, one, 0)

    def spread_sources(step):
        c.rps[...] = c.scat[...].astype(BF16).reshape(B, s.HIB * J, LO)
        c.rpl[step, b] = c.rps[b]
        return plane(P_SPREAD + step, lambda peer: c.rps.at[peer], c.rpl.at[step, b])

    def share_sources(step):
        total = c.rpl[step, 0].astype(F32)
        for q in range(1, B):
            total = total + c.rpl[step, q].astype(F32)
        for q in range(R):
            k, lane = (q * NQ) // LO, (q * NQ) % LO
            c.fzs[step, q] = total[k * J : (k + 1) * J, lane : lane + NQ]
        c.fzl[step, r] = c.fzs[step, r]
        return line(Z_SOURCE + step, lambda peer: c.fzs.at[step, peer], c.fzl.at[step, r])

    def state_grad(step):
        return c.gradq[...] + c.fzl[step].reshape(H, NQ).T

    last = STEPS - 1
    copies = deltas(last, c.cot[nodes_here, :])
    arrive(copies)
    final_in = line(Z_FINAL, lambda peer: c.fin, c.final.at[nodes_here, :])
    node_grads(last)
    sources(last, 0, tiles)
    spread = spread_sources(last)
    weights(last, 0, 3)
    arrive(spread, reuse=True)
    pieces = share_sources(last)
    weights(last, 3, 5)
    arrive(pieces)
    copies = deltas(0, state_grad(last))
    weights(last, 5, tiles)
    arrive(copies)
    def group_rows(t, carry):
        rows = pl.ds(pl.multiple_of(t * GROUP, GROUP), GROUP)
        c.gv[rows, :] = c.gfull[0, jnp.minimum(c.plan[0, t], s.G - 1)]
        return carry

    lax.fori_loop(0, s.V, group_rows, 0, unroll=8)
    grads_t = nt(eye_h, c.gv[...]).astype(BF16)

    def second_weight_rows(k, carry):
        held = [
            c.q0[:, pl.ds(pl.multiple_of((2 * k + p) * GROUP, GROUP), GROUP), :] for p in range(2)
        ]
        held = [x.reshape(s.V * GROUP, H) for x in held]
        more = nn(grads_t, jnp.concatenate(held, axis=1))
        for p in range(2):
            rows = pl.ds(pl.multiple_of((2 * k + p) * H, H), H)
            c.gacc[rows, :] += more[:, p * H : (p + 1) * H]
        return carry

    lax.fori_loop(0, J // 2, second_weight_rows, 0, unroll=4)

    per_owner = jh // OW

    def grad_rows(q):
        return c.gacc[pl.ds(pl.multiple_of(q * per_owner, per_owner), per_owner), :]

    if STRIDE == 1:
        def piece_rows(k):
            return c.gacc[k * per_owner : (k + 1) * per_owner, :].reshape(T, H, H)

        def pieces_in(ref, k):
            return ref.at[k * T : (k + 1) * T]

        pair = []
        for m in range(s.C):
            c.baug[m * T : (m + 1) * T] = piece_rows(s.C + m).astype(BF16)
            x = P_GRAD_PAIR
            cp = push(
                pieces_in(c.baug, m),
                pieces_in(c.w2r, m),
                c.ps.at[x, m],
                c.pr.at[x, m],
                "blk",
                device(0, 1 - core),
            )
            cp.start()
            pair.append(cp)
        sent.extend(pair)
    else:
        c.gsend[...] = c.gacc[...].astype(BF16)

        def own_grads():
            c.gland[b] = grad_rows(owner).astype(BF16)

        when_owner(own_grads)
        grads_wait = to_owners(
            P_GRAD,
            lambda q: c.gsend.at[pl.ds(pl.multiple_of(q * per_owner, per_owner), per_owner), :],
            c.gland.at[b],
        )

    node_grads(0)

    c.sgsend[...] = c.small[...].astype(BF16)

    def small_rows(q):
        return pl.ds(pl.multiple_of(q * s.SMALL, s.SMALL), s.SMALL)

    def own_small():
        c.sgland[b] = c.sgsend[small_rows(owner), :]

    when_owner(own_small)
    small_wait = to_owners(P_SMALL, lambda q: c.sgsend.at[small_rows(q), :], c.sgland.at[b])

    if STRIDE == 1:
        across = []
        for m in list(range(1, s.C)) + [0]:
            if m == 1:
                arrive(pair)
            total = piece_rows(m) + c.w2r[m * T : (m + 1) * T].astype(F32)
            total = total.astype(BF16)
            if m == 0:
                c.w2r[s.C * T : (s.C + 1) * T] = total
                continue
            c.baug[(s.C + m) * T : (s.C + m + 1) * T] = total
            x = P_GRAD
            cp = push(
                pieces_in(c.baug, s.C + m),
                pieces_in(c.w2r, s.C + m),
                c.ps.at[x, m],
                c.pr.at[x, m],
                "blk",
                device(m, core, True),
            )
            cp.start()
            across.append(cp)
        sent.extend(across)

        def grads_wait():
            arrive(across)

    def total_of(ref, rows, count):
        total = ref[0, rows, :].astype(F32)
        for q in range(1, count):
            total = total + ref[q, rows, :].astype(F32)
        return total

    sources(0, 0, tiles)
    spread = spread_sources(0)
    small_wait()

    def reduce_small():
        c.sgz[r] = total_of(c.sgland, slice(None), B).astype(BF16)

    when_owner(reduce_small)
    small_in = line_owner(Z_SMALL, lambda peer: c.sgz.at[r], c.sgz.at[r])
    weights(0, 0, 2)
    grads_wait()

    def reduce_grads():
        for t in range(T):
            if STRIDE == 1:
                total = c.w2r[s.C * T + t].astype(F32)
                for q in range(1, s.C):
                    total = total + c.w2r[(s.C + q) * T + t].astype(F32)
            else:
                total = total_of(c.gland, slice(t * H, (t + 1) * H), B)
            total = total.astype(BF16)
            for q in range(R):
                c.gz[q, t * J : (t + 1) * J, :] = total[q * J : (q + 1) * J, :]
        c.f[r, owner] = c.gz[r]

    when_owner(reduce_grads)
    second_in = line_owner(Z_SECOND, lambda peer: c.gz.at[peer], c.f.at[r, owner])
    weights(0, 2, 5)
    arrive(spread)
    pieces = share_sources(0)
    weights(0, 5, 7)

    def sum_small():
        arrive(small_in)
        c.f[R, owner] = total_of(c.sgz, slice(None), R).astype(BF16)
        arrive(second_in)

    when_owner(sum_small)
    if STRIDE == 1:

        def held_strip(m):
            strip = c.f.at[:, device(m, core, True)]
            return strip, strip

        second_relay, second_wait, _, _ = gather_pairs(
            P_GRAD_ALL, P_GRAD_ALL_PAIR, lambda m: held_strip(0), held_strip
        )
    else:
        second_relay, second_wait, _, _ = from_owners(P_GRAD_ALL, lambda q: c.f.at[:, q])

    weights(0, 7, tiles)

    w1 = c.w1[...]
    c.firsts[...] = jnp.zeros_like(c.firsts)

    def first_layer(t, carry):
        e = edges(t)
        mt = c.mt[:, e]
        pre = nn(w1ta, mt)
        gate = jax.nn.sigmoid(pre)
        pre_grad = c.hg[:, e] * gate * (1.0 + pre * (1.0 - gate))
        high, low = two(pre_grad)
        c.fqs[:, e] = ((nn(w1, high) + nn(w1, low)) * c.gm[:, e].astype(F32)).astype(BF16)
        c.firsts[...] += nt(mt, high) + nt(mt, low)
        return carry

    lax.fori_loop(0, tiles, first_layer, 0)
    edges_here = pl.ds(pl.multiple_of(r * EQ, EQ), EQ)
    c.fql[r] = c.fqs[:, edges_here]
    feats_in = line(
        Z_FEATS,
        lambda peer: c.fqs.at[:, pl.ds(pl.multiple_of(peer * EQ, EQ), EQ)],
        c.fql.at[r],
    )
    c.flz[r] = c.firsts[...]
    firsts_in = line(Z_FIRST, lambda peer: c.firsts, c.flz.at[r])

    arrive(pieces)
    grad = state_grad(0).astype(BF16)
    c.gradl[...] = grad
    c.grads[nodes_here, :] = grad
    grads_in = line(Z_GRADS, lambda peer: c.gradl, c.grads.at[nodes_here, :])

    arrive(feats_in)
    c.ff[:, edges_here] = total_of(c.fql, slice(None), R).astype(BF16)
    feats_all = line(Z_FEATS_ALL, lambda peer: c.ff.at[:, edges_here], c.ff.at[:, edges_here])
    arrive(firsts_in)
    c.flp[b] = total_of(c.flz, slice(None), R)
    firsts_all = plane(P_FIRST, lambda peer: c.flp.at[b], c.flp.at[b])
    second_relay()
    arrive(grads_in)
    arrive(final_in)
    arrive(firsts_all)
    c.fl[...] = total_of(c.flp, slice(None), B)
    arrive(feats_all)
    second_wait()
    for cp in sent:
        cp.wait_send()
    when_owner(lambda: [cp.wait_send() for cp in owner_sent] and None)


FINISH_NAMES = (
    ["f", "ff", "final", "grads", "fl"]
    + ["o_final", "o_grads", "feats", "w2", "win", "wst", "bin", "bst", "w1", "b1", "b2"]
    + ["hf", "hff", "hgrads", "hfl", "wide", "turn", "sems"]
)


def finish(s, *refs):
    c = SimpleNamespace(**dict(zip(FINISH_NAMES, refs)))
    H, J = s.H, s.J
    pairs = [(c.f, c.hf), (c.ff, c.hff), (c.grads, c.hgrads), (c.final, c.o_final)]
    pairs.append((c.fl, c.hfl))
    copies = [pltpu.make_async_copy(x, y, c.sems.at[k]) for k, (x, y) in enumerate(pairs)]
    for cp in copies:
        cp.start()
    copies[0].wait()
    c.wide[...] = c.hf[0 : s.R].reshape(H * J, H).astype(F32)
    for i in range(J):
        c.w2[:, i * H : (i + 1) * H] = c.wide[pl.ds(i, H, stride=J), :].T
    small = c.hf[s.R].reshape(SMALL_ROWS, H).astype(F32)
    for k in range(3):
        cut = slice(k * H, (k + 1) * H)
        c.win[:, cut] = small[k * H : (k + 1) * H]
        c.wst[:, cut] = small[ROW_STATE_WEIGHT + k * H : ROW_STATE_WEIGHT + (k + 1) * H]
    c.bin[...] = small[ROW_INPUT_BIAS : ROW_INPUT_BIAS + 3]
    c.bst[...] = small[ROW_STATE_BIAS : ROW_STATE_BIAS + 3]
    copies[4].wait()
    c.w1[...] = c.hfl[0:16]
    c.b1[...] = c.hfl[16:17]
    c.turn[...] = small[ROW_SECOND_BIAS : ROW_SECOND_BIAS + H].T
    r = lax.axis_index("rep")
    c.b2[...] = c.turn[pl.ds(pl.multiple_of(r * J, J), J), :]
    copies[1].wait()
    c.feats[...] = c.hff[...].astype(F32)
    copies[2].wait()
    c.o_grads[...] = c.hgrads[...].astype(F32)
    copies[3].wait()


def body(
    s,
    node_states,
    edge_feats,
    edge_source,
    edge_target,
    edge_group,
    column_mask,
    edge_count,
    first_weight,
    first_bias,
    second_weight,
    second_bias,
    update_input_weight,
    update_state_weight,
    update_input_bias,
    update_state_bias,
    state_cotangent,
):
    H, N, E = s.H, s.N, s.E
    shapes = scratch(s)
    names = ["in_" + k for k in IN_NAMES] + OUT_NAMES + IN_NAMES + list(shapes)
    sds = jax.ShapeDtypeStruct
    hbm = pl.BlockSpec(memory_space=pl.ANY)
    operands = (
        node_states,
        edge_feats.T,
        edge_source.reshape(1, E),
        edge_target.reshape(1, E),
        edge_group.reshape(1, E),
        column_mask,
        edge_count.reshape(1, 1),
        first_weight,
        first_bias.reshape(1, H),
        second_weight,
        second_bias.reshape(s.J, H),
        update_input_weight,
        update_state_weight,
        update_input_bias.reshape(3, H),
        update_state_bias.reshape(3, H),
        state_cotangent,
    )
    held = [
        pltpu.VMEM((8, 128) if name == "w2" else x.shape, F32 if name == "w2" else x.dtype)
        for name, x in zip(IN_NAMES, operands)
    ]
    final, grads, ff, f, fl = pl.pallas_call(
        functools.partial(whole, s, names),
        out_shape=[
            sds((N, H), F32),
            sds((N, H), BF16),
            sds((16, E), BF16),
            sds((s.R + 1, s.OW, s.T * s.J, H), BF16),
            sds((FIRST_ROWS, H), F32),
        ],
        in_specs=[hbm] * 16,
        out_specs=[VMEM] * 5,
        scratch_shapes=held + list(shapes.values()),
        compiler_params=pltpu.CompilerParams(
            collective_id=0, has_side_effects=True, vmem_limit_bytes=63 * 2**20
        ),
        name="edge_network",
    )(*operands)
    final, grads, feats, w2, win, wst, bin_, bst, w1, b1, b2 = pl.pallas_call(
        functools.partial(finish, s),
        out_shape=[
            sds((N, H), F32),
            sds((N, H), F32),
            sds((16, E), F32),
            sds((H, s.J * H), F32),
            sds((H, 3 * H), F32),
            sds((H, 3 * H), F32),
            sds((3, H), F32),
            sds((3, H), F32),
            sds((16, H), F32),
            sds((1, H), F32),
            sds((s.J, H), F32),
        ],
        in_specs=[hbm] * 5,
        out_specs=[VMEM] * 11,
        scratch_shapes=[
            pltpu.VMEM((s.R + 1, s.OW, s.T * s.J, H), BF16),
            pltpu.VMEM((16, E), BF16),
            pltpu.VMEM((N, H), BF16),
            pltpu.VMEM((FIRST_ROWS, H), F32),
            pltpu.VMEM((H * s.J, H), F32),
            pltpu.VMEM((H, H), F32),
            pltpu.SemaphoreType.DMA((5,)),
        ],
        compiler_params=pltpu.CompilerParams(vmem_limit_bytes=60 * 2**20),
        name="finish",
    )(f, ff, final, grads, fl)
    return (
        final,
        grads,
        feats.T,
        w1,
        b1.reshape(-1),
        w2,
        b2.reshape(-1),
        win,
        wst,
        bin_.reshape(-1),
        bst.reshape(-1),
    )


def solution(mesh):
    in_specs = (
        P("blk", None),
        P("blk", None),
        P("blk"),
        P("blk"),
        P("blk"),
        P(),
        P("blk"),
        P(),
        P(),
        P(None, "rep"),
        P("rep"),
        P(),
        P(),
        P(),
        P(),
        P("blk", None),
    )
    out_specs = (
        P("blk", None),
        P("blk", None),
        P("blk", None),
        P(),
        P(),
        P(None, "rep"),
        P("rep"),
        P(),
        P(),
        P(),
        P(),
    )

    def run(*args):
        nodes, edges, width = args[0].shape[0], args[2].shape[0], args[0].shape[1]
        return body(sizes(mesh, edges, nodes, width), *args)

    return jax.shard_map(run, mesh=mesh, in_specs=in_specs, out_specs=out_specs, check_vma=False)
```

```python
import functools
from types import SimpleNamespace

import jax
import jax.numpy as jnp
from jax import lax
from jax.experimental import pallas as pl
from jax.experimental.pallas import tpu as pltpu
from jax.sharding import PartitionSpec as P

STEPS = 2
TILE = 512
LO = 256
ROWS = 512
SLAB = 32
VISITS = (22, 34)
NEAR = 2
F32, BF16, I32 = jnp.float32, jnp.bfloat16, jnp.int32
MESH = pl.DeviceIdType.MESH
VMEM = pl.BlockSpec(memory_space=pltpu.VMEM)

ROW_STATE_WEIGHT = 384
ROW_INPUT_BIAS = 768
ROW_STATE_BIAS = 776
GROUP = 16
FIRST_ROWS = 32
ROW_SECOND_BIAS = 896
SMALL_ROWS = 1024

(
    P_STATE,
    P_STATE2,
    P_WEIGHT,
    P_WEIGHT_PAIR,
    P_SPREAD,
    P_SPREAD2,
    P_GRAD_PAIR,
    P_GRAD,
    P_SMALL,
    P_FIRST,
    P_GRAD_ALL,
    P_GRAD_ALL_PAIR,
    PLANES,
) = range(13)
(
    Z_WEIGHT,
    Z_BIAS,
    Z_SUM,
    Z_SUM2,
    Z_STATE,
    Z_FINAL,
    Z_DELTA,
    Z_DELTA2,
    Z_SOURCE,
    Z_SOURCE2,
    Z_GRADS,
    Z_FEATS,
    Z_FEATS_ALL,
    Z_SECOND,
    Z_SMALL,
    Z_FIRST,
    LINES,
) = range(17)


def nn(a, b):
    return jnp.dot(a, b, preferred_element_type=F32)


def nt(a, b):
    return lax.dot_general(a, b, (((1,), (1,)), ((), ())), preferred_element_type=F32)


def iota(shape, dim):
    return lax.broadcasted_iota(I32, shape, dim)


def ones_where(condition):
    return jnp.where(condition, 1.0, 0.0).astype(BF16)


def eye(n):
    return ones_where(iota((n, n), 0) == iota((n, n), 1))


def two(x):
    high = x.astype(BF16)
    return high, (x - high.astype(F32)).astype(BF16)


def three(x):
    high, rest = x.astype(BF16), x
    rest = x - high.astype(F32)
    mid = rest.astype(BF16)
    return high, mid, (rest - mid.astype(F32)).astype(BF16)


def nn2(a, x):
    high, low = two(x)
    return nn(a, high) + nn(a, low)


def nt2(x, b):
    high, low = two(x)
    return nt(high, b) + nt(low, b)


def sizes(mesh, edges, nodes, width):
    s = SimpleNamespace()
    s.B, s.R = mesh.shape["blk"], mesh.shape["rep"]
    s.E, s.N, s.H = edges, nodes, width
    s.J = width // s.R
    s.HIB = nodes // LO
    s.HI = s.HIB * s.B
    s.NQ = nodes // s.R
    s.EQ = edges // s.R
    s.OW = min(s.B, 8)
    s.STRIDE = s.B // s.OW
    s.T = s.J // s.OW
    s.KEEP = s.B <= 8
    s.SMALL = SMALL_ROWS // s.OW
    s.C = s.B // 2
    s.G = nodes // GROUP
    s.V = s.G + edges // LO
    return s


def scratch(s):
    v = pltpu.VMEM
    jh = s.J * s.H
    shapes = dict(
        nst=v((s.H, s.N), F32),
        stq=v((STEPS, s.HIB, s.J, LO), BF16),
        tab=v((STEPS, s.B, s.HIB, s.J, LO), BF16),
        ys=v((s.R * s.T, s.J, s.H), F32),
        wsend=v((s.R, s.T, s.J, s.H), BF16),
        w2r=v((s.J, s.H, s.H), BF16),
        b2f=v((s.H, s.H), F32),
        baug=v((s.J, s.H, s.H), BF16),
        w2k=v((s.H, jh), BF16),
        tl=v((1, s.E), I32),
        ohln=v((s.E, LO), BF16),
        mt=v((32, s.E), BF16),
        gm=v((16, s.E), BF16),
        ht=v((s.E // LO, s.H, LO), BF16),
        tlc=v((s.E // LO, 1, LO), I32),
        st=v((STEPS, s.J, s.E), BF16),
        sf=v((s.J, s.E), F32),
        sc=v((s.E // LO, s.J, LO), BF16),
        ge=v((s.H, s.E), BF16),
        smt=v((2 * s.H + s.J, s.N), F32),
        ssum=v((STEPS, s.J, s.N), F32),
        rsq=v((s.R, s.H, s.NQ), F32),
        rsl=v((STEPS, s.R, s.H, s.NQ), F32),
        keep=v((STEPS, 5, s.NQ, s.H), F32),
        keept=v((STEPS, 2, s.H, s.NQ), BF16),
        nsq=v((s.H, s.NQ), BF16),
        fin=v((s.NQ, s.H), F32),
        gq=v((STEPS, s.NQ // GROUP, GROUP, s.H), BF16),
        gfull=v((STEPS, s.G, GROUP, s.H), BF16),
        hg=v((s.H, s.E), F32),
        gacc=v((jh, s.H), F32),
        xs=v((ROWS, TILE), BF16),
        scat=v((s.HI * s.J, LO), F32),
        rps=v((s.B, s.HIB * s.J, LO), BF16),
        rpl=v((STEPS, s.B, s.HIB * s.J, LO), BF16),
        fzs=v((STEPS, s.R, s.J, s.NQ), F32),
        fzl=v((STEPS, s.R, s.J, s.NQ), F32),
        gradq=v((s.NQ, s.H), F32),
        gradl=v((s.NQ, s.H), BF16),
        small=v((SMALL_ROWS, s.H), F32),
        q0=v((s.V, s.J * GROUP, s.H), BF16),
        gv=v((s.V * GROUP, s.H), BF16),
        planv=v((8, 128), I32),
        plan=pltpu.SMEM((8, 128), I32),
        firsts=v((FIRST_ROWS, s.H), F32),
        flz=v((s.R, FIRST_ROWS, s.H), F32),
        flp=v((s.B, FIRST_ROWS, s.H), F32),
        sgsend=v((SMALL_ROWS, s.H), BF16),
        sgland=v((s.B, s.SMALL, s.H), BF16),
        gz=v((s.R, s.T * s.J, s.H), BF16),
        sgz=v((s.R, s.SMALL, s.H), BF16),
        fqs=v((16, s.E), BF16),
        fql=v((s.R, 16, s.EQ), BF16),
        ps=pltpu.SemaphoreType.DMA((PLANES, s.B)),
        pr=pltpu.SemaphoreType.DMA((PLANES, s.B)),
        zs=pltpu.SemaphoreType.DMA((LINES, s.R)),
        zr=pltpu.SemaphoreType.DMA((LINES, s.R)),
        local=pltpu.SemaphoreType.DMA,
        ins=pltpu.SemaphoreType.DMA((len(IN_NAMES),)),
    )
    piece = (jh // s.OW, s.H)
    if s.STRIDE > 1:
        shapes["gland"] = v((s.B,) + piece, BF16)
        shapes["gsend"] = v((jh, s.H), BF16)
    if s.KEEP:
        shapes["mat"] = v((jh, s.E), BF16)
        shapes["sums"] = v((2, s.J, jh // 4), BF16)
    return shapes


IN_NAMES = (
    ["nodes", "feats", "src", "tgt", "grp", "cmask", "count", "w1", "b1"]
    + ["w2", "b2", "win", "wst", "bin", "bst", "cot"]
)
OUT_NAMES = ["final", "grads", "ff", "f", "fl"]


def whole(s, names, *refs):
    c = SimpleNamespace(**dict(zip(names, refs)))
    B, R, H, J, E, N, NQ, EQ = s.B, s.R, s.H, s.J, s.E, s.N, s.NQ, s.EQ
    T, OW, STRIDE = s.T, s.OW, s.STRIDE
    jh = J * H
    tiles = E // TILE
    b = lax.axis_index("blk")
    r = lax.axis_index("rep")
    owner = b // STRIDE
    is_owner = lax.rem(b, STRIDE) == 0
    sent = []

    def push(src, dst, sems, rems, axis, peer):
        return pltpu.make_async_remote_copy(
            src_ref=src,
            dst_ref=dst,
            send_sem=sems,
            recv_sem=rems,
            device_id={axis: peer},
            device_id_type=MESH,
        )

    def plane(x, src_of, dst):
        copies = []
        for d in range(1, B):
            peer = lax.rem(b + d, B)
            cp = push(src_of(peer), dst, c.ps.at[x, d], c.pr.at[x, d], "blk", peer)
            cp.start()
            copies.append(cp)
        sent.extend(copies)
        return copies

    def line(x, src_of, dst):
        copies = []
        for d in range(1, R):
            peer = lax.rem(r + d, R)
            cp = push(src_of(peer), dst, c.zs.at[x, d], c.zr.at[x, d], "rep", peer)
            cp.start()
            copies.append(cp)
        sent.extend(copies)
        return copies

    def arrive(copies, reuse=False):
        for cp in copies:
            cp.wait_recv()
        if reuse:
            release(copies)

    def release(copies):
        for cp in copies:
            cp.wait_send()
            sent[:] = [other for other in sent if other is not cp]

    def when_owner(fn):
        if STRIDE == 1:
            fn()
        else:
            pl.when(is_owner)(fn)

    def line_owner(x, src_of, dst):
        copies = []
        for d in range(1, R):
            peer = lax.rem(r + d, R)
            copies.append(push(src_of(peer), dst, c.zs.at[x, d], c.zr.at[x, d], "rep", peer))
        when_owner(lambda: [cp.start() for cp in copies] and None)
        owner_sent.extend(copies)
        return copies

    owner_sent = []

    def from_owners(x, strip_of):
        copies = []
        for d in range(1, B):
            peer = lax.rem(b + d, B)
            strip = strip_of(owner)
            copies.append(push(strip, strip, c.ps.at[x, d], c.pr.at[x, owner], "blk", peer))
        when_owner(lambda: [cp.start() for cp in copies] and None)
        owner_sent.extend(copies)

        def wait():
            for q in range(OW):

                @pl.when(b != q * STRIDE)
                def _():
                    strip = strip_of(q)
                    peer = lax.rem(b + 1, B)
                    push(strip, strip, c.ps.at[x, 0], c.pr.at[x, q], "blk", peer).wait_recv()

        return lambda: None, wait, [], []

    chip, core = b // 2, lax.rem(b, 2)

    column, line_of = lax.rem(chip, 2), chip // 2
    lines = max(s.C // 2, 1)

    def device(m, its_core, back=False):
        up = lines - m // 2 if back else m // 2
        return 2 * (2 * lax.rem(line_of + up, lines) + lax.rem(column + lax.rem(m, 2), 2)) + its_core

    def slot_rows(at):
        if STRIDE > 1:
            return at
        slot = at // T
        held_by = jnp.where(slot < s.C, core, 1 - core)
        return T * device(lax.rem(slot, s.C), held_by, True) + lax.rem(at, T)

    def slot(k):
        return c.w2r.at[k * T : (k + 1) * T]

    def gather_pairs(x, x2, first_of, then_of, late=s.C):
        first, then = [], []
        for m in range(1, s.C):
            src, dst = first_of(m)
            first.append(push(src, dst, c.ps.at[x, m], c.pr.at[x, m], "blk", device(m, core)))
        for m in range(s.C):
            src, dst = then_of(m)
            then.append(
                push(src, dst, c.ps.at[x2, m], c.pr.at[x2, m], "blk", device(0, 1 - core))
            )
        for cp in first[:late] + then[:1]:
            cp.start()

        def relay(begin=1, end=s.C):
            for m in range(begin, end):
                first[m - 1].wait_recv()
                then[m].start()

        def wait():
            arrive(then)

        sent.extend(first + then)
        return relay, wait, first, then

    def to_owners(x, src_of, dst):
        if STRIDE == 1:
            copies = plane(x, src_of, dst)
            return lambda: arrive(copies)
        for q in range(OW):

            @pl.when(b != q * STRIDE)
            def _():
                push(src_of(q), dst, c.ps.at[x, q], c.pr.at[x, b], "blk", q * STRIDE).start()

        def wait():
            def arrivals():
                for d in range(1, B):
                    peer = lax.rem(b + d, B)
                    push(src_of(0), dst, c.ps.at[x, 0], c.pr.at[x, peer], "blk", peer).wait_recv()

            when_owner(arrivals)
            for q in range(OW):

                @pl.when(b != q * STRIDE)
                def _():
                    push(src_of(q), dst, c.ps.at[x, q], c.pr.at[x, b], "blk", q * STRIDE).wait_send()

        return wait

    def edges(t):
        return pl.ds(pl.multiple_of(t * TILE, TILE), TILE)

    barrier = pltpu.get_barrier_semaphore()
    for d in range(1, B):
        pl.semaphore_signal(
            barrier, inc=1, device_id={"blk": lax.rem(b + d, B)}, device_id_type=MESH
        )
    for d in range(1, R):
        pl.semaphore_signal(
            barrier, inc=1, device_id={"rep": lax.rem(r + d, R)}, device_id_type=MESH
        )

    loads = {}
    for k, name in enumerate(IN_NAMES):
        to = c.w2k if name == "w2" else getattr(c, name)
        loads[name] = pltpu.make_async_copy(getattr(c, "in_" + name), to, c.ins.at[k])
    for name in ["nodes", "w2"]:
        loads[name].start()
    for name in IN_NAMES:
        if name not in ("nodes", "w2"):
            loads[name].start()
    eye_h = eye(H)
    part = pl.ds(pl.multiple_of(r * J, J), J)

    loads["nodes"].wait()
    c.nst[...] = c.nodes[...].T
    own_columns = c.nst[part, :].astype(BF16)
    for k in range(s.HIB):
        c.stq[0, k] = own_columns[:, k * LO : (k + 1) * LO]
    c.tab[0, b] = c.stq[0]
    row = iota((R * T, H), 0)
    pick = ones_where(iota((R * T, H), 1) == (row // T) * J + T * owner + lax.rem(row, T))
    loads["w2"].wait()
    for i in range(J):
        c.ys[:, i, :] = nt(pick, c.w2k[:, i * H : (i + 1) * H])
    c.wsend[...] = c.ys[...].astype(BF16).reshape(R, T, J, H)
    for name in IN_NAMES:
        if name not in ("nodes", "w2"):
            loads[name].wait()
    pl.semaphore_wait(barrier, B - 1 + R - 1)

    states_in = plane(P_STATE, lambda peer: c.stq.at[0], c.tab.at[0, b])
    strip = pl.ds(0 if STRIDE == 1 else pl.multiple_of(T * owner, T), T)
    weight_in = line_owner(Z_WEIGHT, lambda peer: c.wsend.at[peer], c.w2r.at[strip, part, :])
    c.b2f[part, :] = c.b2[...]
    bias_in = line(Z_BIAS, lambda peer: c.b2, c.b2f.at[part, :])

    def own_strip():
        c.w2r[strip, part, :] = c.wsend[r]

    when_owner(own_strip)

    place = iota((1, E), 1)
    c.tl[...] = jnp.where(place < c.count[...], c.tgt[...] - b * N, -1)
    for k in range(E // LO):
        c.tlc[k] = c.tl[:, k * LO : (k + 1) * LO]
    ends = jnp.where(c.tgt[...] - b * N < GROUP * (iota((s.G, E), 0) + 1), 1, 0)
    ends = jnp.sum(ends, axis=1, keepdims=True)
    left_in = jnp.maximum((ends + (LO - 1)) // LO - 1, 0)
    group = iota((s.G, 128), 0)
    leave = group + jnp.where(group == s.G - 1, E // LO - 1, left_in)
    visited = jnp.sum(jnp.where(leave < iota((s.G, 128), 1), 1, 0), axis=0, keepdims=True)
    c.planv[...] = jnp.broadcast_to(visited, (8, 128))
    plan_copy = pltpu.make_async_copy(c.planv, c.plan, c.local)
    plan_copy.start()
    cmt = nt(eye(16), c.cmask[...].astype(F32).astype(BF16)).astype(BF16)
    b1 = three(c.b1[...])
    first = jnp.concatenate(
        [c.w1[...].astype(F32)] + [x.astype(F32) for x in b1] + [jnp.zeros((13, H), F32)], axis=0
    ).astype(BF16)
    w1ta = nt(eye_h, first).astype(BF16)
    eye_t = eye(LO)

    def target_rows(t):
        return ones_where(iota((N, TILE), 0) == c.tl[:, edges(t)])

    def low_rows(t):
        return ones_where(iota((LO, TILE), 0) == (c.src[:, edges(t)] & (LO - 1)))

    per_tile = TILE // LO

    def put(ref, t, value):
        for k in range(per_tile):
            ref[t * per_tile + k] = value[:, k * LO : (k + 1) * LO]

    def hidden_of(t):
        return jnp.concatenate([c.ht[t * per_tile + k] for k in range(per_tile)], axis=1)

    def prepare(t, carry):
        e = edges(t)
        groups = ones_where(iota((16, TILE), 0) == c.grp[:, e])
        gm = nn(cmt, groups)
        c.gm[:, e] = gm.astype(BF16)
        masked = c.feats[:, e].astype(F32) * gm
        ones = jnp.where(iota((16, TILE), 0) < 3, 1.0, 0.0)
        mt = jnp.concatenate([masked, ones], axis=0).astype(BF16)
        c.mt[:, e] = mt
        pre = nn(w1ta, mt)
        hidden = (pre * jax.nn.sigmoid(pre)).astype(BF16)
        put(c.ht, t, hidden)
        lows = low_rows(t)
        for k in range(TILE // LO):
            rows = pl.ds(pl.multiple_of(t * TILE + k * LO, LO), LO)
            c.ohln[rows, :] = nt(eye_t, lows[:, k * LO : (k + 1) * LO]).astype(BF16)
        return carry

    lax.fori_loop(0, tiles, prepare, 0)

    when_owner(lambda: arrive(weight_in))
    if STRIDE == 1:
        weight_relay, weight_wait, weight_chip, weight_pair = gather_pairs(
            P_WEIGHT,
            P_WEIGHT_PAIR,
            lambda m: (slot(0), slot(m)),
            lambda m: (slot(m), slot(s.C + m)),
        )
    else:
        weight_relay, weight_wait, weight_chip, weight_pair = from_owners(
            P_WEIGHT, lambda q: c.w2r.at[pl.ds(pl.multiple_of(T * q, T), T)]
        )

    to_slots = ones_where(iota((J, J), 1) == slot_rows(iota((J, J), 0)))
    from_slots = ones_where(iota((J, J), 0) == slot_rows(iota((J, J), 1)))

    def gather(step):
        if STRIDE == 1:
            for q in range(B):
                for k in range(s.HIB):
                    c.tab[step, q, k] = nn(to_slots, c.tab[step, q, k]).astype(BF16)

        def one(t, carry):
            e = edges(t)
            lows = low_rows(t)
            high = c.src[:, e] // LO
            total = jnp.zeros((J, TILE), F32)
            per = ROWS // J
            for g in range(s.HI // per):
                blocks = per // s.HIB
                table = c.tab[step, g * blocks : (g + 1) * blocks].reshape(ROWS, LO)
                rows = nn(table, lows)
                for k in range(per):
                    total = total + jnp.where(high == g * per + k, rows[k * J : (k + 1) * J], 0.0)
            c.st[step, :, e] = total.astype(BF16)
            c.sf[:, e] = total
            if step == 0:
                put(c.sc, t, total.astype(BF16))
            return carry

        lax.fori_loop(0, tiles, one, 0, unroll=2)

    arrive(states_in)
    gather(0)
    arrive(bias_in)
    b2 = jnp.concatenate(three(c.b2f[...]), axis=1)

    def bias_columns(j, carry):
        at = iota((3 * H, H), 0)
        to = iota((3 * H, H), 1)
        move = ones_where((lax.rem(at, H) == r * J + slot_rows(j)) & (to == at // H))
        c.baug[j] = nn(b2, move).astype(BF16)
        return carry

    lax.fori_loop(0, J, bias_columns, 0, unroll=8)

    def turned(j, carry):
        c.w2k[:, pl.ds(pl.multiple_of(j * H, H), H)] = nt(eye_h, c.w2r[j]).astype(BF16)
        return carry

    chunk = ROWS // H

    def hidden_rows(t):
        ones = jnp.where(iota((H, TILE), 0) < 3, 1.0, 0.0).astype(BF16)
        return jnp.concatenate([hidden_of(t), ones], axis=0)

    def held_messages(t):
        e = edges(t)
        parts = []
        for k in range(H // SLAB):
            total = jnp.zeros((SLAB, TILE), F32)
            for j in range(J):
                at = j * H + k * SLAB
                total = total + c.mat[at : at + SLAB, e].astype(F32) * c.sf[j : j + 1, e]
            parts.append(total)
        return jnp.concatenate(parts, axis=0)

    half, few = J // 2, H // 2
    if s.KEEP:
        rows, columns = iota((J, half * few), 0), iota((J, half * few), 1) // few
        for k in range(2):
            c.sums[k] = ones_where(rows == slot_rows(columns + k * half))

    def held_sources(e):
        grads = c.ge[:, e]
        total = jnp.zeros((J, TILE), F32)
        for k in range(2):
            held = c.mat[k * half * H : (k + 1) * half * H, e].reshape(half, H, TILE)
            product = held * grads[None]
            product = product[:, :few] + product[:, few:]
            total = total + nn(c.sums[k], product.reshape(half * few, TILE))
        return total

    def matrices(k, e, hidden):
        cut = slice(k * chunk, (k + 1) * chunk)
        left = jnp.concatenate(
            [c.w2r[cut].reshape(ROWS, H), c.baug[cut].reshape(ROWS, H)], axis=1
        )
        return nn(left, hidden).astype(BF16).astype(F32)

    def first_pass(strips, start):
        def one(t, carry):
            e = edges(t)
            hidden = hidden_rows(t)
            total = jnp.zeros((H, TILE), F32) if start else c.hg[:, e]
            for q in strips:
                cut = slice(q * T, (q + 1) * T)
                left = jnp.concatenate(
                    [c.w2r[cut].reshape(T * H, H), c.baug[cut].reshape(T * H, H)], axis=1
                )
                low = nn(left, hidden).astype(BF16)
                c.mat[q * T * H : (q + 1) * T * H, e] = low
                m = low.astype(F32)
                for p in range(T):
                    total = total + m[p * H : (p + 1) * H] * c.sf[q * T + p : q * T + p + 1, e]
            c.hg[:, e] = total
            return carry

        lax.fori_loop(0, tiles, one, 0, unroll=4 if len(strips) < 3 else 2)

    def messages(step):
        c.smt[...] = jnp.zeros_like(c.smt)

        def one(t, carry):
            e = edges(t)
            low = c.st[step, :, e]
            if s.KEEP:
                total = held_messages(t) if step > 0 else c.hg[:, e]
            else:
                source = low.astype(F32)
                hidden = hidden_rows(t)
                total = jnp.zeros((H, TILE), F32)
                for k in range(J // chunk):
                    m = matrices(k, e, hidden)
                    for q in range(chunk):
                        j = k * chunk + q
                        total = total + m[q * H : (q + 1) * H] * source[j : j + 1, :]
            high, rest = two(total)
            rows = jnp.concatenate([high, rest, low], axis=0)
            c.smt[...] += nt(rows, target_rows(t))
            return carry

        lax.fori_loop(0, tiles, one, 0, unroll=2)
        summed = c.smt[0:H, :] + c.smt[H : 2 * H, :]
        c.ssum[step] = c.smt[2 * H : 2 * H + J, :]
        for q in range(R):
            c.rsq[q] = summed[:, q * NQ : (q + 1) * NQ]
        c.rsl[step, r] = c.rsq[r]
        return line(Z_SUM + step, lambda peer: c.rsq.at[peer], c.rsl.at[step, r])

    def gate_bias(ref):
        return jnp.concatenate([ref[k : k + 1, :] for k in range(3)], axis=1)

    def gates(step, before, before_t):
        summed = c.rsl[step, 0]
        for q in range(1, R):
            summed = summed + c.rsl[step, q]
        summed_low = summed.T.astype(BF16)
        gi = nn(summed_low, c.win[...]) + gate_bias(c.bin)
        gs = nn(before.astype(BF16), c.wst[...]) + gate_bias(c.bst)
        reset = jax.nn.sigmoid(gi[:, :H] + gs[:, :H])
        update = jax.nn.sigmoid(gi[:, H : 2 * H] + gs[:, H : 2 * H])
        state_part = gs[:, 2 * H :]
        candidate = jnp.tanh(gi[:, 2 * H :] + reset * state_part)
        for k, x in enumerate((before, reset, update, candidate, state_part)):
            c.keep[step, k] = x
        c.keept[step, 0] = summed.astype(BF16)
        c.keept[step, 1] = before_t
        return (1.0 - update) * candidate + update * before

    def products(begin, end):
        def one(t, carry):
            g = c.plan[0, t]
            ch = t - g
            mine = ones_where(iota((GROUP, LO), 0) + g * GROUP == c.tlc[ch])
            source = c.sc[ch].astype(F32)
            parts = []
            for j in range(J):
                row = jnp.broadcast_to(source[j : j + 1, :], (GROUP, LO)).astype(BF16)
                parts.append(row * mine)
            c.q0[t] = nt(jnp.concatenate(parts, axis=0), c.ht[ch]).astype(BF16)
            return carry

        lax.fori_loop(begin, end, one, 0)

    plan_copy.wait()
    nodes_here = pl.ds(pl.multiple_of(r * NQ, NQ), NQ)
    groups_here = pl.ds(pl.multiple_of(r * (NQ // GROUP), NQ // GROUP), NQ // GROUP)
    if s.KEEP:
        near = NEAR + 1
        first_pass([0], True)
        weight_relay()
        first_pass(range(1, s.C), False)
        arrive(weight_pair)
        first_pass(range(s.C, OW), False)
    else:
        weight_wait()
    sums = messages(0)
    lax.fori_loop(0, J, turned, 0, unroll=8)
    products(0, VISITS[0])
    arrive(sums, reuse=True)
    release(weight_chip + weight_pair)
    state = gates(0, c.nodes[nodes_here, :], c.nst[:, nodes_here].astype(BF16))
    state_t = state.T.astype(BF16)
    c.nsq[...] = state_t
    hib = r // (LO // NQ)
    lanes = pl.ds(pl.multiple_of(lax.rem(r, LO // NQ) * NQ, NQ), NQ)
    c.stq[1, hib, :, lanes] = c.nsq[part, :]
    pieces = line(
        Z_STATE,
        lambda peer: c.nsq.at[pl.ds(pl.multiple_of(peer * J, J), J), :],
        c.stq.at[1, hib, :, lanes],
    )
    products(VISITS[0], VISITS[1])
    arrive(pieces)
    c.tab[1, b] = c.stq[1]
    states_in = plane(P_STATE2, lambda peer: c.stq.at[1], c.tab.at[1, b])
    products(VISITS[1], s.V)
    arrive(states_in)
    gather(1)
    sums = messages(1)
    arrive(sums)
    final = gates(1, state, state_t)
    c.fin[...] = final
    c.final[nodes_here, :] = final

    c.small[...] = jnp.zeros_like(c.small)
    c.gacc[...] = jnp.zeros_like(c.gacc)

    def deltas(step, grad):
        before, reset, update, candidate, state_part = [c.keep[step, k] for k in range(5)]
        dn = grad * (1.0 - update)
        dz = grad * (before - candidate)
        dpn = dn * (1.0 - candidate * candidate)
        dpz = dz * update * (1.0 - update)
        dpr = dpn * state_part * reset * (1.0 - reset)
        to_input = jnp.concatenate([dpr, dpz, dpn], axis=1)
        to_state = jnp.concatenate([dpr, dpz, dpn * reset], axis=1)
        summed_grad = nt2(to_input, c.win[...]).astype(BF16)
        c.gq[step] = summed_grad.reshape(NQ // GROUP, GROUP, H)
        c.gfull[step, groups_here] = c.gq[step]
        copies = line(Z_DELTA + step, lambda peer: c.gq.at[step], c.gfull.at[step, groups_here])
        gwi = nn2(c.keept[step, 0], to_input)
        gws = nn2(c.keept[step, 1], to_state)
        gbi = jnp.sum(to_input, axis=0, keepdims=True)
        gbs = jnp.sum(to_state, axis=0, keepdims=True)
        for k in range(3):
            cut = slice(k * H, (k + 1) * H)
            c.small[k * H : (k + 1) * H, :] += gwi[:, cut]
            c.small[ROW_STATE_WEIGHT + k * H : ROW_STATE_WEIGHT + (k + 1) * H, :] += gws[:, cut]
            c.small[ROW_INPUT_BIAS + k : ROW_INPUT_BIAS + k + 1, :] += gbi[:, cut]
            c.small[ROW_STATE_BIAS + k : ROW_STATE_BIAS + k + 1, :] += gbs[:, cut]
        c.gradq[...] = grad * update + nt2(to_state, c.wst[...])
        return copies

    def node_grads(step):
        held = c.gfull[step].reshape(N, H)
        gt = nt(eye_h, held).astype(BF16)

        def one(t, carry):
            c.ge[:, edges(t)] = nn(gt, target_rows(t)).astype(BF16)
            return carry

        lax.fori_loop(0, tiles, one, 0, unroll=2)
    def second_bias_grads(step):
        held = c.gfull[step].reshape(N, H)
        rows = pl.ds(ROW_SECOND_BIAS + pl.multiple_of(r * J, J), J)
        high, low = [nn(from_slots, x).astype(BF16) for x in two(c.ssum[step])]
        c.small[rows, :] += nn(high, held) + nn(low, held)

    def weights_tile(step, t, second):
        e = edges(t)
        at_edges = c.ge[:, e]
        source = c.st[step, :, e].astype(F32)
        got = None if step == STEPS - 1 else c.hg[:, e]
        spread = at_edges.reshape(H // 16, 16, TILE)
        for k in range(jh // ROWS):
            parts = []
            for j in range(k * ROWS // H, (k + 1) * ROWS // H):
                row = jnp.broadcast_to(source[j : j + 1, :], (16, TILE)).astype(BF16)
                parts.append((spread * row[None]).reshape(H, TILE))
            outer = jnp.concatenate(parts, axis=0)
            rows = slice(k * ROWS, (k + 1) * ROWS)
            more = nn(c.w2k[:, rows], outer)
            got = more if got is None else got + more
            if second:
                c.gacc[rows, :] += nt(outer, hidden_of(t))
        c.hg[:, e] = got

    def weights(step, begin, end):
        def one(t, carry):
            weights_tile(step, t, step == STEPS - 1)
            return carry

        lax.fori_loop(begin, end, one, 0, unroll=2 if step == 0 else 1)

    def sources(step, begin, end):
        if begin == 0:
            c.scat[...] = jnp.zeros_like(c.scat)

        def one(t, carry):
            e = edges(t)
            if s.KEEP:
                got = held_sources(e)
            else:
                at_edges = c.ge[:, e].astype(F32)
                hidden = hidden_rows(t)
                parts = []
                for k in range(J // chunk):
                    m = matrices(k, e, hidden)
                    for q in range(chunk):
                        parts.append(
                            jnp.sum(m[q * H : (q + 1) * H] * at_edges, axis=0, keepdims=True)
                        )
                got = jnp.concatenate(parts, axis=0)
            high = c.src[:, e] // LO
            per = ROWS // J
            for g in range(s.HI // per):
                for k in range(per):
                    c.xs[k * J : (k + 1) * J, :] = jnp.where(high == g * per + k, got, 0.0).astype(
                        BF16
                    )
                c.scat[g * ROWS : (g + 1) * ROWS, :] += nn(c.xs[...], c.ohln[e, :])
            return carry

        lax.fori_loop(begin, end, one, 0)

    def spread_sources(step):
        c.rps[...] = c.scat[...].astype(BF16).reshape(B, s.HIB * J, LO)
        c.rpl[step, b] = c.rps[b]
        return plane(P_SPREAD + step, lambda peer: c.rps.at[peer], c.rpl.at[step, b])

    def share_sources(step):
        total = c.rpl[step, 0].astype(F32)
        for q in range(1, B):
            total = total + c.rpl[step, q].astype(F32)
        for q in range(R):
            k, lane = (q * NQ) // LO, (q * NQ) % LO
            c.fzs[step, q] = total[k * J : (k + 1) * J, lane : lane + NQ]
        c.fzl[step, r] = c.fzs[step, r]
        return line(Z_SOURCE + step, lambda peer: c.fzs.at[step, peer], c.fzl.at[step, r])

    def state_grad(step):
        return c.gradq[...] + c.fzl[step].reshape(H, NQ).T

    last = STEPS - 1
    copies = deltas(last, c.cot[nodes_here, :])
    arrive(copies)
    final_in = line(Z_FINAL, lambda peer: c.fin, c.final.at[nodes_here, :])
    node_grads(last)
    sources(last, 0, tiles)
    spread = spread_sources(last)
    second_bias_grads(last)
    weights(last, 0, 3)
    arrive(spread, reuse=True)
    pieces = share_sources(last)
    weights(last, 3, 5)
    arrive(pieces)
    copies = deltas(0, state_grad(last))
    weights(last, 5, tiles)
    arrive(copies)
    def group_rows(t, carry):
        rows = pl.ds(pl.multiple_of(t * GROUP, GROUP), GROUP)
        c.gv[rows, :] = c.gfull[0, jnp.minimum(c.plan[0, t], s.G - 1)]
        return carry

    lax.fori_loop(0, s.V, group_rows, 0, unroll=8)
    grads_t = nt(eye_h, c.gv[...]).astype(BF16)

    def second_weight_rows(k, carry):
        held = [
            c.q0[:, pl.ds(pl.multiple_of((2 * k + p) * GROUP, GROUP), GROUP), :] for p in range(2)
        ]
        held = [x.reshape(s.V * GROUP, H) for x in held]
        more = nn(grads_t, jnp.concatenate(held, axis=1))
        for p in range(2):
            rows = pl.ds(pl.multiple_of((2 * k + p) * H, H), H)
            c.gacc[rows, :] += more[:, p * H : (p + 1) * H]
        return carry

    lax.fori_loop(0, J // 2, second_weight_rows, 0, unroll=4)

    per_owner = jh // OW

    def grad_rows(q):
        return c.gacc[pl.ds(pl.multiple_of(q * per_owner, per_owner), per_owner), :]

    if STRIDE == 1:
        def piece_rows(k):
            return c.gacc[k * per_owner : (k + 1) * per_owner, :].reshape(T, H, H)

        def pieces_in(ref, k):
            return ref.at[k * T : (k + 1) * T]

        pair = []
        for m in range(s.C):
            c.baug[m * T : (m + 1) * T] = piece_rows(s.C + m).astype(BF16)
            x = P_GRAD_PAIR
            cp = push(
                pieces_in(c.baug, m),
                pieces_in(c.w2r, m),
                c.ps.at[x, m],
                c.pr.at[x, m],
                "blk",
                device(0, 1 - core),
            )
            cp.start()
            pair.append(cp)
        sent.extend(pair)
    else:
        c.gsend[...] = c.gacc[...].astype(BF16)

        def own_grads():
            c.gland[b] = grad_rows(owner).astype(BF16)

        when_owner(own_grads)
        grads_wait = to_owners(
            P_GRAD,
            lambda q: c.gsend.at[pl.ds(pl.multiple_of(q * per_owner, per_owner), per_owner), :],
            c.gland.at[b],
        )

    node_grads(0)
    second_bias_grads(0)

    c.sgsend[...] = c.small[...].astype(BF16)

    def small_rows(q):
        return pl.ds(pl.multiple_of(q * s.SMALL, s.SMALL), s.SMALL)

    def own_small():
        c.sgland[b] = c.sgsend[small_rows(owner), :]

    when_owner(own_small)
    small_wait = to_owners(P_SMALL, lambda q: c.sgsend.at[small_rows(q), :], c.sgland.at[b])

    if STRIDE == 1:
        across = []
        for m in list(range(1, s.C)) + [0]:
            if m == 1:
                arrive(pair)
            total = piece_rows(m) + c.w2r[m * T : (m + 1) * T].astype(F32)
            total = total.astype(BF16)
            if m == 0:
                c.w2r[s.C * T : (s.C + 1) * T] = total
                continue
            c.baug[(s.C + m) * T : (s.C + m + 1) * T] = total
            x = P_GRAD
            cp = push(
                pieces_in(c.baug, s.C + m),
                pieces_in(c.w2r, s.C + m),
                c.ps.at[x, m],
                c.pr.at[x, m],
                "blk",
                device(m, core, True),
            )
            cp.start()
            across.append(cp)
        sent.extend(across)

        def grads_wait():
            arrive(across)

    def total_of(ref, rows, count):
        total = ref[0, rows, :].astype(F32)
        for q in range(1, count):
            total = total + ref[q, rows, :].astype(F32)
        return total

    sources(0, 0, tiles)
    spread = spread_sources(0)
    small_wait()

    def reduce_small():
        c.sgz[r] = total_of(c.sgland, slice(None), B).astype(BF16)

    when_owner(reduce_small)
    small_in = line_owner(Z_SMALL, lambda peer: c.sgz.at[r], c.sgz.at[r])
    weights(0, 0, 2)
    grads_wait()

    def reduce_grads():
        for t in range(T):
            if STRIDE == 1:
                total = c.w2r[s.C * T + t].astype(F32)
                for q in range(1, s.C):
                    total = total + c.w2r[(s.C + q) * T + t].astype(F32)
            else:
                total = total_of(c.gland, slice(t * H, (t + 1) * H), B)
            total = total.astype(BF16)
            for q in range(R):
                c.gz[q, t * J : (t + 1) * J, :] = total[q * J : (q + 1) * J, :]
        c.f[r, owner] = c.gz[r]

    when_owner(reduce_grads)
    second_in = line_owner(Z_SECOND, lambda peer: c.gz.at[peer], c.f.at[r, owner])
    weights(0, 2, 6)
    arrive(spread)
    pieces = share_sources(0)
    weights(0, 6, tiles)

    def sum_small():
        arrive(small_in)
        c.f[R, owner] = total_of(c.sgz, slice(None), R).astype(BF16)
        arrive(second_in)

    when_owner(sum_small)
    if STRIDE == 1:

        def held_strip(m):
            strip = c.f.at[:, device(m, core, True)]
            return strip, strip

        second_relay, second_wait, _, _ = gather_pairs(
            P_GRAD_ALL, P_GRAD_ALL_PAIR, lambda m: held_strip(0), held_strip
        )
    else:
        second_relay, second_wait, _, _ = from_owners(P_GRAD_ALL, lambda q: c.f.at[:, q])

    arrive(pieces)
    grad = state_grad(0).astype(BF16)
    c.gradl[...] = grad
    c.grads[nodes_here, :] = grad
    grads_in = line(Z_GRADS, lambda peer: c.gradl, c.grads.at[nodes_here, :])

    w1 = c.w1[...]
    c.firsts[...] = jnp.zeros_like(c.firsts)

    def first_layer(t, carry):
        e = edges(t)
        mt = c.mt[:, e]
        pre = nn(w1ta, mt)
        gate = jax.nn.sigmoid(pre)
        pre_grad = c.hg[:, e] * gate * (1.0 + pre * (1.0 - gate))
        pre_grad = pre_grad.astype(BF16)
        c.fqs[:, e] = (nn(w1, pre_grad) * c.gm[:, e].astype(F32)).astype(BF16)
        c.firsts[...] += nt(mt, pre_grad)
        return carry

    lax.fori_loop(0, tiles, first_layer, 0, unroll=2)
    edges_here = pl.ds(pl.multiple_of(r * EQ, EQ), EQ)
    c.fql[r] = c.fqs[:, edges_here]
    feats_in = line(
        Z_FEATS,
        lambda peer: c.fqs.at[:, pl.ds(pl.multiple_of(peer * EQ, EQ), EQ)],
        c.fql.at[r],
    )
    c.flz[r] = c.firsts[...]
    firsts_in = line(Z_FIRST, lambda peer: c.firsts, c.flz.at[r])

    arrive(feats_in)
    c.ff[:, edges_here] = total_of(c.fql, slice(None), R).astype(BF16)
    feats_all = line(Z_FEATS_ALL, lambda peer: c.ff.at[:, edges_here], c.ff.at[:, edges_here])
    arrive(firsts_in)
    c.flp[b] = total_of(c.flz, slice(None), R)
    firsts_all = plane(P_FIRST, lambda peer: c.flp.at[b], c.flp.at[b])
    second_relay()
    arrive(grads_in)
    arrive(final_in)
    arrive(firsts_all)
    c.fl[...] = total_of(c.flp, slice(None), B)
    arrive(feats_all)
    second_wait()
    for cp in sent:
        cp.wait_send()
    when_owner(lambda: [cp.wait_send() for cp in owner_sent] and None)


FINISH_NAMES = (
    ["f", "ff", "final", "grads", "fl"]
    + ["o_final", "o_grads", "feats", "w2", "win", "wst", "bin", "bst", "w1", "b1", "b2"]
    + ["hf", "hff", "hgrads", "hfl", "wide", "turn", "sems"]
)


def finish(s, *refs):
    c = SimpleNamespace(**dict(zip(FINISH_NAMES, refs)))
    H, J = s.H, s.J
    pairs = [(c.f, c.hf), (c.ff, c.hff), (c.grads, c.hgrads), (c.final, c.o_final)]
    pairs.append((c.fl, c.hfl))
    copies = [pltpu.make_async_copy(x, y, c.sems.at[k]) for k, (x, y) in enumerate(pairs)]
    for cp in copies:
        cp.start()
    copies[0].wait()
    c.wide[...] = c.hf[0 : s.R].reshape(H * J, H).astype(F32)
    for i in range(J):
        c.w2[:, i * H : (i + 1) * H] = c.wide[pl.ds(i, H, stride=J), :].T
    small = c.hf[s.R].reshape(SMALL_ROWS, H).astype(F32)
    for k in range(3):
        cut = slice(k * H, (k + 1) * H)
        c.win[:, cut] = small[k * H : (k + 1) * H]
        c.wst[:, cut] = small[ROW_STATE_WEIGHT + k * H : ROW_STATE_WEIGHT + (k + 1) * H]
    c.bin[...] = small[ROW_INPUT_BIAS : ROW_INPUT_BIAS + 3]
    c.bst[...] = small[ROW_STATE_BIAS : ROW_STATE_BIAS + 3]
    copies[4].wait()
    c.w1[...] = c.hfl[0:16]
    c.b1[...] = c.hfl[16:17]
    c.turn[...] = small[ROW_SECOND_BIAS : ROW_SECOND_BIAS + H].T
    r = lax.axis_index("rep")
    c.b2[...] = c.turn[pl.ds(pl.multiple_of(r * J, J), J), :]
    copies[1].wait()
    c.feats[...] = c.hff[...].astype(F32)
    copies[2].wait()
    c.o_grads[...] = c.hgrads[...].astype(F32)
    copies[3].wait()


def body(
    s,
    node_states,
    edge_feats,
    edge_source,
    edge_target,
    edge_group,
    column_mask,
    edge_count,
    first_weight,
    first_bias,
    second_weight,
    second_bias,
    update_input_weight,
    update_state_weight,
    update_input_bias,
    update_state_bias,
    state_cotangent,
):
    H, N, E = s.H, s.N, s.E
    shapes = scratch(s)
    names = ["in_" + k for k in IN_NAMES] + OUT_NAMES + IN_NAMES + list(shapes)
    sds = jax.ShapeDtypeStruct
    hbm = pl.BlockSpec(memory_space=pl.ANY)
    operands = (
        node_states,
        edge_feats.T,
        edge_source.reshape(1, E),
        edge_target.reshape(1, E),
        edge_group.reshape(1, E),
        column_mask,
        edge_count.reshape(1, 1),
        first_weight,
        first_bias.reshape(1, H),
        second_weight,
        second_bias.reshape(s.J, H),
        update_input_weight,
        update_state_weight,
        update_input_bias.reshape(3, H),
        update_state_bias.reshape(3, H),
        state_cotangent,
    )
    held = [
        pltpu.VMEM((8, 128) if name == "w2" else x.shape, F32 if name == "w2" else x.dtype)
        for name, x in zip(IN_NAMES, operands)
    ]
    final, grads, ff, f, fl = pl.pallas_call(
        functools.partial(whole, s, names),
        out_shape=[
            sds((N, H), F32),
            sds((N, H), BF16),
            sds((16, E), BF16),
            sds((s.R + 1, s.OW, s.T * s.J, H), BF16),
            sds((FIRST_ROWS, H), F32),
        ],
        in_specs=[hbm] * 16,
        out_specs=[VMEM] * 5,
        scratch_shapes=held + list(shapes.values()),
        compiler_params=pltpu.CompilerParams(
            collective_id=0, has_side_effects=True, vmem_limit_bytes=63 * 2**20
        ),
        name="edge_network",
    )(*operands)
    final, grads, feats, w2, win, wst, bin_, bst, w1, b1, b2 = pl.pallas_call(
        functools.partial(finish, s),
        out_shape=[
            sds((N, H), F32),
            sds((N, H), F32),
            sds((16, E), F32),
            sds((H, s.J * H), F32),
            sds((H, 3 * H), F32),
            sds((H, 3 * H), F32),
            sds((3, H), F32),
            sds((3, H), F32),
            sds((16, H), F32),
            sds((1, H), F32),
            sds((s.J, H), F32),
        ],
        in_specs=[hbm] * 5,
        out_specs=[VMEM] * 11,
        scratch_shapes=[
            pltpu.VMEM((s.R + 1, s.OW, s.T * s.J, H), BF16),
            pltpu.VMEM((16, E), BF16),
            pltpu.VMEM((N, H), BF16),
            pltpu.VMEM((FIRST_ROWS, H), F32),
            pltpu.VMEM((H * s.J, H), F32),
            pltpu.VMEM((H, H), F32),
            pltpu.SemaphoreType.DMA((5,)),
        ],
        compiler_params=pltpu.CompilerParams(vmem_limit_bytes=60 * 2**20),
        name="finish",
    )(f, ff, final, grads, fl)
    return (
        final,
        grads,
        feats.T,
        w1,
        b1.reshape(-1),
        w2,
        b2.reshape(-1),
        win,
        wst,
        bin_.reshape(-1),
        bst.reshape(-1),
    )


def solution(mesh):
    in_specs = (
        P("blk", None),
        P("blk", None),
        P("blk"),
        P("blk"),
        P("blk"),
        P(),
        P("blk"),
        P(),
        P(),
        P(None, "rep"),
        P("rep"),
        P(),
        P(),
        P(),
        P(),
        P("blk", None),
    )
    out_specs = (
        P("blk", None),
        P("blk", None),
        P("blk", None),
        P(),
        P(),
        P(None, "rep"),
        P("rep"),
        P(),
        P(),
        P(),
        P(),
    )

    def run(*args):
        nodes, edges, width = args[0].shape[0], args[2].shape[0], args[0].shape[1]
        return body(sizes(mesh, edges, nodes, width), *args)

    return jax.shard_map(run, mesh=mesh, in_specs=in_specs, out_specs=out_specs, check_vma=False)
```

```python
import functools
from types import SimpleNamespace

import jax
import jax.numpy as jnp
from jax import lax
from jax.experimental import pallas as pl
from jax.experimental.pallas import tpu as pltpu
from jax.sharding import PartitionSpec as P

STEPS = 2
TILE = 512
LO = 256
ROWS = 512
SLAB = 32
VISITS = (22, 34)
NEAR = 2
F32, BF16, I32 = jnp.float32, jnp.bfloat16, jnp.int32
MESH = pl.DeviceIdType.MESH
VMEM = pl.BlockSpec(memory_space=pltpu.VMEM)

ROW_STATE_WEIGHT = 384
ROW_INPUT_BIAS = 768
ROW_STATE_BIAS = 776
GROUP = 16
FIRST_ROWS = 32
ROW_SECOND_BIAS = 896
SMALL_ROWS = 1024

(
    P_STATE,
    P_STATE2,
    P_WEIGHT,
    P_WEIGHT_PAIR,
    P_SPREAD,
    P_SPREAD2,
    P_GRAD_PAIR,
    P_GRAD,
    P_SMALL,
    P_FIRST,
    P_GRAD_ALL,
    P_GRAD_ALL_PAIR,
    PLANES,
) = range(13)
(
    Z_WEIGHT,
    Z_BIAS,
    Z_SUM,
    Z_SUM2,
    Z_STATE,
    Z_FINAL,
    Z_DELTA,
    Z_DELTA2,
    Z_SOURCE,
    Z_SOURCE2,
    Z_GRADS,
    Z_FEATS,
    Z_FEATS_ALL,
    Z_SECOND,
    Z_SMALL,
    Z_FIRST,
    LINES,
) = range(17)


def nn(a, b):
    return jnp.dot(a, b, preferred_element_type=F32)


def nt(a, b):
    return lax.dot_general(a, b, (((1,), (1,)), ((), ())), preferred_element_type=F32)


def iota(shape, dim):
    return lax.broadcasted_iota(I32, shape, dim)


def ones_where(condition):
    return jnp.where(condition, 1.0, 0.0).astype(BF16)


def eye(n):
    return ones_where(iota((n, n), 0) == iota((n, n), 1))


def two(x):
    high = x.astype(BF16)
    return high, (x - high.astype(F32)).astype(BF16)


def three(x):
    high, rest = x.astype(BF16), x
    rest = x - high.astype(F32)
    mid = rest.astype(BF16)
    return high, mid, (rest - mid.astype(F32)).astype(BF16)


def nn2(a, x):
    high, low = two(x)
    return nn(a, high) + nn(a, low)


def nt2(x, b):
    high, low = two(x)
    return nt(high, b) + nt(low, b)


def sizes(mesh, edges, nodes, width):
    s = SimpleNamespace()
    s.B, s.R = mesh.shape["blk"], mesh.shape["rep"]
    s.E, s.N, s.H = edges, nodes, width
    s.J = width // s.R
    s.HIB = nodes // LO
    s.HI = s.HIB * s.B
    s.NQ = nodes // s.R
    s.EQ = edges // s.R
    s.OW = min(s.B, 8)
    s.STRIDE = s.B // s.OW
    s.T = s.J // s.OW
    s.KEEP = s.B <= 8
    s.SMALL = SMALL_ROWS // s.OW
    s.C = s.B // 2
    s.G = nodes // GROUP
    s.V = s.G + edges // LO
    return s


def scratch(s):
    v = pltpu.VMEM
    jh = s.J * s.H
    shapes = dict(
        nst=v((s.H, s.N), F32),
        stq=v((STEPS, s.HIB, s.J, LO), BF16),
        tab=v((STEPS, s.B, s.HIB, s.J, LO), BF16),
        ys=v((s.R * s.T, s.J, s.H), F32),
        wsend=v((s.R, s.T, s.J, s.H), BF16),
        w2r=v((s.J, s.H, s.H), BF16),
        b2f=v((s.H, s.H), F32),
        baug=v((s.J, s.H, s.H), BF16),
        w2k=v((s.H, jh), BF16),
        tl=v((1, s.E), I32),
        ohln=v((s.E, LO), BF16),
        mt=v((32, s.E), BF16),
        gm=v((16, s.E), BF16),
        ht=v((s.E // LO, s.H, LO), BF16),
        tlc=v((s.E // LO, 1, LO), I32),
        st=v((STEPS, s.J, s.E), BF16),
        sf=v((s.J, s.E), F32),
        sc=v((s.E // LO, s.J, LO), BF16),
        ge=v((s.H, s.E), BF16),
        smt=v((2 * s.H + s.J, s.N), F32),
        ssum=v((STEPS, s.J, s.N), F32),
        rsq=v((s.R, s.H, s.NQ), F32),
        rsl=v((STEPS, s.R, s.H, s.NQ), F32),
        keep=v((STEPS, 5, s.NQ, s.H), F32),
        keept=v((STEPS, 2, s.H, s.NQ), BF16),
        nsq=v((s.H, s.NQ), BF16),
        fin=v((s.NQ, s.H), F32),
        gq=v((STEPS, s.NQ // GROUP, GROUP, s.H), BF16),
        gfull=v((STEPS, s.G, GROUP, s.H), BF16),
        hg=v((s.H, s.E), F32),
        gacc=v((jh, s.H), F32),
        xs=v((ROWS, TILE), BF16),
        scat=v((s.HI * s.J, LO), F32),
        rps=v((s.B, s.HIB * s.J, LO), BF16),
        rpl=v((STEPS, s.B, s.HIB * s.J, LO), BF16),
        fzs=v((STEPS, s.R, s.J, s.NQ), BF16),
        fzl=v((STEPS, s.R, s.J, s.NQ), BF16),
        gradq=v((s.NQ, s.H), F32),
        gradl=v((s.NQ, s.H), BF16),
        small=v((SMALL_ROWS, s.H), F32),
        q0=v((s.V, s.J * GROUP, s.H), BF16),
        gv=v((s.V * GROUP, s.H), BF16),
        planv=v((8, 128), I32),
        plan=pltpu.SMEM((8, 128), I32),
        firsts=v((FIRST_ROWS, s.H), F32),
        flz=v((s.R, FIRST_ROWS, s.H), F32),
        flp=v((s.B, FIRST_ROWS, s.H), F32),
        sgsend=v((SMALL_ROWS, s.H), BF16),
        sgland=v((s.B, s.SMALL, s.H), BF16),
        gz=v((s.R, s.T * s.J, s.H), BF16),
        sgz=v((s.R, s.SMALL, s.H), BF16),
        fqs=v((16, s.E), BF16),
        fql=v((s.R, 16, s.EQ), BF16),
        ps=pltpu.SemaphoreType.DMA((PLANES, s.B)),
        pr=pltpu.SemaphoreType.DMA((PLANES, s.B)),
        zs=pltpu.SemaphoreType.DMA((LINES, s.R)),
        zr=pltpu.SemaphoreType.DMA((LINES, s.R)),
        local=pltpu.SemaphoreType.DMA,
        ins=pltpu.SemaphoreType.DMA((len(IN_NAMES),)),
    )
    piece = (jh // s.OW, s.H)
    if s.STRIDE > 1:
        shapes["gland"] = v((s.B,) + piece, BF16)
        shapes["gsend"] = v((jh, s.H), BF16)
    if s.KEEP:
        shapes["mat"] = v((jh, s.E), BF16)
        shapes["sums"] = v((2, s.J, jh // 4), BF16)
    return shapes


IN_NAMES = (
    ["nodes", "feats", "src", "tgt", "grp", "cmask", "count", "w1", "b1"]
    + ["w2", "b2", "win", "wst", "bin", "bst", "cot"]
)
OUT_NAMES = ["final", "grads", "ff", "f", "fl"]


def whole(s, names, *refs):
    c = SimpleNamespace(**dict(zip(names, refs)))
    B, R, H, J, E, N, NQ, EQ = s.B, s.R, s.H, s.J, s.E, s.N, s.NQ, s.EQ
    T, OW, STRIDE = s.T, s.OW, s.STRIDE
    jh = J * H
    tiles = E // TILE
    b = lax.axis_index("blk")
    r = lax.axis_index("rep")
    owner = b // STRIDE
    is_owner = lax.rem(b, STRIDE) == 0
    sent = []

    def push(src, dst, sems, rems, axis, peer):
        return pltpu.make_async_remote_copy(
            src_ref=src,
            dst_ref=dst,
            send_sem=sems,
            recv_sem=rems,
            device_id={axis: peer},
            device_id_type=MESH,
        )

    def plane(x, src_of, dst):
        copies = []
        for d in range(1, B):
            peer = lax.rem(b + d, B)
            cp = push(src_of(peer), dst, c.ps.at[x, d], c.pr.at[x, d], "blk", peer)
            cp.start()
            copies.append(cp)
        sent.extend(copies)
        return copies

    def line(x, src_of, dst):
        copies = []
        for d in sorted(range(1, R), key=lambda d: abs(d - R / 2)):
            peer = lax.rem(r + d, R)
            cp = push(src_of(peer), dst, c.zs.at[x, d], c.zr.at[x, d], "rep", peer)
            cp.start()
            copies.append(cp)
        sent.extend(copies)
        return copies

    def arrive(copies, reuse=False):
        for cp in copies:
            cp.wait_recv()
        if reuse:
            release(copies)

    def release(copies):
        for cp in copies:
            cp.wait_send()
            sent[:] = [other for other in sent if other is not cp]

    def when_owner(fn):
        if STRIDE == 1:
            fn()
        else:
            pl.when(is_owner)(fn)

    def line_owner(x, src_of, dst):
        copies = []
        for d in range(1, R):
            peer = lax.rem(r + d, R)
            copies.append(push(src_of(peer), dst, c.zs.at[x, d], c.zr.at[x, d], "rep", peer))
        when_owner(lambda: [cp.start() for cp in copies] and None)
        owner_sent.extend(copies)
        return copies

    owner_sent = []

    def from_owners(x, strip_of):
        copies = []
        for d in range(1, B):
            peer = lax.rem(b + d, B)
            strip = strip_of(owner)
            copies.append(push(strip, strip, c.ps.at[x, d], c.pr.at[x, owner], "blk", peer))
        when_owner(lambda: [cp.start() for cp in copies] and None)
        owner_sent.extend(copies)

        def wait():
            for q in range(OW):

                @pl.when(b != q * STRIDE)
                def _():
                    strip = strip_of(q)
                    peer = lax.rem(b + 1, B)
                    push(strip, strip, c.ps.at[x, 0], c.pr.at[x, q], "blk", peer).wait_recv()

        return lambda: None, wait, [], []

    chip, core = b // 2, lax.rem(b, 2)

    column, line_of = lax.rem(chip, 2), chip // 2
    lines = max(s.C // 2, 1)

    def device(m, its_core, back=False):
        up = lines - m // 2 if back else m // 2
        return 2 * (2 * lax.rem(line_of + up, lines) + lax.rem(column + lax.rem(m, 2), 2)) + its_core

    def slot_rows(at):
        if STRIDE > 1:
            return at
        slot = at // T
        held_by = jnp.where(slot < s.C, core, 1 - core)
        return T * device(lax.rem(slot, s.C), held_by, True) + lax.rem(at, T)

    def slot(k):
        return c.w2r.at[k * T : (k + 1) * T]

    def gather_pairs(x, x2, first_of, then_of, late=s.C):
        first, then = [], []
        for m in range(1, s.C):
            src, dst = first_of(m)
            first.append(push(src, dst, c.ps.at[x, m], c.pr.at[x, m], "blk", device(m, core)))
        for m in range(s.C):
            src, dst = then_of(m)
            then.append(
                push(src, dst, c.ps.at[x2, m], c.pr.at[x2, m], "blk", device(0, 1 - core))
            )
        for cp in first[:late] + then[:1]:
            cp.start()

        def relay(begin=1, end=s.C):
            for m in range(begin, end):
                first[m - 1].wait_recv()
                then[m].start()

        def wait():
            arrive(then)

        sent.extend(first + then)
        return relay, wait, first, then

    def to_owners(x, src_of, dst):
        if STRIDE == 1:
            copies = plane(x, src_of, dst)
            return lambda: arrive(copies)
        for q in range(OW):

            @pl.when(b != q * STRIDE)
            def _():
                push(src_of(q), dst, c.ps.at[x, q], c.pr.at[x, b], "blk", q * STRIDE).start()

        def wait():
            def arrivals():
                for d in range(1, B):
                    peer = lax.rem(b + d, B)
                    push(src_of(0), dst, c.ps.at[x, 0], c.pr.at[x, peer], "blk", peer).wait_recv()

            when_owner(arrivals)
            for q in range(OW):

                @pl.when(b != q * STRIDE)
                def _():
                    push(src_of(q), dst, c.ps.at[x, q], c.pr.at[x, b], "blk", q * STRIDE).wait_send()

        return wait

    def edges(t):
        return pl.ds(pl.multiple_of(t * TILE, TILE), TILE)

    barrier = pltpu.get_barrier_semaphore()
    for d in range(1, B):
        pl.semaphore_signal(
            barrier, inc=1, device_id={"blk": lax.rem(b + d, B)}, device_id_type=MESH
        )
    for d in range(1, R):
        pl.semaphore_signal(
            barrier, inc=1, device_id={"rep": lax.rem(r + d, R)}, device_id_type=MESH
        )

    loads = {}
    for k, name in enumerate(IN_NAMES):
        to = c.w2k if name == "w2" else getattr(c, name)
        loads[name] = pltpu.make_async_copy(getattr(c, "in_" + name), to, c.ins.at[k])
    for name in ["nodes", "w2"]:
        loads[name].start()
    for name in IN_NAMES:
        if name not in ("nodes", "w2"):
            loads[name].start()
    eye_h = eye(H)
    part = pl.ds(pl.multiple_of(r * J, J), J)

    loads["nodes"].wait()
    c.nst[...] = c.nodes[...].T
    own_columns = c.nst[part, :].astype(BF16)
    for k in range(s.HIB):
        c.stq[0, k] = own_columns[:, k * LO : (k + 1) * LO]
    c.tab[0, b] = c.stq[0]
    row = iota((R * T, H), 0)
    pick = ones_where(iota((R * T, H), 1) == (row // T) * J + T * owner + lax.rem(row, T))
    loads["w2"].wait()
    for i in range(J):
        c.ys[:, i, :] = nt(pick, c.w2k[:, i * H : (i + 1) * H])
    c.wsend[...] = c.ys[...].astype(BF16).reshape(R, T, J, H)
    for name in IN_NAMES:
        if name not in ("nodes", "w2"):
            loads[name].wait()
    pl.semaphore_wait(barrier, B - 1 + R - 1)

    states_in = plane(P_STATE, lambda peer: c.stq.at[0], c.tab.at[0, b])
    strip = pl.ds(0 if STRIDE == 1 else pl.multiple_of(T * owner, T), T)
    weight_in = line_owner(Z_WEIGHT, lambda peer: c.wsend.at[peer], c.w2r.at[strip, part, :])
    c.b2f[part, :] = c.b2[...]
    bias_in = line(Z_BIAS, lambda peer: c.b2, c.b2f.at[part, :])

    def own_strip():
        c.w2r[strip, part, :] = c.wsend[r]

    when_owner(own_strip)

    place = iota((1, E), 1)
    c.tl[...] = jnp.where(place < c.count[...], c.tgt[...] - b * N, -1)
    for k in range(E // LO):
        c.tlc[k] = c.tl[:, k * LO : (k + 1) * LO]
    ends = jnp.where(c.tgt[...] - b * N < GROUP * (iota((s.G, E), 0) + 1), 1, 0)
    ends = jnp.sum(ends, axis=1, keepdims=True)
    left_in = jnp.maximum((ends + (LO - 1)) // LO - 1, 0)
    group = iota((s.G, 128), 0)
    leave = group + jnp.where(group == s.G - 1, E // LO - 1, left_in)
    visited = jnp.sum(jnp.where(leave < iota((s.G, 128), 1), 1, 0), axis=0, keepdims=True)
    c.planv[...] = jnp.broadcast_to(visited, (8, 128))
    plan_copy = pltpu.make_async_copy(c.planv, c.plan, c.local)
    plan_copy.start()
    cmt = nt(eye(16), c.cmask[...].astype(F32).astype(BF16)).astype(BF16)
    b1 = three(c.b1[...])
    first = jnp.concatenate(
        [c.w1[...].astype(F32)] + [x.astype(F32) for x in b1] + [jnp.zeros((13, H), F32)], axis=0
    ).astype(BF16)
    w1ta = nt(eye_h, first).astype(BF16)
    eye_t = eye(LO)

    def target_rows(t):
        return ones_where(iota((N, TILE), 0) == c.tl[:, edges(t)])

    def low_rows(t):
        return ones_where(iota((LO, TILE), 0) == (c.src[:, edges(t)] & (LO - 1)))

    per_tile = TILE // LO

    def put(ref, t, value):
        for k in range(per_tile):
            ref[t * per_tile + k] = value[:, k * LO : (k + 1) * LO]

    def hidden_of(t):
        return jnp.concatenate([c.ht[t * per_tile + k] for k in range(per_tile)], axis=1)

    def prepare(t, carry):
        e = edges(t)
        groups = ones_where(iota((16, TILE), 0) == c.grp[:, e])
        gm = nn(cmt, groups)
        c.gm[:, e] = gm.astype(BF16)
        masked = c.feats[:, e].astype(F32) * gm
        ones = jnp.where(iota((16, TILE), 0) < 3, 1.0, 0.0)
        mt = jnp.concatenate([masked, ones], axis=0).astype(BF16)
        c.mt[:, e] = mt
        pre = nn(w1ta, mt)
        hidden = (pre * jax.nn.sigmoid(pre)).astype(BF16)
        put(c.ht, t, hidden)
        lows = low_rows(t)
        for k in range(TILE // LO):
            rows = pl.ds(pl.multiple_of(t * TILE + k * LO, LO), LO)
            c.ohln[rows, :] = nt(eye_t, lows[:, k * LO : (k + 1) * LO]).astype(BF16)
        return carry

    lax.fori_loop(0, tiles, prepare, 0)

    when_owner(lambda: arrive(weight_in))
    if STRIDE == 1:
        weight_relay, weight_wait, weight_chip, weight_pair = gather_pairs(
            P_WEIGHT,
            P_WEIGHT_PAIR,
            lambda m: (slot(0), slot(m)),
            lambda m: (slot(m), slot(s.C + m)),
        )
    else:
        weight_relay, weight_wait, weight_chip, weight_pair = from_owners(
            P_WEIGHT, lambda q: c.w2r.at[pl.ds(pl.multiple_of(T * q, T), T)]
        )

    to_slots = ones_where(iota((J, J), 1) == slot_rows(iota((J, J), 0)))
    from_slots = ones_where(iota((J, J), 0) == slot_rows(iota((J, J), 1)))

    def gather(step):
        if STRIDE == 1:
            for q in range(B):
                for k in range(s.HIB):
                    c.tab[step, q, k] = nn(to_slots, c.tab[step, q, k]).astype(BF16)

        def one(t, carry):
            e = edges(t)
            lows = low_rows(t)
            high = c.src[:, e] // LO
            total = jnp.zeros((J, TILE), F32)
            per = ROWS // J
            for g in range(s.HI // per):
                blocks = per // s.HIB
                table = c.tab[step, g * blocks : (g + 1) * blocks].reshape(ROWS, LO)
                rows = nn(table, lows)
                for k in range(per):
                    total = total + jnp.where(high == g * per + k, rows[k * J : (k + 1) * J], 0.0)
            c.st[step, :, e] = total.astype(BF16)
            c.sf[:, e] = total
            if step == 0:
                put(c.sc, t, total.astype(BF16))
            return carry

        lax.fori_loop(0, tiles, one, 0, unroll=2)

    arrive(states_in)
    gather(0)
    arrive(bias_in)
    b2 = jnp.concatenate(three(c.b2f[...]), axis=1)

    def bias_columns(j, carry):
        at = iota((3 * H, H), 0)
        to = iota((3 * H, H), 1)
        move = ones_where((lax.rem(at, H) == r * J + slot_rows(j)) & (to == at // H))
        c.baug[j] = nn(b2, move).astype(BF16)
        return carry

    lax.fori_loop(0, J, bias_columns, 0, unroll=8)

    def turned(j, carry):
        c.w2k[:, pl.ds(pl.multiple_of(j * H, H), H)] = nt(eye_h, c.w2r[j]).astype(BF16)
        return carry

    chunk = ROWS // H

    def hidden_rows(t):
        ones = jnp.where(iota((H, TILE), 0) < 3, 1.0, 0.0).astype(BF16)
        return jnp.concatenate([hidden_of(t), ones], axis=0)

    def held_messages(t):
        e = edges(t)
        parts = []
        for k in range(H // SLAB):
            total = jnp.zeros((SLAB, TILE), F32)
            for j in range(J):
                at = j * H + k * SLAB
                total = total + c.mat[at : at + SLAB, e].astype(F32) * c.sf[j : j + 1, e]
            parts.append(total)
        return jnp.concatenate(parts, axis=0)

    half, few = J // 2, H // 2
    if s.KEEP:
        rows, columns = iota((J, half * few), 0), iota((J, half * few), 1) // few
        for k in range(2):
            c.sums[k] = ones_where(rows == slot_rows(columns + k * half))

    def held_sources(e):
        grads = c.ge[:, e]
        total = jnp.zeros((J, TILE), F32)
        for k in range(2):
            held = c.mat[k * half * H : (k + 1) * half * H, e].reshape(half, H, TILE)
            product = held * grads[None]
            product = product[:, :few] + product[:, few:]
            total = total + nn(c.sums[k], product.reshape(half * few, TILE))
        return total

    def matrices(k, e, hidden):
        cut = slice(k * chunk, (k + 1) * chunk)
        left = jnp.concatenate(
            [c.w2r[cut].reshape(ROWS, H), c.baug[cut].reshape(ROWS, H)], axis=1
        )
        return nn(left, hidden).astype(BF16).astype(F32)

    def first_pass(strips, start):
        def one(t, carry):
            e = edges(t)
            hidden = hidden_rows(t)
            total = jnp.zeros((H, TILE), F32) if start else c.hg[:, e]
            for q in strips:
                cut = slice(q * T, (q + 1) * T)
                left = jnp.concatenate(
                    [c.w2r[cut].reshape(T * H, H), c.baug[cut].reshape(T * H, H)], axis=1
                )
                low = nn(left, hidden).astype(BF16)
                c.mat[q * T * H : (q + 1) * T * H, e] = low
                m = low.astype(F32)
                for p in range(T):
                    total = total + m[p * H : (p + 1) * H] * c.sf[q * T + p : q * T + p + 1, e]
            c.hg[:, e] = total
            return carry

        lax.fori_loop(0, tiles, one, 0, unroll=4 if len(strips) < 3 else 2)

    def messages(step):
        c.smt[...] = jnp.zeros_like(c.smt)

        def one(t, carry):
            e = edges(t)
            low = c.st[step, :, e]
            if s.KEEP:
                total = held_messages(t) if step > 0 else c.hg[:, e]
            else:
                source = low.astype(F32)
                hidden = hidden_rows(t)
                total = jnp.zeros((H, TILE), F32)
                for k in range(J // chunk):
                    m = matrices(k, e, hidden)
                    for q in range(chunk):
                        j = k * chunk + q
                        total = total + m[q * H : (q + 1) * H] * source[j : j + 1, :]
            high, rest = two(total)
            rows = jnp.concatenate([high, rest, low], axis=0)
            c.smt[...] += nt(rows, target_rows(t))
            return carry

        lax.fori_loop(0, tiles, one, 0, unroll=2)
        summed = c.smt[0:H, :] + c.smt[H : 2 * H, :]
        c.ssum[step] = c.smt[2 * H : 2 * H + J, :]
        for q in range(R):
            c.rsq[q] = summed[:, q * NQ : (q + 1) * NQ]
        c.rsl[step, r] = c.rsq[r]
        return line(Z_SUM + step, lambda peer: c.rsq.at[peer], c.rsl.at[step, r])

    def gate_bias(ref):
        return jnp.concatenate([ref[k : k + 1, :] for k in range(3)], axis=1)

    def gates(step, before, before_t):
        summed = c.rsl[step, 0]
        for q in range(1, R):
            summed = summed + c.rsl[step, q]
        summed_low = summed.T.astype(BF16)
        gi = nn(summed_low, c.win[...]) + gate_bias(c.bin)
        gs = nn(before.astype(BF16), c.wst[...]) + gate_bias(c.bst)
        reset = jax.nn.sigmoid(gi[:, :H] + gs[:, :H])
        update = jax.nn.sigmoid(gi[:, H : 2 * H] + gs[:, H : 2 * H])
        state_part = gs[:, 2 * H :]
        candidate = jnp.tanh(gi[:, 2 * H :] + reset * state_part)
        for k, x in enumerate((before, reset, update, candidate, state_part)):
            c.keep[step, k] = x
        c.keept[step, 0] = summed.astype(BF16)
        c.keept[step, 1] = before_t
        return (1.0 - update) * candidate + update * before

    def products(begin, end):
        def one(t, carry):
            g = c.plan[0, t]
            ch = t - g
            mine = ones_where(iota((GROUP, LO), 0) + g * GROUP == c.tlc[ch])
            source = c.sc[ch].astype(F32)
            parts = []
            for j in range(J):
                row = jnp.broadcast_to(source[j : j + 1, :], (GROUP, LO)).astype(BF16)
                parts.append(row * mine)
            c.q0[t] = nt(jnp.concatenate(parts, axis=0), c.ht[ch]).astype(BF16)
            return carry

        lax.fori_loop(begin, end, one, 0)

    plan_copy.wait()
    nodes_here = pl.ds(pl.multiple_of(r * NQ, NQ), NQ)
    groups_here = pl.ds(pl.multiple_of(r * (NQ // GROUP), NQ // GROUP), NQ // GROUP)
    if s.KEEP:
        near = NEAR + 1
        first_pass([0], True)
        weight_relay()
        first_pass(range(1, s.C), False)
        arrive(weight_pair)
        first_pass(range(s.C, OW), False)
    else:
        weight_wait()
    sums = messages(0)
    lax.fori_loop(0, J, turned, 0, unroll=8)
    products(0, VISITS[0])
    arrive(sums, reuse=True)
    release(weight_chip + weight_pair)
    state = gates(0, c.nodes[nodes_here, :], c.nst[:, nodes_here].astype(BF16))
    state_t = state.T.astype(BF16)
    c.nsq[...] = state_t
    hib = r // (LO // NQ)
    lanes = pl.ds(pl.multiple_of(lax.rem(r, LO // NQ) * NQ, NQ), NQ)
    c.stq[1, hib, :, lanes] = c.nsq[part, :]
    pieces = line(
        Z_STATE,
        lambda peer: c.nsq.at[pl.ds(pl.multiple_of(peer * J, J), J), :],
        c.stq.at[1, hib, :, lanes],
    )
    products(VISITS[0], VISITS[1])
    arrive(pieces)
    c.tab[1, b] = c.stq[1]
    states_in = plane(P_STATE2, lambda peer: c.stq.at[1], c.tab.at[1, b])
    products(VISITS[1], s.V)
    arrive(states_in)
    gather(1)
    sums = messages(1)
    arrive(sums)
    final = gates(1, state, state_t)
    c.fin[...] = final
    c.final[nodes_here, :] = final

    c.small[...] = jnp.zeros_like(c.small)
    c.gacc[...] = jnp.zeros_like(c.gacc)

    def deltas(step, grad):
        before, reset, update, candidate, state_part = [c.keep[step, k] for k in range(5)]
        dn = grad * (1.0 - update)
        dz = grad * (before - candidate)
        dpn = dn * (1.0 - candidate * candidate)
        dpz = dz * update * (1.0 - update)
        dpr = dpn * state_part * reset * (1.0 - reset)
        to_input = jnp.concatenate([dpr, dpz, dpn], axis=1)
        to_state = jnp.concatenate([dpr, dpz, dpn * reset], axis=1)
        summed_grad = nt2(to_input, c.win[...]).astype(BF16)
        c.gq[step] = summed_grad.reshape(NQ // GROUP, GROUP, H)
        c.gfull[step, groups_here] = c.gq[step]
        copies = line(Z_DELTA + step, lambda peer: c.gq.at[step], c.gfull.at[step, groups_here])
        gwi = nn2(c.keept[step, 0], to_input)
        gws = nn2(c.keept[step, 1], to_state)
        gbi = jnp.sum(to_input, axis=0, keepdims=True)
        gbs = jnp.sum(to_state, axis=0, keepdims=True)
        for k in range(3):
            cut = slice(k * H, (k + 1) * H)
            c.small[k * H : (k + 1) * H, :] += gwi[:, cut]
            c.small[ROW_STATE_WEIGHT + k * H : ROW_STATE_WEIGHT + (k + 1) * H, :] += gws[:, cut]
            c.small[ROW_INPUT_BIAS + k : ROW_INPUT_BIAS + k + 1, :] += gbi[:, cut]
            c.small[ROW_STATE_BIAS + k : ROW_STATE_BIAS + k + 1, :] += gbs[:, cut]
        c.gradq[...] = grad * update + nt2(to_state, c.wst[...])
        return copies

    def node_grads(step):
        held = c.gfull[step].reshape(N, H)
        gt = nt(eye_h, held).astype(BF16)

        def one(t, carry):
            c.ge[:, edges(t)] = nn(gt, target_rows(t)).astype(BF16)
            return carry

        lax.fori_loop(0, tiles, one, 0, unroll=2)
    def second_bias_grads(step):
        held = c.gfull[step].reshape(N, H)
        rows = pl.ds(ROW_SECOND_BIAS + pl.multiple_of(r * J, J), J)
        high, low = [nn(from_slots, x).astype(BF16) for x in two(c.ssum[step])]
        c.small[rows, :] += nn(high, held) + nn(low, held)

    def weights_tile(step, t, second):
        e = edges(t)
        at_edges = c.ge[:, e]
        source = c.st[step, :, e].astype(F32)
        got = None if step == STEPS - 1 else c.hg[:, e]
        spread = at_edges.reshape(H // 16, 16, TILE)
        for k in range(jh // ROWS):
            parts = []
            for j in range(k * ROWS // H, (k + 1) * ROWS // H):
                row = jnp.broadcast_to(source[j : j + 1, :], (16, TILE)).astype(BF16)
                parts.append((spread * row[None]).reshape(H, TILE))
            outer = jnp.concatenate(parts, axis=0)
            rows = slice(k * ROWS, (k + 1) * ROWS)
            more = nn(c.w2k[:, rows], outer)
            got = more if got is None else got + more
            if second:
                c.gacc[rows, :] += nt(outer, hidden_of(t))
        c.hg[:, e] = got

    def weights(step, begin, end):
        def one(t, carry):
            weights_tile(step, t, step == STEPS - 1)
            return carry

        lax.fori_loop(begin, end, one, 0, unroll=2 if step == 0 else 1)

    def sources(step, begin, end):
        if begin == 0:
            c.scat[...] = jnp.zeros_like(c.scat)

        def one(t, carry):
            e = edges(t)
            if s.KEEP:
                got = held_sources(e)
            else:
                at_edges = c.ge[:, e].astype(F32)
                hidden = hidden_rows(t)
                parts = []
                for k in range(J // chunk):
                    m = matrices(k, e, hidden)
                    for q in range(chunk):
                        parts.append(
                            jnp.sum(m[q * H : (q + 1) * H] * at_edges, axis=0, keepdims=True)
                        )
                got = jnp.concatenate(parts, axis=0)
            high = c.src[:, e] // LO
            per = ROWS // J
            for g in range(s.HI // per):
                for k in range(per):
                    c.xs[k * J : (k + 1) * J, :] = jnp.where(high == g * per + k, got, 0.0).astype(
                        BF16
                    )
                c.scat[g * ROWS : (g + 1) * ROWS, :] += nn(c.xs[...], c.ohln[e, :])
            return carry

        lax.fori_loop(begin, end, one, 0)

    def spread_sources(step):
        c.rps[...] = c.scat[...].astype(BF16).reshape(B, s.HIB * J, LO)
        c.rpl[step, b] = c.rps[b]
        return plane(P_SPREAD + step, lambda peer: c.rps.at[peer], c.rpl.at[step, b])

    def share_sources(step):
        total = c.rpl[step, 0].astype(F32)
        for q in range(1, B):
            total = total + c.rpl[step, q].astype(F32)
        for q in range(R):
            k, lane = (q * NQ) // LO, (q * NQ) % LO
            c.fzs[step, q] = total[k * J : (k + 1) * J, lane : lane + NQ].astype(BF16)
        c.fzl[step, r] = c.fzs[step, r]
        return line(Z_SOURCE + step, lambda peer: c.fzs.at[step, peer], c.fzl.at[step, r])

    def state_grad(step):
        return c.gradq[...] + c.fzl[step].reshape(H, NQ).astype(F32).T

    last = STEPS - 1
    copies = deltas(last, c.cot[nodes_here, :])
    arrive(copies)
    final_in = line(Z_FINAL, lambda peer: c.fin, c.final.at[nodes_here, :])
    node_grads(last)
    sources(last, 0, tiles)
    spread = spread_sources(last)
    second_bias_grads(last)
    weights(last, 0, 3)
    arrive(spread, reuse=True)
    pieces = share_sources(last)
    weights(last, 3, 5)
    arrive(pieces)
    copies = deltas(0, state_grad(last))
    weights(last, 5, tiles)
    arrive(copies)
    def group_rows(t, carry):
        rows = pl.ds(pl.multiple_of(t * GROUP, GROUP), GROUP)
        c.gv[rows, :] = c.gfull[0, jnp.minimum(c.plan[0, t], s.G - 1)]
        return carry

    lax.fori_loop(0, s.V, group_rows, 0, unroll=8)
    grads_t = nt(eye_h, c.gv[...]).astype(BF16)

    def second_weight_rows(k, carry):
        held = [
            c.q0[:, pl.ds(pl.multiple_of((2 * k + p) * GROUP, GROUP), GROUP), :] for p in range(2)
        ]
        held = [x.reshape(s.V * GROUP, H) for x in held]
        more = nn(grads_t, jnp.concatenate(held, axis=1))
        for p in range(2):
            rows = pl.ds(pl.multiple_of((2 * k + p) * H, H), H)
            c.gacc[rows, :] += more[:, p * H : (p + 1) * H]
        return carry

    lax.fori_loop(0, J // 2, second_weight_rows, 0, unroll=4)

    per_owner = jh // OW

    def grad_rows(q):
        return c.gacc[pl.ds(pl.multiple_of(q * per_owner, per_owner), per_owner), :]

    if STRIDE == 1:
        def piece_rows(k):
            return c.gacc[k * per_owner : (k + 1) * per_owner, :].reshape(T, H, H)

        def pieces_in(ref, k):
            return ref.at[k * T : (k + 1) * T]

        pair = []
        for m in range(s.C):
            c.baug[m * T : (m + 1) * T] = piece_rows(s.C + m).astype(BF16)
            x = P_GRAD_PAIR
            cp = push(
                pieces_in(c.baug, m),
                pieces_in(c.w2r, m),
                c.ps.at[x, m],
                c.pr.at[x, m],
                "blk",
                device(0, 1 - core),
            )
            cp.start()
            pair.append(cp)
        sent.extend(pair)
    else:
        c.gsend[...] = c.gacc[...].astype(BF16)

        def own_grads():
            c.gland[b] = grad_rows(owner).astype(BF16)

        when_owner(own_grads)
        grads_wait = to_owners(
            P_GRAD,
            lambda q: c.gsend.at[pl.ds(pl.multiple_of(q * per_owner, per_owner), per_owner), :],
            c.gland.at[b],
        )

    node_grads(0)
    second_bias_grads(0)

    c.sgsend[...] = c.small[...].astype(BF16)

    def small_rows(q):
        return pl.ds(pl.multiple_of(q * s.SMALL, s.SMALL), s.SMALL)

    def own_small():
        c.sgland[b] = c.sgsend[small_rows(owner), :]

    when_owner(own_small)
    small_wait = to_owners(P_SMALL, lambda q: c.sgsend.at[small_rows(q), :], c.sgland.at[b])

    if STRIDE == 1:
        across = []
        for m in list(range(1, s.C)) + [0]:
            if m == 1:
                arrive(pair)
            total = piece_rows(m) + c.w2r[m * T : (m + 1) * T].astype(F32)
            total = total.astype(BF16)
            if m == 0:
                c.w2r[s.C * T : (s.C + 1) * T] = total
                continue
            c.baug[(s.C + m) * T : (s.C + m + 1) * T] = total
            x = P_GRAD
            cp = push(
                pieces_in(c.baug, s.C + m),
                pieces_in(c.w2r, s.C + m),
                c.ps.at[x, m],
                c.pr.at[x, m],
                "blk",
                device(m, core, True),
            )
            cp.start()
            across.append(cp)
        sent.extend(across)

        def grads_wait():
            arrive(across)

    def total_of(ref, rows, count):
        total = ref[0, rows, :].astype(F32)
        for q in range(1, count):
            total = total + ref[q, rows, :].astype(F32)
        return total

    sources(0, 0, tiles)
    spread = spread_sources(0)
    small_wait()

    def reduce_small():
        c.sgz[r] = total_of(c.sgland, slice(None), B).astype(BF16)

    when_owner(reduce_small)
    small_in = line_owner(Z_SMALL, lambda peer: c.sgz.at[r], c.sgz.at[r])
    weights(0, 0, 2)
    grads_wait()

    def reduce_grads():
        for t in range(T):
            if STRIDE == 1:
                total = c.w2r[s.C * T + t].astype(F32)
                for q in range(1, s.C):
                    total = total + c.w2r[(s.C + q) * T + t].astype(F32)
            else:
                total = total_of(c.gland, slice(t * H, (t + 1) * H), B)
            total = total.astype(BF16)
            for q in range(R):
                c.gz[q, t * J : (t + 1) * J, :] = total[q * J : (q + 1) * J, :]
        c.f[r, owner] = c.gz[r]

    when_owner(reduce_grads)
    second_in = line_owner(Z_SECOND, lambda peer: c.gz.at[peer], c.f.at[r, owner])
    weights(0, 2, 4)
    arrive(spread)
    pieces = share_sources(0)
    weights(0, 4, tiles)

    def sum_small():
        arrive(small_in)
        c.f[R, owner] = total_of(c.sgz, slice(None), R).astype(BF16)
        arrive(second_in)

    when_owner(sum_small)
    if STRIDE == 1:

        def held_strip(m):
            strip = c.f.at[:, device(m, core, True)]
            return strip, strip

        second_relay, second_wait, _, _ = gather_pairs(
            P_GRAD_ALL, P_GRAD_ALL_PAIR, lambda m: held_strip(0), held_strip
        )
    else:
        second_relay, second_wait, _, _ = from_owners(P_GRAD_ALL, lambda q: c.f.at[:, q])

    arrive(pieces)
    grad = state_grad(0).astype(BF16)
    c.gradl[...] = grad
    c.grads[nodes_here, :] = grad
    grads_in = line(Z_GRADS, lambda peer: c.gradl, c.grads.at[nodes_here, :])

    w1 = c.w1[...]
    c.firsts[...] = jnp.zeros_like(c.firsts)

    def first_layer(t, carry):
        e = edges(t)
        mt = c.mt[:, e]
        pre = nn(w1ta, mt)
        gate = jax.nn.sigmoid(pre)
        pre_grad = c.hg[:, e] * gate * (1.0 + pre * (1.0 - gate))
        pre_grad = pre_grad.astype(BF16)
        c.fqs[:, e] = (nn(w1, pre_grad) * c.gm[:, e].astype(F32)).astype(BF16)
        c.firsts[...] += nt(mt, pre_grad)
        return carry

    lax.fori_loop(0, tiles, first_layer, 0, unroll=2)
    edges_here = pl.ds(pl.multiple_of(r * EQ, EQ), EQ)
    c.fql[r] = c.fqs[:, edges_here]
    feats_in = line(
        Z_FEATS,
        lambda peer: c.fqs.at[:, pl.ds(pl.multiple_of(peer * EQ, EQ), EQ)],
        c.fql.at[r],
    )
    c.flz[r] = c.firsts[...]
    firsts_in = line(Z_FIRST, lambda peer: c.firsts, c.flz.at[r])

    arrive(feats_in)
    c.ff[:, edges_here] = total_of(c.fql, slice(None), R).astype(BF16)
    feats_all = line(Z_FEATS_ALL, lambda peer: c.ff.at[:, edges_here], c.ff.at[:, edges_here])
    arrive(firsts_in)
    c.flp[b] = total_of(c.flz, slice(None), R)
    firsts_all = plane(P_FIRST, lambda peer: c.flp.at[b], c.flp.at[b])
    second_relay()
    arrive(grads_in)
    arrive(final_in)
    arrive(firsts_all)
    c.fl[...] = total_of(c.flp, slice(None), B)
    arrive(feats_all)
    second_wait()
    for cp in sent:
        cp.wait_send()
    when_owner(lambda: [cp.wait_send() for cp in owner_sent] and None)


FINISH_NAMES = (
    ["f", "ff", "final", "grads", "fl"]
    + ["o_final", "o_grads", "feats", "w2", "win", "wst", "bin", "bst", "w1", "b1", "b2"]
    + ["hf", "hff", "hgrads", "hfl", "wide", "turn", "sems"]
)


def finish(s, *refs):
    c = SimpleNamespace(**dict(zip(FINISH_NAMES, refs)))
    H, J = s.H, s.J
    pairs = [(c.f, c.hf), (c.ff, c.hff), (c.grads, c.hgrads), (c.final, c.o_final)]
    pairs.append((c.fl, c.hfl))
    copies = [pltpu.make_async_copy(x, y, c.sems.at[k]) for k, (x, y) in enumerate(pairs)]
    for cp in copies:
        cp.start()
    copies[0].wait()
    c.wide[...] = c.hf[0 : s.R].reshape(H * J, H).astype(F32)
    for i in range(J):
        c.w2[:, i * H : (i + 1) * H] = c.wide[pl.ds(i, H, stride=J), :].T
    small = c.hf[s.R].reshape(SMALL_ROWS, H).astype(F32)
    for k in range(3):
        cut = slice(k * H, (k + 1) * H)
        c.win[:, cut] = small[k * H : (k + 1) * H]
        c.wst[:, cut] = small[ROW_STATE_WEIGHT + k * H : ROW_STATE_WEIGHT + (k + 1) * H]
    c.bin[...] = small[ROW_INPUT_BIAS : ROW_INPUT_BIAS + 3]
    c.bst[...] = small[ROW_STATE_BIAS : ROW_STATE_BIAS + 3]
    copies[4].wait()
    c.w1[...] = c.hfl[0:16]
    c.b1[...] = c.hfl[16:17]
    c.turn[...] = small[ROW_SECOND_BIAS : ROW_SECOND_BIAS + H].T
    r = lax.axis_index("rep")
    c.b2[...] = c.turn[pl.ds(pl.multiple_of(r * J, J), J), :]
    copies[1].wait()
    c.feats[...] = c.hff[...].astype(F32)
    copies[2].wait()
    c.o_grads[...] = c.hgrads[...].astype(F32)
    copies[3].wait()


def body(
    s,
    node_states,
    edge_feats,
    edge_source,
    edge_target,
    edge_group,
    column_mask,
    edge_count,
    first_weight,
    first_bias,
    second_weight,
    second_bias,
    update_input_weight,
    update_state_weight,
    update_input_bias,
    update_state_bias,
    state_cotangent,
):
    H, N, E = s.H, s.N, s.E
    shapes = scratch(s)
    names = ["in_" + k for k in IN_NAMES] + OUT_NAMES + IN_NAMES + list(shapes)
    sds = jax.ShapeDtypeStruct
    hbm = pl.BlockSpec(memory_space=pl.ANY)
    operands = (
        node_states,
        edge_feats.T,
        edge_source.reshape(1, E),
        edge_target.reshape(1, E),
        edge_group.reshape(1, E),
        column_mask,
        edge_count.reshape(1, 1),
        first_weight,
        first_bias.reshape(1, H),
        second_weight,
        second_bias.reshape(s.J, H),
        update_input_weight,
        update_state_weight,
        update_input_bias.reshape(3, H),
        update_state_bias.reshape(3, H),
        state_cotangent,
    )
    held = [
        pltpu.VMEM((8, 128) if name == "w2" else x.shape, F32 if name == "w2" else x.dtype)
        for name, x in zip(IN_NAMES, operands)
    ]
    final, grads, ff, f, fl = pl.pallas_call(
        functools.partial(whole, s, names),
        out_shape=[
            sds((N, H), F32),
            sds((N, H), BF16),
            sds((16, E), BF16),
            sds((s.R + 1, s.OW, s.T * s.J, H), BF16),
            sds((FIRST_ROWS, H), F32),
        ],
        in_specs=[hbm] * 16,
        out_specs=[VMEM] * 5,
        scratch_shapes=held + list(shapes.values()),
        compiler_params=pltpu.CompilerParams(
            collective_id=0, has_side_effects=True, vmem_limit_bytes=63 * 2**20
        ),
        name="edge_network",
    )(*operands)
    final, grads, feats, w2, win, wst, bin_, bst, w1, b1, b2 = pl.pallas_call(
        functools.partial(finish, s),
        out_shape=[
            sds((N, H), F32),
            sds((N, H), F32),
            sds((16, E), F32),
            sds((H, s.J * H), F32),
            sds((H, 3 * H), F32),
            sds((H, 3 * H), F32),
            sds((3, H), F32),
            sds((3, H), F32),
            sds((16, H), F32),
            sds((1, H), F32),
            sds((s.J, H), F32),
        ],
        in_specs=[hbm] * 5,
        out_specs=[VMEM] * 11,
        scratch_shapes=[
            pltpu.VMEM((s.R + 1, s.OW, s.T * s.J, H), BF16),
            pltpu.VMEM((16, E), BF16),
            pltpu.VMEM((N, H), BF16),
            pltpu.VMEM((FIRST_ROWS, H), F32),
            pltpu.VMEM((H * s.J, H), F32),
            pltpu.VMEM((H, H), F32),
            pltpu.SemaphoreType.DMA((5,)),
        ],
        compiler_params=pltpu.CompilerParams(vmem_limit_bytes=60 * 2**20),
        name="finish",
    )(f, ff, final, grads, fl)
    return (
        final,
        grads,
        feats.T,
        w1,
        b1.reshape(-1),
        w2,
        b2.reshape(-1),
        win,
        wst,
        bin_.reshape(-1),
        bst.reshape(-1),
    )


def solution(mesh):
    in_specs = (
        P("blk", None),
        P("blk", None),
        P("blk"),
        P("blk"),
        P("blk"),
        P(),
        P("blk"),
        P(),
        P(),
        P(None, "rep"),
        P("rep"),
        P(),
        P(),
        P(),
        P(),
        P("blk", None),
    )
    out_specs = (
        P("blk", None),
        P("blk", None),
        P("blk", None),
        P(),
        P(),
        P(None, "rep"),
        P("rep"),
        P(),
        P(),
        P(),
        P(),
    )

    def run(*args):
        nodes, edges, width = args[0].shape[0], args[2].shape[0], args[0].shape[1]
        return body(sizes(mesh, edges, nodes, width), *args)

    return jax.shard_map(run, mesh=mesh, in_specs=in_specs, out_specs=out_specs, check_vma=False)
```
